32 devices in a mesh: grp: 2 (over y), ex: 4 (over z), feat: 4 (over x, core).
Axes of the slice: x: 2, y: 2, z: 4, core: 2. Of those that a mesh axis runs over, the one named last changes fastest.
Arguments:
- train_grads: bfloat16 [2048, 65536], P(('grp', 'ex'), 'feat'), parts along dimension 0, may hold values from -6 to 6
- test_grads: bfloat16 [256, 65536], P('ex', 'feat'), may hold values from -0.03125 to 0.03125
- hess_diag: float32 [65536], P('feat'), may hold values from 0.05 to 5
Outputs:
- scores: float32 [2048, 256], P(('grp', 'ex'), 'feat'), parts along dimension 0
The draws below stay inside these ranges and needn't reach their ends.
There are 2 independent parts, one for each index of `grp`. The reference program is written for one: setup_inputs(seed, part) draws one part's arguments, and reference() takes and returns one part's arrays. A program takes and returns all parts, laid end to end along the dimension named above; an argument that names none is the same for every part. Nothing has to cross between parts.
All inputs are finite; a program needn't handle non-finite values.
Results may differ from the reference program's by a relative error of at most 0.0029.
Values may be sent and summed in bfloat16 or wider, within the bound.
No kernel may reach another device: no remote copies, remote signals or barrier semaphores. Data moves between devices by JAX's collectives and lax.ppermute only.
A program may use at most 64 MiB of HBM per device.

```python
import math
import jax
import jax.numpy as jnp

FEATS = 65536
DOCS = 1024
QUERIES = 256


def raised(entries, own_key, source, target, blocks, factor):
    def block_of(dim):
        return (jnp.arange(entries.shape[dim]) // (entries.shape[dim] // blocks)).reshape((-1,) + (1,) * (entries.ndim - 1 - dim))

    near = jax.random.permutation(own_key, blocks)[block_of(target)]
    second = (block_of(target) + blocks // 2) % blocks
    return jnp.where((block_of(source) == near) | (block_of(source) == second), factor * entries, entries)


def level_of(key, extent, cuts, smallest, top_value):
    loudness = 1.0
    for position, parts in cuts:
        draws = jax.random.uniform(jax.random.fold_in(jax.random.fold_in(key, 6), position), (parts,), jnp.float32, smallest / len(cuts), top_value / len(cuts))
        loudness = loudness * jnp.repeat(jnp.exp(draws), extent[position] // parts).reshape((-1,) + (1,) * (len(extent) - 1 - position))
    return loudness


def noise(stream_key, shape, width, bound, cuts=(), kind=jnp.bfloat16):
    values = width * jax.random.normal(stream_key, shape, jnp.float32)
    if cuts:
        values = values * level_of(stream_key, shape, cuts, -0.22, 0.18)
    return jnp.clip(values, -bound, bound).astype(kind)


def bell_draw_with(rng, dims, spread, reach, cuts, heavy, dtype=jnp.bfloat16):
    array = spread * jax.random.normal(rng, dims, jnp.float32)
    if cuts:
        array = array * level_of(rng, dims, cuts, -0.22, 0.18)
    return jnp.clip(raised(array, jax.random.fold_in(rng, 3), *heavy), -reach, reach).astype(dtype)


def setup_inputs(seed: int = 0, part: int = 0) -> dict:
    key_list = jax.random.split(jax.random.key(seed), 4)
    own_keys = jax.random.split(jax.random.fold_in(key_list[3], part), 4)
    train_grads = noise(own_keys[0], (DOCS, FEATS), 1.0, 6.0, ((0, 4), (1, 4)))
    test_grads = bell_draw_with(key_list[1], (QUERIES, FEATS), FEATS ** -0.5, 0.03125, ((0, 4), (1, 4)), (1, 0, 4, 2.0))
    hess_diag = jnp.clip(jnp.exp(math.log(5.0) - 4.6051702 * jax.random.uniform(key_list[2], (FEATS,), jnp.float32) ** level_of(key_list[2], (FEATS,), ((0, 4),), -0.2, 0.2)), 0.05, 5.0)
    return {"train_grads": train_grads, "test_grads": test_grads, "hess_diag": hess_diag}


def reference(train_grads, test_grads, hess_diag):
    inverse = 1.0 / (hess_diag + jnp.float32(0.1))
    precond = (test_grads.astype(jnp.float32) * inverse[None, :]).astype(jnp.bfloat16)
    return jnp.dot(train_grads, precond.T, preferred_element_type=jnp.float32)
```

```python
import jax
import jax.numpy as jnp
from jax import lax
from jax.sharding import PartitionSpec as P

CHAINS = 2
CONTRACT = (((1,), (1,)), ((), ()))


def ring(n, shift):
    return [(i, (i + shift) % n) for i in range(n)]


def solution(mesh):
    n_grp, n_ex, n_feat = (mesh.shape[a] for a in ("grp", "ex", "feat"))

    def on_device(train, test, hess):
        feats = train.shape[1]
        queries = test.shape[0]
        grp, ex, feat = (lax.axis_index(a) for a in ("grp", "ex", "feat"))
        inverse = 1.0 / (hess + jnp.float32(0.1))
        precond = (test.astype(jnp.float32) * inverse[None, :]).astype(jnp.bfloat16)

        share = feats // n_grp
        width = share // CHAINS

        def times(block, start):
            part = lax.dynamic_slice_in_dim(train, start, block.shape[1], axis=1)
            return lax.dot_general(part, block, CONTRACT, preferred_element_type=jnp.float32)

        held = [
            lax.dynamic_slice_in_dim(precond, grp * share + k * width, width, axis=1)
            for k in range(CHAINS)
        ]
        sums = [times(precond, 0)]
        for step in range(1, n_ex):
            total = jnp.zeros((train.shape[0], queries), jnp.float32)
            for k in range(CHAINS):
                held[k] = lax.ppermute(held[k], "ex", ring(n_ex, 1))
                total += times(held[k], grp * share + k * width)
                for shift in range(1, n_grp):
                    other = lax.ppermute(held[k], "grp", ring(n_grp, shift))
                    source = (grp - shift) % n_grp
                    total += times(other, source * share + k * width)
            sums.append(total)

        stacked = jnp.stack(sums)
        order = (ex - jnp.arange(n_ex)) % n_ex
        blocks = jnp.take(stacked, order, axis=0)
        per_out = n_ex * queries // n_feat
        scores = jnp.moveaxis(blocks, 0, 1).reshape(train.shape[0], n_ex * queries)

        pieces = scores.reshape(train.shape[0], n_feat, per_out)
        pieces = jnp.moveaxis(pieces, 1, 0)
        bit = 1
        while bit < n_feat:
            mine = (feat // bit) % 2
            pairs = pieces.reshape((-1, 2) + pieces.shape[1:])
            keep = lax.dynamic_index_in_dim(pairs, mine, axis=1, keepdims=False)
            send = lax.dynamic_index_in_dim(pairs, 1 - mine, axis=1, keepdims=False)
            partner = [(i, i ^ bit) for i in range(n_feat)]
            pieces = keep + lax.ppermute(send, "feat", partner)
            bit *= 2
        return pieces[0]

    return jax.shard_map(
        on_device,
        mesh=mesh,
        in_specs=(P(("grp", "ex"), "feat"), P("ex", "feat"), P("feat")),
        out_specs=P(("grp", "ex"), "feat"),
        check_vma=False,
    )
```

```python
import jax
import jax.numpy as jnp
from jax import lax
from jax.sharding import PartitionSpec as P

CHAINS = 4
CONTRACT = (((1,), (1,)), ((), ()))


def ring(n, shift):
    return [(i, (i + shift) % n) for i in range(n)]


def solution(mesh):
    n_grp, n_ex, n_feat = (mesh.shape[a] for a in ("grp", "ex", "feat"))

    def on_device(train, test, hess):
        feats = train.shape[1]
        queries = test.shape[0]
        grp, ex, feat = (lax.axis_index(a) for a in ("grp", "ex", "feat"))
        inverse = 1.0 / (hess + jnp.float32(0.1))

        share = feats // n_grp
        width = share // CHAINS

        def times(block, start):
            part = lax.dynamic_slice_in_dim(train, start, block.shape[1], axis=1)
            scale = lax.dynamic_slice_in_dim(inverse, start, block.shape[1], axis=0)
            precond = (block.astype(jnp.float32) * scale[None, :]).astype(jnp.bfloat16)
            return lax.dot_general(part, precond, CONTRACT, preferred_element_type=jnp.float32)

        held = [
            lax.dynamic_slice_in_dim(test, grp * share + k * width, width, axis=1)
            for k in range(CHAINS)
        ]
        sums = [times(test, 0)]
        for step in range(1, n_ex):
            total = jnp.zeros((train.shape[0], queries), jnp.float32)
            for k in range(CHAINS):
                held[k] = lax.ppermute(held[k], "ex", ring(n_ex, 1))
                total += times(held[k], grp * share + k * width)
                for shift in range(1, n_grp):
                    other = lax.ppermute(held[k], "grp", ring(n_grp, shift))
                    source = (grp - shift) % n_grp
                    total += times(other, source * share + k * width)
            sums.append(total)

        stacked = jnp.stack(sums)
        order = (ex - jnp.arange(n_ex)) % n_ex
        blocks = jnp.take(stacked, order, axis=0)
        per_out = n_ex * queries // n_feat
        scores = jnp.moveaxis(blocks, 0, 1).reshape(train.shape[0], n_ex * queries)

        pieces = scores.reshape(train.shape[0], n_feat, per_out)
        pieces = jnp.moveaxis(pieces, 1, 0)
        bit = 1
        while bit < n_feat:
            mine = (feat // bit) % 2
            pairs = pieces.reshape((-1, 2) + pieces.shape[1:])
            keep = lax.dynamic_index_in_dim(pairs, mine, axis=1, keepdims=False)
            send = lax.dynamic_index_in_dim(pairs, 1 - mine, axis=1, keepdims=False)
            partner = [(i, i ^ bit) for i in range(n_feat)]
            pieces = keep + lax.ppermute(send, "feat", partner)
            bit *= 2
        return pieces[0]

    return jax.shard_map(
        on_device,
        mesh=mesh,
        in_specs=(P(("grp", "ex"), "feat"), P("ex", "feat"), P("feat")),
        out_specs=P(("grp", "ex"), "feat"),
        check_vma=False,
    )
```

```python
import jax
import jax.numpy as jnp
from jax import lax
from jax.sharding import PartitionSpec as P

CONTRACT = (((1,), (1,)), ((), ()))


GATES = {
    "R2B_": ("Y1A_",),
    "L2B_": ("Y1A_",),
    "Y1B_": ("Y1A_",),
    "M3A_": ("R2A_", "L2A_"),
    "Y2A_": ("R2A_", "L2A_"),
    "R1S_": ("Y1B_",),
    "L1S_": ("R2B_", "L2B_"),
    "Y2B_": ("R2B_", "L2B_"),
    "M3B_": ("Y2A_",),
    "M2S_": ("R1S_", "L1S_"),
    "R1T_": ("R1S_", "L1S_"),
    "L1T_": ("Y2B_",),
    "R2T_": ("F1",),
    "L2T_": ("F1",),
    "M3T_": ("F2",),
    "E1": ("G",),
}


def plan(feats, n_ex):
    if n_ex == 4:
        first, second = feats // 2, feats // 4
        ship = (2 * first + second) // 8
    else:
        first, second, ship = feats * 9 // 16, feats * 5 // 16, 0
    return ship, first, second, feats - first - second - ship


def solution(mesh):
    n_grp, n_ex, n_feat = (mesh.shape[a] for a in ("grp", "ex", "feat"))

    def on_device(train, test, hess):
        docs, feats = train.shape
        queries = test.shape[0]
        half = queries // n_grp
        grp, ex, feat = (lax.axis_index(a) for a in ("grp", "ex", "feat"))
        low = ex < n_ex // 2
        w_ship, w_first, w_second, w_last = plan(feats, n_ex)
        inverse = 1.0 / (hess + jnp.float32(0.1))

        rolled = lax.dynamic_slice_in_dim(
            jnp.concatenate([test] * 2, axis=0) if n_grp > 1 else test, grp * half, queries, axis=0
        )

        def among(members):
            found = jnp.bool_(False)
            for i in members:
                found = found | (ex == i)
            return found

        done = {}

        def send(name, block, axis, pairs):
            waits = [done[g] for g in GATES.get(name, ()) if g in done]
            if waits:
                block = lax.optimization_barrier((block, waits))[0]
            done[name] = lax.ppermute(block, axis, pairs)
            return done[name]

        class Spread:
            def __init__(self, name, block, first=0, last=n_ex - 1):
                self.name = name
                self.span = range(first, last + 1)
                self.right, self.left = {0: block}, {0: block}

            def hop(self, t, cargo=None):
                down = [(i + 1, i) for i in self.span if i + t < n_ex]
                up = [(i - 1, i) for i in self.span if i >= t]
                if not down and not up:
                    return None
                apart = not (
                    {s for s, _ in down} & {s for s, _ in up}
                    or {d for _, d in down} & {d for _, d in up}
                )
                if apart:
                    block = jnp.where(
                        among([s for s, _ in down]), self.right[t - 1], self.left[t - 1]
                    )
                    if cargo is not None:
                        block = jnp.where(is_end, cargo, block)
                        down, up = down + [ends[1]], up + [ends[0]]
                    block = send(f"M{t}{self.name}", block, "ex", down + up)
                    self.right[t] = self.left[t] = block
                else:
                    right, left = self.right[t - 1], self.left[t - 1]
                    if cargo is not None:
                        right = jnp.where(ex == n_ex - 1, cargo, right)
                        left = jnp.where(ex == 0, cargo, left)
                        down, up = down + [ends[1]], up + [ends[0]]
                    self.right[t] = send(f"R{t}{self.name}", right, "ex", down)
                    self.left[t] = send(f"L{t}{self.name}", left, "ex", up)
                return jnp.where(low, self.left[t], self.right[t])

            def take(self, t):
                if 2 * t <= n_ex:
                    return jnp.where(low, self.right[t], self.left[t])
                back = jnp.where(low, self.left[n_ex - t], self.right[n_ex - t])
                if t not in self.right:
                    return back
                arrived = (ex + t < n_ex) | (ex >= t)
                return jnp.where(arrived, jnp.where(low, self.right[t], self.left[t]), back)

        def swap(name, block):
            blocks = [block]
            for shift in range(1, n_grp):
                pairs = [(i, (i - shift) % n_grp) for i in range(n_grp)]
                blocks.append(send(name, block, "grp", pairs))
            return blocks

        def times(rows, docs_part, start):
            width = rows.shape[1]
            scale = inverse[start : start + width]
            precond = (rows.astype(jnp.float32) * scale[None, :]).astype(jnp.bfloat16)
            return lax.dot_general(precond, docs_part, CONTRACT, preferred_element_type=jnp.float32)

        direction = jnp.where(low, 1, -1)

        def sum_over_feat(name, sums):
            per_out = n_ex * queries // n_feat
            pieces = sums.reshape(n_ex * n_grp, half, docs)

            def rows_of(target):
                got = []
                for k in range(per_out // half):
                    place = target * (per_out // half) + k
                    t = (direction * (place // n_grp - ex)) % n_ex
                    h = (place % n_grp - grp) % n_grp
                    got.append(lax.dynamic_index_in_dim(pieces, t * n_grp + h, 0, keepdims=False))
                return jnp.concatenate(got, axis=0)

            bit = 1
            count = n_feat
            held = None
            while bit < n_feat:
                count //= 2
                mine = feat % (2 * bit)
                theirs = mine ^ bit
                partner = [(i, i ^ bit) for i in range(n_feat)]
                if held is None:
                    keep = jnp.stack([rows_of(2 * j + mine) for j in range(count)])
                    away = jnp.stack([rows_of(2 * j + theirs) for j in range(count)])
                else:
                    pairs = held.reshape(count, 2, per_out, docs)
                    up = mine // bit
                    keep = lax.dynamic_index_in_dim(pairs, up, 1, keepdims=False)
                    away = lax.dynamic_index_in_dim(pairs, 1 - up, 1, keepdims=False)
                held = keep + send(f"{name}{bit}", away, "feat", partner)
                bit *= 2
            return rows_of(0) if held is None else held[0]

        starts, at = [], 0
        for width in (w_ship, w_first, w_second, w_last):
            starts.append(at)
            at += width
        own = lambda start, width: rolled[:, start : start + width]

        ends = [(0, 1), (n_ex - 1, n_ex - 2)]
        is_end = (ex == 0) | (ex == n_ex - 1)
        a, b = Spread("A_", own(starts[1], w_first)[:half]), Spread("B_", own(starts[2], w_second)[:half])
        chunks = [(starts[1], w_first), (starts[2], w_second)]
        arrived = [[own(s, w)] for s, w in chunks]
        tail = Spread("T_", own(starts[3], w_last))
        shipped = Spread("S_", own(0, w_ship), 1, n_ex - 2) if w_ship else None

        groups = docs // half
        crates, crate_at = {}, 0

        def crate(width):
            nonlocal crate_at
            width //= groups
            piece = train[:, crate_at : crate_at + width].reshape(groups, half, width)
            crate_at += width
            return jnp.concatenate([piece[g] for g in range(groups)], axis=1)

        def uncrate(block):
            return jnp.concatenate(jnp.split(block, groups, axis=1), axis=0)

        cargo = {}
        if w_ship:
            cargo = {(2, 0): crate(w_first), (3, 0): crate(w_first), (2, 1): crate(w_second)}
        landed = {}
        for t in range(1, n_ex):
            for k, spread in enumerate((a, b)):
                landed[t, k] = spread.hop(t, cargo.get((t, k)))
                arrived[k].extend(swap(f"Y{t}{spread.name}", spread.take(t)))
            if t == 2 and shipped:
                for u in range(1, n_ex):
                    shipped.hop(u)
        if shipped:
            tail.hop(1)
        sums = jnp.zeros((n_ex * queries, docs), jnp.float32)
        if shipped:
            rows = jnp.concatenate([own(0, w_ship)] + [shipped.take(t) for t in range(1, n_ex)])
            away = jnp.concatenate([uncrate(landed[key]) for key in cargo], axis=1)
            sums = jnp.where(is_end, 0.0, times(rows, train[:, :w_ship], 0))
            far = sum_over_feat("F", times(rows, away, 0))
            back = send("G", far, "ex", [(d, s) for s, d in ends])
        for t in range(2 if shipped else 1, n_ex):
            tail.hop(t)
        for (s, w), rows in zip(chunks, arrived):
            sums += times(jnp.concatenate(rows), train[:, s : s + w], s)
        rows = jnp.concatenate([own(starts[3], w_last)] + [tail.take(t) for t in range(1, n_ex)])
        sums += times(rows, train[:, starts[3] :], starts[3])
        out = sum_over_feat("E", sums)
        if shipped:
            out += back
        return out.T

    return jax.shard_map(
        on_device,
        mesh=mesh,
        in_specs=(P(("grp", "ex"), "feat"), P("ex", "feat"), P("feat")),
        out_specs=P(("grp", "ex"), "feat"),
        check_vma=False,
    )
```

```python
import functools

import jax
import jax.numpy as jnp
import numpy as np
from jax import lax
from jax.experimental import pallas as pl
from jax.experimental.pallas import tpu as pltpu
from jax.sharding import PartitionSpec as P

CONTRACT = (((1,), (1,)), ((), ()))
LANES = 128

GATES = {
    "E1S": ("Y1A",),
    "O1S": ("Y1A",),
    "Y1B": ("Y1A",),
    "E3A": ("E2A",),
    "Y2A": ("O2A",),
    "E2B": ("Y1B",),
    "O2B": ("O1S",),
    "O2S": ("Y2A",),
    "Y3A": ("Y2A",),
    "E1T": ("Y2A", "E3A"),
    "O1T": ("O2S",),
    "F1": ("Y3A",),
    "Y3B": ("Y2B",),
    "O2T": ("F1",),
    "E3T": ("F2", "Y2B"),
    "Z1": ("G",),
}


def plan(feats, n_ex):
    if n_ex == 4:
        first, second = feats // 2, feats // 4
        ship = (2 * first + second) // 8
    else:
        first, second, ship = feats // 2, feats * 3 // 8, 0
    return first, second, ship, feats - first - second - ship


def arrival(n_ex):
    if n_ex == 4:
        return [[0, 1, 2, 3], [1, 0, 2, 3], [2, 3, 1, 0], [3, 2, 1, 0]]
    return [[(i - t) % n_ex for t in range(n_ex)] for i in range(n_ex)]


def scores_kernel(n_rows, has_base, offsets, *refs):
    rows, (scale, train) = refs[:n_rows], refs[n_rows : n_rows + 2]
    base = refs[n_rows + 2] if has_base else None
    out, total = refs[-2:]
    step = pl.program_id(0)
    block = jnp.concatenate([r[...] for r in rows], axis=0)
    precond = (block.astype(jnp.float32) * scale[...]).astype(jnp.bfloat16)
    part = lax.dot_general(precond, train[...], CONTRACT, preferred_element_type=jnp.float32)

    @pl.when(step == 0)
    def _():
        total[...] = part

    @pl.when(step > 0)
    def _():
        total[...] += part

    @pl.when(step == pl.num_programs(0) - 1)
    def _():
        count = offsets.shape[0]
        size = out.shape[0] // count
        for i in range(count):
            at = pl.multiple_of(offsets[i], size)
            value = total[pl.ds(at, size), :]
            if has_base:
                value += base[i * size : (i + 1) * size, :]
            out[i * size : (i + 1) * size, :] = value


def scores(offsets, test, received, scale, train, start, width, train_start, base=None):
    docs = train.shape[0]
    tile = next(t for t in (1024, 512, 256, 128) if all(v % t == 0 for v in (start, width, train_start)))
    lead, at = start // tile, train_start // tile
    in_specs = [pl.BlockSpec((test.shape[0], tile), lambda k, _: (0, lead + k))]
    in_specs += [pl.BlockSpec((r.shape[0], tile), lambda k, _: (0, k)) for r in received]
    in_specs += [
        pl.BlockSpec((1, tile), lambda k, _: (0, lead + k)),
        pl.BlockSpec((docs, tile), lambda k, _: (0, at + k)),
    ]
    operands = [test, *received, scale, train]
    queries = test.shape[0] + sum(r.shape[0] for r in received)
    if base is not None:
        in_specs.append(pl.BlockSpec((queries, docs), lambda k, _: (0, 0)))
        operands.append(base)
    return pl.pallas_call(
        functools.partial(scores_kernel, 1 + len(received), base is not None),
        out_shape=jax.ShapeDtypeStruct((queries, docs), jnp.float32),
        grid_spec=pltpu.PrefetchScalarGridSpec(
            num_scalar_prefetch=1,
            grid=(width // tile,),
            in_specs=in_specs,
            out_specs=pl.BlockSpec((queries, docs), lambda k, _: (0, 0)),
            scratch_shapes=[pltpu.VMEM((queries, docs), jnp.float32)],
        ),
        cost_estimate=pl.CostEstimate(
            flops=2 * queries * docs * width,
            bytes_accessed=2 * (queries + docs) * width,
            transcendentals=0,
        ),
        compiler_params=pltpu.CompilerParams(vmem_limit_bytes=12 * 1024 * 1024),
    )(offsets, *operands)


def solution(mesh):
    n_grp, n_ex, n_feat = (mesh.shape[a] for a in ("grp", "ex", "feat"))
    assert n_grp <= 2

    def on_device(train, test, hess):
        docs, feats = train.shape
        queries = test.shape[0]
        half = queries // n_grp
        grp, ex, feat = (lax.axis_index(a) for a in ("grp", "ex", "feat"))
        is_end = (ex == 0) | (ex == n_ex - 1)
        scale = (1.0 / (hess + jnp.float32(0.1))).reshape(1, feats)

        whole, halved = [], []
        for i, owners in enumerate(arrival(n_ex)):
            for g in range(n_grp):
                whole.append([])
                halved.append([])
                for b in range(n_ex):
                    t = owners.index(b)
                    for h in range(n_grp):
                        whole[-1].append(t * queries + h * half)
                        halved[-1].append(t * queries + ((h - g) % n_grp if t else h) * half)
        row = ex * n_grp + grp
        whole, halved = (
            lax.dynamic_index_in_dim(jnp.asarray(np.array(v, np.int32)), row, 0, keepdims=False)
            for v in (whole, halved)
        )

        done = {}

        def send(name, block, axis, pairs):
            waits = [done[g] for g in GATES.get(name, ()) if g in done]
            if waits:
                block = lax.optimization_barrier((block, waits))[0]
            done[name] = lax.ppermute(block, axis, pairs)
            return done[name]

        def links(parity, toward):
            pairs = []
            for i in range(parity, n_ex - 1, 2):
                pairs += [(s, d) for s, d in ((i, i + 1), (i + 1, i)) if d in toward]
            return pairs

        everyone, inner, outer = range(n_ex), range(1, n_ex - 1), (0, n_ex - 1)

        class Line:
            def __init__(self, name, block, cargo=(None, None), shipping=False):
                self.name, self.block, self.cargo, self.shipping = name, block, cargo, shipping

            def outer(self, t):
                block = self.block if t == 1 else done[f"O{t - 1}{self.name}"]
                toward = everyone if t == 1 else outer
                if self.shipping:
                    toward = inner
                elif t > 1 and self.cargo[t - 2] is not None:
                    block = jnp.where(is_end, self.cargo[t - 2], block)
                    toward = everyone
                return send(f"E{t}{self.name}", block, "ex", links(0, toward))

            def middle(self, t):
                block = self.block if t == 1 else done[f"E{t - 1}{self.name}"]
                return send(f"O{t}{self.name}", block, "ex", links(1, inner))

            def take(self, t):
                if t == 1:
                    return done[f"E1{self.name}"]
                if self.shipping:
                    return done[f"O{t - 1}{self.name}"]
                return jnp.where(is_end, done[f"E{t}{self.name}"], done[f"O{t - 1}{self.name}"])

        def swap(name, block):
            if n_grp == 1:
                return [block]
            return [block, send(name, block, "grp", [(0, 1), (1, 0)])]

        def sum_over_feat(name, sums):
            held = sums.reshape(n_feat, -1, docs)
            bit = 1
            while bit < n_feat:
                pairs = held.reshape((-1, 2) + held.shape[1:])
                mine = (feat // bit) % 2
                keep = lax.dynamic_index_in_dim(pairs, mine, 1, keepdims=False)
                away = lax.dynamic_index_in_dim(pairs, 1 - mine, 1, keepdims=False)
                partner = [(i, i ^ bit) for i in range(n_feat)]
                held = keep + send(f"{name}{bit}", away, "feat", partner)
                bit *= 2
            return held[0]

        w_first, w_second, w_ship, w_last = plan(feats, n_ex)
        at_first, at_second, at_ship, at_last = np.cumsum([0, w_first, w_second, w_ship]).tolist()

        def part(start, width):
            if n_grp == 1:
                return test[:, start : start + width]
            return lax.dynamic_slice(test, (grp * half, start), (half, width))

        times = functools.partial(scores, test=test, scale=scale)
        halves = [("A", at_first, w_first), ("B", at_second, w_second)]
        got = {name: [] for name in "ABST"}
        base = None

        if n_ex == 4:
            ends = [(0, 1), (n_ex - 1, n_ex - 2)]
            groups = docs // half

            def crate(start, width):
                piece = train[:, start : start + width].reshape(groups, half, width)
                return jnp.moveaxis(piece, 0, 1).reshape(half, groups * width)

            def uncrate(block):
                return jnp.concatenate(jnp.split(block, groups, axis=1), axis=0)

            wide, narrow = w_first // groups, w_second // groups
            a = Line("A", part(at_first, w_first), (crate(at_ship, wide), crate(at_ship + wide, wide)))
            b = Line("B", part(at_second, w_second), (crate(at_ship + 2 * wide, narrow), None))
            s = Line("S", test[:, at_ship : at_ship + w_ship], shipping=True)
            tail = Line("T", test[:, at_last:])

            def swapped(line, t):
                got[line.name] += swap(f"Y{t}{line.name}", line.take(t))

            a.outer(1), a.middle(1), b.outer(1), b.middle(1)
            swapped(a, 1)
            a.outer(2), a.middle(2), s.outer(1), s.middle(1)
            swapped(b, 1), swapped(a, 2)
            a.outer(3), b.outer(2), b.middle(2), s.middle(2)
            swapped(a, 3)
            tail.outer(1), b.outer(3)
            swapped(b, 2)
            got["S"] = [s.take(t) for t in range(1, n_ex)]
            away = jnp.concatenate([uncrate(done[k]) for k in ("E2A", "E3A", "E2B")], axis=1)
            far = times(whole, received=got["S"], train=away, start=at_ship, width=w_ship, train_start=0)
            far = sum_over_feat("F", far)
            tail.middle(1), tail.outer(2), tail.middle(2)
            swapped(b, 3)
            back = send("G", far, "ex", [(d, s) for s, d in ends])
            tail.outer(3)
            got["T"] = [tail.take(t) for t in range(1, n_ex)]
            near = times(
                whole, received=got["S"], train=train, start=at_ship, width=w_ship, train_start=at_ship
            )
            base = jnp.where(is_end, 0.0, near)
        else:
            ring = [(i, (i + 1) % n_ex) for i in range(n_ex)]
            held = {"A": part(at_first, w_first), "B": part(at_second, w_second), "T": test[:, at_last:]}
            for t in range(1, n_ex):
                for name in held:
                    held[name] = send(f"R{t}{name}", held[name], "ex", ring)
                    got[name] += [held[name]] if name == "T" else swap(f"Y{t}{name}", held[name])

        for name, start, width in halves:
            base = times(
                halved, received=got[name], train=train, start=start, width=width, train_start=start,
                base=base,
            )
        total = times(
            whole, received=got["T"], train=train, start=at_last, width=w_last, train_start=at_last,
            base=base,
        )
        out = sum_over_feat("Z", total)
        if n_ex == 4:
            out += back
        return out.T

    return jax.shard_map(
        on_device,
        mesh=mesh,
        in_specs=(P(("grp", "ex"), "feat"), P("ex", "feat"), P("feat")),
        out_specs=P(("grp", "ex"), "feat"),
        check_vma=False,
    )
```

```python
import functools

import jax
import jax.numpy as jnp
from jax import lax
from jax.experimental import pallas as pl
from jax.experimental.pallas import tpu as pltpu
from jax.sharding import PartitionSpec as P

CONTRACT = (((1,), (1,)), ((), ()))
LINE, RING = (8, 5, 2, 1), (8, 5, 0, 3)
KEPT = ((0, 1, 2, 3), (1, 0, 2, 3), (2, 3, 1, 0), (3, 2, 1, 0))

GATES = {
    "E1T": ("E1B", "O1B"),
    "O1T": ("E1B", "O1B"),
    "Y1B": ("Y1A",),
    "E2B": ("E2A",),
    "Y2A": ("Y1A",),
    "O2B": ("O2A",),
    "OS": ("O1T", "E1T"),
    "E3A": ("E1T",),
    "E3B": ("E2B",),
    "Y2B": ("Y2A",),
    "E2T": ("E2B", "Y2A"),
    "O2T": ("OS",),
    "Y3A": ("Y2A",),
    "F1": ("Y2B",),
    "E3T": ("F1", "E2T"),
    "Y3B": ("Y2B",),
    "Z1": ("G",),
}


def pack_kernel(n_grp, plans, test, *rest):
    outs, sem = rest[:-1], rest[-1]
    copies = []
    for out, parts in zip(outs, plans):
        for slot, (row, col) in enumerate(parts):
            _, rows, cols = out.shape
            at = lax.axis_index("grp") * rows if row is None and n_grp > 1 else row or 0
            source = test.at[pl.ds(pl.multiple_of(at, rows), rows), pl.ds(col, cols)]
            copies.append(pltpu.make_async_copy(source, out.at[slot], sem.at[len(copies)]))
    for copy in copies:
        copy.start()
    for copy in copies:
        copy.wait()


def pack(n_grp, test, plans, rows, cols):
    return pl.pallas_call(
        functools.partial(pack_kernel, n_grp, plans),
        out_shape=[jax.ShapeDtypeStruct((len(p), rows, cols), test.dtype) for p in plans],
        in_specs=[pl.BlockSpec(memory_space=pl.ANY)],
        out_specs=[pl.BlockSpec(memory_space=pl.ANY)] * len(plans),
        scratch_shapes=[pltpu.SemaphoreType.DMA((sum(len(p) for p in plans),))],
        cost_estimate=pl.CostEstimate(flops=0, bytes_accessed=1 << 20, transcendentals=0),
    )(test)


def scores_kernel(n_grp, n_ex, halved, n_rows, has_base, *refs):
    rows, (scale, train) = refs[:n_rows], refs[n_rows : n_rows + 2]
    base = refs[n_rows + 2] if has_base else None
    out, total = refs[-2:]
    step = pl.program_id(0)
    block = jnp.concatenate([r[...] for r in rows], axis=0)
    precond = (block.astype(jnp.float32) * scale[...]).astype(jnp.bfloat16)
    part = lax.dot_general(precond, train[...], CONTRACT, preferred_element_type=jnp.float32)

    @pl.when(step == 0)
    def _():
        total[...] = part

    @pl.when(step > 0)
    def _():
        total[...] += part

    @pl.when(step == pl.num_programs(0) - 1)
    def _():
        ex, grp = lax.axis_index("ex"), lax.axis_index("grp")
        queries = out.shape[0] // n_ex
        half = queries // n_grp
        for b in range(n_ex):
            if n_ex == 4:
                t = jnp.int32(0)
                for i, kept in enumerate(KEPT):
                    t = jnp.where(ex == i, kept.index(b), t)
            else:
                t = lax.rem(ex + (n_ex - b), n_ex)
            for h in range(n_grp):
                place = h
                if halved and n_grp > 1:
                    place = jnp.where(t == 0, h, lax.rem(h + n_grp - grp, n_grp))
                at = pl.multiple_of(t * queries + place * half, half)
                value = total[pl.ds(at, half), :]
                to = b * queries + h * half
                if has_base:
                    value += base[to : to + half, :]
                out[to : to + half, :] = value


def scores(n_grp, n_ex, test, received, scale, train, unit, start, count, train_start, halved=False, base=None):
    docs = train.shape[0]
    in_specs = [pl.BlockSpec((test.shape[0], unit), lambda k: (0, start + k))]
    operands = [test]
    for array, first in received:
        in_specs.append(
            pl.BlockSpec((None,) + array.shape[1:], functools.partial(lambda f, k: (f + k, 0, 0), first))
        )
        operands.append(array)
    in_specs += [
        pl.BlockSpec((1, unit), lambda k: (0, start + k)),
        pl.BlockSpec((docs, unit), lambda k: (0, train_start + k)),
    ]
    operands += [scale, train]
    queries = test.shape[0] * n_ex
    if base is not None:
        in_specs.append(pl.BlockSpec((queries, docs), lambda k: (0, 0)))
        operands.append(base)
    return pl.pallas_call(
        functools.partial(
            scores_kernel, n_grp, n_ex, halved, 1 + len(received), base is not None
        ),
        out_shape=jax.ShapeDtypeStruct((queries, docs), jnp.float32),
        grid=(count,),
        in_specs=in_specs,
        out_specs=pl.BlockSpec((queries, docs), lambda k: (0, 0)),
        scratch_shapes=[pltpu.VMEM((queries, docs), jnp.float32)],
        cost_estimate=pl.CostEstimate(
            flops=2 * queries * docs * unit * count,
            bytes_accessed=2 * (queries + docs) * unit * count,
            transcendentals=0,
        ),
        compiler_params=pltpu.CompilerParams(vmem_limit_bytes=16 * 1024 * 1024),
    )(*operands)


def solution(mesh):
    n_grp, n_ex, n_feat = (mesh.shape[a] for a in ("grp", "ex", "feat"))
    assert n_grp <= 2
    line = n_ex == 4

    def on_device(train, test, hess):
        docs, feats = train.shape
        queries = test.shape[0]
        half = queries // n_grp
        unit = feats // 16
        n_a, n_b, n_s, n_t = LINE if line else RING
        at_b, at_s, at_t = n_a, n_a + n_b, n_a + n_b + n_s
        ex, feat = lax.axis_index("ex"), lax.axis_index("feat")
        is_end = (ex == 0) | (ex == n_ex - 1)
        done = {}

        def send(name, block, axis, pairs):
            waits = [done[g] for g in GATES.get(name, ()) if g in done]
            if waits:
                block = lax.optimization_barrier((block, waits))[0]
            done[name] = lax.ppermute(block, axis, pairs)
            return done[name]

        outer = [(i, i ^ 1) for i in range(n_ex)]
        middle = [(0, 0), (1, 2), (2, 1), (3, 3)]
        ring = [(i, (i + 1) % n_ex) for i in range(n_ex)]

        def hop(name, block, t):
            if t > 1:
                send(f"E{t}{name}", block, "ex", outer)
                if t < n_ex - 1:
                    send(f"O{t}{name}", done[f"E1{name}"], "ex", middle)
            else:
                send(f"E1{name}", block, "ex", outer)
                send(f"O1{name}", block, "ex", middle)

        def taken(name, t):
            if t == 1:
                return done[f"E1{name}"]
            return jnp.where(is_end, done[f"E{t}{name}"], done[f"O{t - 1}{name}"])

        def swap(name, block):
            if n_grp == 1:
                return [(block, 0)]
            return [(block, 0), (send(name, block, "grp", [(0, 1), (1, 0)]), 0)]

        def sum_over_feat(name, sums):
            held = sums.reshape(n_feat, -1, docs)
            bit = 1
            while bit < n_feat:
                pairs = held.reshape((-1, 2) + held.shape[1:])
                mine = (feat // bit) % 2
                keep = lax.dynamic_index_in_dim(pairs, mine, 1, keepdims=False)
                away = lax.dynamic_index_in_dim(pairs, 1 - mine, 1, keepdims=False)
                partner = [(i, i ^ bit) for i in range(n_feat)]
                held = keep + send(f"{name}{bit}", away, "feat", partner)
                bit *= 2
            return held[0]

        def halves(first, count):
            return [(None, (first + k) * unit) for k in range(count)]

        (a,) = pack(n_grp, test, [halves(0, n_a)], half, unit)
        plans = [halves(at_b, n_b)]
        if line:
            plans.append([(h * half, (at_s + k) * unit) for h in range(n_grp) for k in range(n_s)])
        b, *own_s = pack(n_grp, test, plans, half, unit)
        (tail,) = pack(1, test, [[(0, (at_t + k) * unit) for k in range(n_t)]], queries, unit)
        scale = (1.0 / (hess + jnp.float32(0.1))).reshape(1, feats)
        times = functools.partial(scores, n_grp, n_ex, test, scale=scale, unit=unit)
        got = {"A": [], "B": [], "T": []}

        def swapped(name, t):
            got[name] += swap(f"Y{t}{name}", taken(name, t))

        base = back = None
        if line:
            own_s = own_s[0]
            n_own = own_s.shape[0]
            groups = docs // half

            def slots(first, last, column):
                piece = train[first * half : last * half, column * unit : (column + 1) * unit]
                return piece.reshape(last - first, half, unit)

            cut = n_a - n_own
            cargo_2a = jnp.concatenate([own_s, slots(0, cut, at_s)])
            cargo_2b = jnp.concatenate([slots(cut, groups, at_s)] + [tail[:, :half]] * (n_b - groups + cut))
            cargo_3a = slots(0, groups, at_s + 1)

            hop("A", a, 1), hop("B", b, 1)
            swapped("A", 1)
            hop("A", jnp.where(is_end, cargo_2a, done["O1A"]), 2)
            hop("T", tail, 1)
            swapped("B", 1), swapped("A", 2)
            hop("B", jnp.where(is_end, cargo_2b, done["O1B"]), 2)
            end_s = done["E2A"][:n_own]
            send("OS", jnp.concatenate([own_s, end_s]), "ex", middle)
            hop("A", jnp.where(is_end, cargo_3a, done["O2A"]), 3)
            hop("B", done["O2B"], 3)
            swapped("B", 2)
            hop("T", done["O1T"], 2)
            swapped("A", 3)
            rows_s = [(end_s, h * n_s) for h in range(n_grp)]
            rows_s += [(done["OS"], h * n_s) for h in range(2 * n_grp)]
            first = jnp.concatenate([done["E2A"][n_own:], done["E2B"][: groups - cut]])
            away = jnp.concatenate([first.reshape(docs, unit), done["E3A"].reshape(docs, unit)], axis=1)
            far = times(received=rows_s, train=away, start=at_s, count=n_s, train_start=0)
            far = sum_over_feat("F", far)
            swapped("B", 3)
            hop("T", done["O2T"], 3)
            back = send("G", far, "ex", outer)
            near = times(received=rows_s, train=train, start=at_s, count=n_s, train_start=at_s)
            base = jnp.where(is_end, 0.0, near)
            got["T"] = [(taken("T", t), 0) for t in range(1, n_ex)]
        else:
            held = {"A": a, "B": b, "T": tail}
            for t in range(1, n_ex):
                for name in held:
                    held[name] = send(f"R{t}{name}", held[name], "ex", ring)
                    got[name] += [(held[name], 0)] if name == "T" else swap(f"Y{t}{name}", held[name])

        for name, start, count in (("A", 0, n_a), ("T", at_t, n_t), ("B", at_b, n_b)):
            base = times(
                received=got[name], train=train, start=start, count=count, train_start=start,
                halved=name != "T" and n_grp > 1, base=base,
            )
        out = sum_over_feat("Z", base)
        if line:
            out += jnp.where(is_end, back, 0.0)
        return out.T

    return jax.shard_map(
        on_device,
        mesh=mesh,
        in_specs=(P(("grp", "ex"), "feat"), P("ex", "feat"), P("feat")),
        out_specs=P(("grp", "ex"), "feat"),
        check_vma=False,
    )
```

```python
import functools

import jax
import jax.numpy as jnp
from jax import lax
from jax.experimental import pallas as pl
from jax.experimental.pallas import tpu as pltpu
from jax.sharding import PartitionSpec as P

CONTRACT = (((1,), (1,)), ((), ()))
A, B, T = 8, 7, 1

GATES = {
    "R3A": ("Y1A",),
    "R1T": ("Y1B",),
    "R2T": ("Y2A",),
    "R3B": ("Y1B",),
    "R3T": ("R3B", "Y2B"),
}


def scores_kernel(n_grp, n_ex, halved, n_rows, has_base, *refs):
    rows, (scale, train) = refs[:n_rows], refs[n_rows : n_rows + 2]
    base = refs[n_rows + 2] if has_base else None
    out, total = refs[-2:]
    step = pl.program_id(0)
    block = jnp.concatenate([r[...] for r in rows], axis=0)
    precond = (block.astype(jnp.float32) * scale[...]).astype(jnp.bfloat16)
    part = lax.dot_general(precond, train[...], CONTRACT, preferred_element_type=jnp.float32)

    @pl.when(step == 0)
    def _():
        total[...] = part

    @pl.when(step > 0)
    def _():
        total[...] += part

    @pl.when(step == pl.num_programs(0) - 1)
    def _():
        ex, grp = lax.axis_index("ex"), lax.axis_index("grp")
        queries = out.shape[0] // n_ex
        half = queries // n_grp
        for b in range(n_ex):
            t = lax.rem(ex + (n_ex - b), n_ex)
            for h in range(n_grp):
                place = h
                if halved and n_grp > 1:
                    place = jnp.where(t == 0, h, lax.rem(h + n_grp - grp, n_grp))
                at = pl.multiple_of(t * queries + place * half, half)
                value = total[pl.ds(at, half), :]
                to = b * queries + h * half
                if has_base:
                    value += base[to : to + half, :]
                out[to : to + half, :] = value


def scores(n_grp, n_ex, test, scale, train, unit, start, received, halved, base=None):
    docs = train.shape[0]
    width = received[0].shape[1]
    column = lambda k: (0, start + k)
    in_specs = [pl.BlockSpec((test.shape[0], unit), column)]
    in_specs += [pl.BlockSpec((r.shape[0], unit), lambda k: (0, k)) for r in received]
    in_specs += [pl.BlockSpec((1, unit), column), pl.BlockSpec((docs, unit), column)]
    operands = [test, *received, scale, train]
    queries = test.shape[0] * n_ex
    if base is not None:
        in_specs.append(pl.BlockSpec((queries, docs), lambda k: (0, 0)))
        operands.append(base)
    return pl.pallas_call(
        functools.partial(
            scores_kernel, n_grp, n_ex, halved, 1 + len(received), base is not None
        ),
        out_shape=jax.ShapeDtypeStruct((queries, docs), jnp.float32),
        grid=(width // unit,),
        in_specs=in_specs,
        out_specs=pl.BlockSpec((queries, docs), lambda k: (0, 0)),
        scratch_shapes=[pltpu.VMEM((queries, docs), jnp.float32)],
        cost_estimate=pl.CostEstimate(
            flops=2 * queries * docs * width,
            bytes_accessed=2 * (queries + docs) * width,
            transcendentals=0,
        ),
        compiler_params=pltpu.CompilerParams(vmem_limit_bytes=16 * 1024 * 1024),
    )(*operands)


def solution(mesh):
    n_grp, n_ex, n_feat = (mesh.shape[a] for a in ("grp", "ex", "feat"))
    assert n_grp <= 2

    def on_device(train, test, hess):
        docs, feats = train.shape
        queries = test.shape[0]
        half = queries // n_grp
        unit = feats // (A + B + T)
        grp, feat = lax.axis_index("grp"), lax.axis_index("feat")
        done = {}

        def send(name, block, axis, pairs):
            waits = [done[g] for g in GATES.get(name, ()) if g in done]
            if waits:
                block = lax.optimization_barrier((block, waits))[0]
            done[name] = lax.ppermute(block, axis, pairs)
            return done[name]

        ring = [(i, (i + 1) % n_ex) for i in range(n_ex)]

        def swap(name, block):
            if n_grp == 1:
                return [block]
            return [block, send(name, block, "grp", [(0, 1), (1, 0)])]

        def sum_over_feat(name, sums):
            held = sums.reshape(n_feat, -1, docs)
            bit = 1
            while bit < n_feat:
                pairs = held.reshape((-1, 2) + held.shape[1:])
                mine = (feat // bit) % 2
                keep = lax.dynamic_index_in_dim(pairs, mine, 1, keepdims=False)
                away = lax.dynamic_index_in_dim(pairs, 1 - mine, 1, keepdims=False)
                partner = [(i, i ^ bit) for i in range(n_feat)]
                held = keep + send(f"{name}{bit}", away, "feat", partner)
                bit *= 2
            return held[0]

        def share(start, width):
            columns = slice(start * unit, (start + width) * unit)
            if n_grp == 1:
                return test[:, columns]
            return jnp.where(grp == 0, test[:half, columns], test[half:, columns])

        chunks = {"A": (0, A), "B": (A, B), "T": (A + B, T)}
        held = {"A": share(0, A), "B": share(A, B), "T": test[:, (A + B) * unit :]}
        got = {name: [] for name in chunks}
        for t in range(1, n_ex):
            for name in chunks:
                held[name] = send(f"R{t}{name}", held[name], "ex", ring)
                got[name] += [held[name]] if name == "T" else swap(f"Y{t}{name}", held[name])

        scale = (1.0 / (hess + jnp.float32(0.1))).reshape(1, feats)
        sums = None
        for name in "ATB":
            sums = scores(
                n_grp, n_ex, test, scale, train, unit, chunks[name][0], got[name],
                halved=name != "T" and n_grp > 1, base=sums,
            )
        return sum_over_feat("Z", sums).T

    return jax.shard_map(
        on_device,
        mesh=mesh,
        in_specs=(P(("grp", "ex"), "feat"), P("ex", "feat"), P("feat")),
        out_specs=P(("grp", "ex"), "feat"),
        check_vma=False,
    )
```

```python
import jax
import jax.numpy as jnp
from jax import lax
from jax.sharding import PartitionSpec as P

CONTRACT = (((1,), (1,)), ((), ()))


def solution(mesh):
    n_grp, n_ex, n_feat = (mesh.shape[a] for a in ("grp", "ex", "feat"))

    def on_device(train, test, hess):
        docs, feats = train.shape
        queries = test.shape[0]
        grp, feat = lax.axis_index("grp"), lax.axis_index("feat")
        share = feats // n_grp
        inverse = 1.0 / (hess + jnp.float32(0.1))
        mine = lax.dynamic_slice_in_dim(test, grp * share, share, axis=1)
        scale = lax.dynamic_slice_in_dim(inverse, grp * share, share, axis=0)
        precond = (mine.astype(jnp.float32) * scale[None, :]).astype(jnp.bfloat16)
        gathered = lax.all_gather(precond, ("grp", "ex"), axis=0, tiled=True)

        sums = jnp.zeros((n_ex * queries, docs), jnp.float32)
        for g in range(n_grp):
            rows = gathered[g * n_ex * queries : (g + 1) * n_ex * queries]
            sums += lax.dot_general(
                rows, train[:, g * share : (g + 1) * share], CONTRACT, preferred_element_type=jnp.float32
            )

        held = sums.reshape(n_feat, -1, docs)
        bit = 1
        while bit < n_feat:
            pairs = held.reshape((-1, 2) + held.shape[1:])
            up = (feat // bit) % 2
            keep = lax.dynamic_index_in_dim(pairs, up, 1, keepdims=False)
            away = lax.dynamic_index_in_dim(pairs, 1 - up, 1, keepdims=False)
            held = keep + lax.ppermute(away, "feat", [(i, i ^ bit) for i in range(n_feat)])
            bit *= 2
        return held[0].T

    return jax.shard_map(
        on_device,
        mesh=mesh,
        in_specs=(P(("grp", "ex"), "feat"), P("ex", "feat"), P("feat")),
        out_specs=P(("grp", "ex"), "feat"),
        check_vma=False,
    )
```

```python
import functools

import jax
import jax.numpy as jnp
from jax import lax
from jax.experimental import pallas as pl
from jax.experimental.pallas import tpu as pltpu
from jax.sharding import PartitionSpec as P

CONTRACT = (((1,), (1,)), ((), ()))
CHUNKS = (4, 4, 4, 4)


def scores_kernel(n_grp, n_ex, start, unit, n_rows, has_base, last, *refs):
    test, *received = refs[:n_rows]
    scale, train = refs[n_rows : n_rows + 2]
    out = refs[-2] if last else refs[-1]
    total = refs[-1]
    width = received[0].shape[1]
    sums = refs[n_rows + 2][...] if has_base else None
    for at in range(0, width, unit):
        here, there = slice(at, at + unit), slice(start + at, start + at + unit)
        block = jnp.concatenate([test[:, there]] + [r[:, here] for r in received], axis=0)
        precond = (block.astype(jnp.float32) * scale[:, there]).astype(jnp.bfloat16)
        part = lax.dot_general(
            precond, train[:, there], CONTRACT, preferred_element_type=jnp.float32
        )
        sums = part if sums is None else sums + part
    total[...] = sums
    if last:
        ex, grp = lax.axis_index("ex"), lax.axis_index("grp")
        queries = test.shape[0]
        half = queries // n_grp
        for b in range(n_ex):
            t = lax.rem(ex + (n_ex - b), n_ex)
            for h in range(n_grp):
                place = jnp.where(t == 0, h, lax.rem(h + n_grp - grp, n_grp))
                at = pl.multiple_of(t * queries + place * half, half)
                to = b * queries + h * half
                out[to : to + half, :] = total[pl.ds(at, half), :]


def scores(n_grp, n_ex, test, scale, train, start, unit, received, base, last):
    docs, width = train.shape[0], received[0].shape[1]
    queries = test.shape[0] * n_ex
    operands = [test, *received, scale, train] + ([] if base is None else [base])
    shape = (queries, docs)
    return pl.pallas_call(
        functools.partial(
            scores_kernel, n_grp, n_ex, start, unit, 1 + len(received), base is not None, last
        ),
        out_shape=jax.ShapeDtypeStruct(shape, jnp.float32),
        in_specs=[pl.BlockSpec(memory_space=pltpu.VMEM)] * len(operands),
        out_specs=pl.BlockSpec(memory_space=pltpu.VMEM),
        scratch_shapes=[pltpu.VMEM(shape, jnp.float32)] if last else [],
        cost_estimate=pl.CostEstimate(
            flops=2 * queries * docs * width,
            bytes_accessed=2 * (queries + docs) * width,
            transcendentals=0,
        ),
        compiler_params=pltpu.CompilerParams(vmem_limit_bytes=24 * 1024 * 1024),
    )(*operands)


def solution(mesh):
    n_grp, n_ex, n_feat = (mesh.shape[a] for a in ("grp", "ex", "feat"))
    assert n_grp <= 2

    def on_device(train, test, hess):
        docs, feats = train.shape
        queries = test.shape[0]
        half = queries // n_grp
        unit = feats // sum(CHUNKS)
        grp, feat = lax.axis_index("grp"), lax.axis_index("feat")
        ring = [(i, (i + 1) % n_ex) for i in range(n_ex)]
        hops, swaps = [], []

        def after(block, *waits):
            return lax.optimization_barrier((block, waits))[0] if waits else block

        def hop(block):
            hops.append(lax.ppermute(after(block, *hops[-2:-1], *swaps[-4:-3]), "ex", ring))
            return hops[-1]

        def swap(block):
            if n_grp == 1:
                return [block]
            swaps.append(lax.ppermute(after(block, *swaps[-2:-1]), "grp", [(0, 1), (1, 0)]))
            return [block, swaps[-1]]

        def sum_over_feat(sums):
            held = sums.reshape(n_feat, -1, docs)
            bit = 1
            while bit < n_feat:
                pairs = held.reshape((-1, 2) + held.shape[1:])
                mine = (feat // bit) % 2
                keep = lax.dynamic_index_in_dim(pairs, mine, 1, keepdims=False)
                away = lax.dynamic_index_in_dim(pairs, 1 - mine, 1, keepdims=False)
                held = keep + lax.ppermute(away, "feat", [(i, i ^ bit) for i in range(n_feat)])
                bit *= 2
            return held[0]

        def share(start, width):
            columns = slice(start, start + width)
            if n_grp == 1:
                return test[:, columns]
            return jnp.where(grp == 0, test[:half, columns], test[half:, columns])

        starts, at = [], 0
        for width in CHUNKS:
            starts.append(at)
            at += width * unit
        held = [share(start, width * unit) for start, width in zip(starts, CHUNKS)]
        got = [[] for _ in CHUNKS]
        for t in range(1, n_ex):
            for c in range(len(CHUNKS)):
                held[c] = hop(held[c])
                got[c] += swap(held[c])

        scale = (1.0 / (hess + jnp.float32(0.1))).reshape(1, feats)
        sums = None
        for c, start in enumerate(starts):
            sums = scores(
                n_grp, n_ex, test, scale, train, start, unit, got[c], sums, c == len(CHUNKS) - 1
            )
        return sum_over_feat(sums).T

    return jax.shard_map(
        on_device,
        mesh=mesh,
        in_specs=(P(("grp", "ex"), "feat"), P("ex", "feat"), P("feat")),
        out_specs=P(("grp", "ex"), "feat"),
        check_vma=False,
    )
```

```python
import functools

import jax
import jax.numpy as jnp
from jax import lax
from jax.experimental import pallas as pl
from jax.experimental.pallas import tpu as pltpu
from jax.sharding import PartitionSpec as P

CONTRACT = (((1,), (1,)), ((), ()))
CHUNKS = (4, 4, 4, 4)


def product(rows, scale, train, unit):
    total = None
    for at in range(0, train.shape[1], unit):
        here = slice(at, at + unit)
        precond = (rows(here).astype(jnp.float32) * scale(here)).astype(jnp.bfloat16)
        part = lax.dot_general(
            precond, train[:, here], CONTRACT, preferred_element_type=jnp.float32
        )
        total = part if total is None else total + part
    return total


def own_kernel(starts, unit, test, scale, *refs):
    trains, out = refs[:-1], refs[-1]
    total = None
    for start, train in zip(starts, trains):
        column = lambda here: slice(start + here.start, start + here.stop)
        part = product(lambda here: test[:, column(here)], lambda here: scale[:, column(here)], train, unit)
        total = part if total is None else total + part
    out[...] = total


def arrived_rows(parts):
    return lambda here: jnp.concatenate([p[:, here] for p in parts], axis=0)


def part_kernel(start, unit, n_parts, has_base, *refs):
    parts, (scale, train) = refs[:n_parts], refs[n_parts : n_parts + 2]
    column = lambda here: scale[:, start + here.start : start + here.stop]
    total = product(arrived_rows(parts), column, train, unit)
    refs[-1][...] = total + refs[n_parts + 2][...] if has_base else total


def last_kernel(n_grp, n_ex, start, unit, n_parts, *refs):
    parts, (scale, train) = refs[:n_parts], refs[n_parts : n_parts + 2]
    sums, (out, kept) = refs[n_parts + 2 : -2], refs[-2:]
    column = lambda here: scale[:, start + here.start : start + here.stop]
    total = product(arrived_rows(parts), column, train, unit) + sums[-1][...]
    queries = total.shape[0]
    half = queries // n_grp
    for t, value in enumerate([s[...] for s in sums[:-1]] + [total]):
        kept[t * queries : (t + 1) * queries, :] = value
    ex, grp = lax.axis_index("ex"), lax.axis_index("grp")
    for b in range(n_ex):
        t = lax.rem(ex + (n_ex - b), n_ex)
        for h in range(n_grp):
            place = jnp.where(t == 0, h, lax.rem(h + n_grp - grp, n_grp))
            at = pl.multiple_of(t * queries + place * half, half)
            to = b * queries + h * half
            out[to : to + half, :] = kept[pl.ds(at, half), :]


def call(kernel, rows, docs, width, operands, scratch=()):
    return pl.pallas_call(
        kernel,
        out_shape=jax.ShapeDtypeStruct((rows, docs), jnp.float32),
        in_specs=[pl.BlockSpec(memory_space=pltpu.VMEM)] * len(operands),
        out_specs=pl.BlockSpec(memory_space=pltpu.VMEM),
        scratch_shapes=scratch,
        cost_estimate=pl.CostEstimate(
            flops=2 * rows * docs * width, bytes_accessed=2 * (rows + docs) * width, transcendentals=0
        ),
        compiler_params=pltpu.CompilerParams(vmem_limit_bytes=16 * 1024 * 1024),
    )(*operands)


def solution(mesh):
    n_grp, n_ex, n_feat = (mesh.shape[a] for a in ("grp", "ex", "feat"))
    assert n_grp <= 2

    def on_device(train, test, hess):
        docs, feats = train.shape
        queries = test.shape[0]
        half = queries // n_grp
        unit = feats // sum(CHUNKS)
        grp, feat = lax.axis_index("grp"), lax.axis_index("feat")
        ring = [(i, (i + 1) % n_ex) for i in range(n_ex)]
        hops, swaps, made, first = [], [], [], []

        def after(block, *waits):
            return lax.optimization_barrier((block, waits))[0] if waits else block

        def hop(block):
            waits = hops[-2:-1] + swaps[-4:-3] + made[-6:-5] + (first if len(hops) == 3 else [])
            hops.append(lax.ppermute(after(block, *waits), "ex", ring))
            return hops[-1]

        def swap(block):
            if n_grp == 1:
                return [block]
            swaps.append(lax.ppermute(after(block, *swaps[-2:-1]), "grp", [(0, 1), (1, 0)]))
            return [block, swaps[-1]]

        def sum_over_feat(sums):
            held = sums.reshape(n_feat, -1, docs)
            bit = 1
            while bit < n_feat:
                pairs = held.reshape((-1, 2) + held.shape[1:])
                mine = (feat // bit) % 2
                keep = lax.dynamic_index_in_dim(pairs, mine, 1, keepdims=False)
                away = lax.dynamic_index_in_dim(pairs, 1 - mine, 1, keepdims=False)
                held = keep + lax.ppermute(away, "feat", [(i, i ^ bit) for i in range(n_feat)])
                bit *= 2
            return held[0]

        def share(rows, start, width):
            columns = slice(start, start + width)
            if n_grp == 1:
                return rows[:, columns]
            return jnp.where(grp == 0, rows[:half, columns], rows[half:, columns])

        scale = (1.0 / (hess + jnp.float32(0.1))).reshape(1, feats)
        widths = [width * unit for width in CHUNKS]
        starts = [sum(widths[:c]) for c in range(len(widths))]
        held = []
        for start, width in zip(starts, widths):
            held.append(share(after(test, *held[-1:]), start, width))
        trains = [train[:, start : start + width] for start, width in zip(starts, widths)]
        own = call(
            functools.partial(own_kernel, starts, unit), queries, docs, feats, [test, scale, *trains]
        )
        first.append(own)
        sums = [own]
        for t in range(1, n_ex):
            total = None
            for c, (start, width) in enumerate(zip(starts, widths)):
                held[c] = hop(held[c])
                parts = swap(held[c])
                operands = [*parts, scale, trains[c]]
                if t == n_ex - 1 and c == len(widths) - 1:
                    total = call(
                        functools.partial(last_kernel, n_grp, n_ex, start, unit, len(parts)),
                        n_ex * queries, docs, width, [*operands, *sums, total],
                        [pltpu.VMEM((n_ex * queries, docs), jnp.float32)],
                    )
                else:
                    total = call(
                        functools.partial(part_kernel, start, unit, len(parts), total is not None),
                        queries, docs, width, operands + ([] if total is None else [total]),
                    )
                made.append(total)
            sums.append(total)
        return sum_over_feat(sums[-1]).T


    return jax.shard_map(
        on_device,
        mesh=mesh,
        in_specs=(P(("grp", "ex"), "feat"), P("ex", "feat"), P("feat")),
        out_specs=P(("grp", "ex"), "feat"),
        check_vma=False,
    )
```

```python
import functools

import jax
import jax.numpy as jnp
from jax import lax
from jax.experimental import pallas as pl
from jax.experimental.pallas import tpu as pltpu
from jax.sharding import PartitionSpec as P

CONTRACT = (((1,), (1,)), ((), ()))
CHUNKS = (4, 4, 4, 3, 1)


def product(rows, scale, train, unit):
    total = None
    for at in range(0, train.shape[1], unit):
        here = slice(at, at + unit)
        precond = (rows(here).astype(jnp.float32) * scale(here)).astype(jnp.bfloat16)
        part = lax.dot_general(
            precond, train[:, here], CONTRACT, preferred_element_type=jnp.float32
        )
        total = part if total is None else total + part
    return total


def own_kernel(starts, unit, test, scale, *refs):
    trains, out = refs[:-1], refs[-1]
    total = None
    for start, train in zip(starts, trains):
        column = lambda here: slice(start + here.start, start + here.stop)
        part = product(lambda here: test[:, column(here)], lambda here: scale[:, column(here)], train, unit)
        total = part if total is None else total + part
    out[...] = total


def arrived(groups, scale, refs):
    refs, total = list(refs), None
    for start, unit, count in groups:
        parts, train, refs = refs[:count], refs[count], refs[count + 1 :]
        rows = lambda here: jnp.concatenate([p[:, here] for p in parts], axis=0)
        column = lambda here: scale[:, start + here.start : start + here.stop]
        part = product(rows, column, train, unit)
        total = part if total is None else total + part
    return total, refs


def part_kernel(groups, scale, *refs):
    total, (*base, out) = arrived(groups, scale, refs)
    out[...] = total + base[0][...] if base else total


def last_kernel(n_grp, n_ex, groups, scale, *refs):
    total, (*sums, out, kept) = arrived(groups, scale, refs)
    queries = total.shape[0]
    half = queries // n_grp
    for t, value in enumerate([s[...] for s in sums[:-1]] + [total + sums[-1][...]]):
        kept[t * queries : (t + 1) * queries, :] = value
    ex, grp = lax.axis_index("ex"), lax.axis_index("grp")
    for b in range(n_ex):
        t = lax.rem(ex + (n_ex - b), n_ex)
        for h in range(n_grp):
            place = jnp.where(t == 0, h, lax.rem(h + n_grp - grp, n_grp))
            at = pl.multiple_of(t * queries + place * half, half)
            to = b * queries + h * half
            out[to : to + half, :] = kept[pl.ds(at, half), :]


def call(kernel, rows, docs, width, operands, scratch=()):
    return pl.pallas_call(
        kernel,
        out_shape=jax.ShapeDtypeStruct((rows, docs), jnp.float32),
        in_specs=[pl.BlockSpec(memory_space=pltpu.VMEM)] * len(operands),
        out_specs=pl.BlockSpec(memory_space=pltpu.VMEM),
        scratch_shapes=scratch,
        cost_estimate=pl.CostEstimate(
            flops=2 * rows * docs * width, bytes_accessed=2 * (rows + docs) * width, transcendentals=0
        ),
        compiler_params=pltpu.CompilerParams(vmem_limit_bytes=4 * 1024 * 1024),
    )(*operands)


def solution(mesh):
    n_grp, n_ex, n_feat = (mesh.shape[a] for a in ("grp", "ex", "feat"))
    assert n_grp <= 2

    def on_device(train, test, hess):
        docs, feats = train.shape
        queries = test.shape[0]
        half = queries // n_grp
        unit = feats // sum(CHUNKS)
        grp, feat = lax.axis_index("grp"), lax.axis_index("feat")
        ring = [(i, (i + 1) % n_ex) for i in range(n_ex)]
        hops, swaps, made, first = [], [], [], []

        def after(block, *waits):
            return lax.optimization_barrier((block, waits))[0] if waits else block

        def hop(block):
            waits = hops[-2:-1] + swaps[-4:-3] + (first if len(hops) == 3 else [])
            hops.append(lax.ppermute(after(block, *waits), "ex", ring))
            return hops[-1]

        def swap(block):
            if n_grp == 1:
                return [block]
            waits = swaps[-2:-1] + made[-3:-2]
            swaps.append(lax.ppermute(after(block, *waits), "grp", [(0, 1), (1, 0)]))
            return [block, swaps[-1]]

        def sum_over_feat(sums):
            held = sums.reshape(n_feat, -1, docs)
            bit = 1
            while bit < n_feat:
                pairs = held.reshape((-1, 2) + held.shape[1:])
                mine = (feat // bit) % 2
                keep = lax.dynamic_index_in_dim(pairs, mine, 1, keepdims=False)
                away = lax.dynamic_index_in_dim(pairs, 1 - mine, 1, keepdims=False)
                held = keep + lax.ppermute(away, "feat", [(i, i ^ bit) for i in range(n_feat)])
                bit *= 2
            return held[0]

        def share(rows, start, width, other):
            columns = slice(start, start + width)
            if n_grp == 1:
                return rows[:, columns]
            return jnp.where(grp == other, rows[:half, columns], rows[half:, columns])

        scale = (1.0 / (hess + jnp.float32(0.1))).reshape(1, feats)
        widths = [width * unit for width in CHUNKS]
        starts = [sum(widths[:c]) for c in range(len(widths))]
        held = []
        for c, (start, width) in enumerate(zip(starts, widths)):
            rows = after(test, *held[-1:])
            mine = share(rows, start, width, 0)
            if c == len(widths) - 1 and n_grp > 1:
                mine = jnp.concatenate([mine, share(rows, start, width, 1)])
            held.append(mine)
        trains = [train[:, start : start + width] for start, width in zip(starts, widths)]
        own = call(
            functools.partial(own_kernel, starts, unit), queries, docs, feats, [test, scale, *trains]
        )
        first.append(own)
        final, whole = n_ex - 1, len(widths) - 1
        order = [(t, c) for t in range(1, final) for c in range(whole)]
        waiting = [(t, whole) for t in range(1, n_ex)]
        for c in range(whole):
            order.append((final, c))
            order += [waiting.pop(0) for _ in range(len(waiting) // (whole - c))]

        sums, groups, operands = [own] + [None] * final, [], []
        for t, c in order:
            held[c] = hop(held[c])
            parts = [held[c]] if c == whole else swap(held[c])
            group, arrays = (starts[c], unit, len(parts)), [*parts, trains[c]]
            if t == final and c >= whole - 1:
                groups.append(group)
                operands += arrays
                continue
            base = [] if sums[t] is None else [sums[t]]
            sums[t] = call(
                functools.partial(part_kernel, [group]), queries, docs, widths[c], [scale, *arrays, *base]
            )
            made.append(sums[t])
        out = call(
            functools.partial(last_kernel, n_grp, n_ex, groups),
            n_ex * queries, docs, sum(widths[whole - 1 :]), [scale, *operands, *sums],
            [pltpu.VMEM((n_ex * queries, docs), jnp.float32)],
        )
        return sum_over_feat(out).T


    return jax.shard_map(
        on_device,
        mesh=mesh,
        in_specs=(P(("grp", "ex"), "feat"), P("ex", "feat"), P("feat")),
        out_specs=P(("grp", "ex"), "feat"),
        check_vma=False,
    )
```

```python
import functools

import jax
import jax.numpy as jnp
from jax import lax
from jax.experimental import pallas as pl
from jax.experimental.pallas import tpu as pltpu
from jax.sharding import PartitionSpec as P

CONTRACT = (((1,), (1,)), ((), ()))
CHUNKS = (4, 4, 4, 3, 1)


def fetches(sems, rows, train, rows_buf, train_buf, start, unit):
    copies, at = [], 0
    for block in rows:
        copies.append((block, rows_buf.at[pl.ds(at, block.shape[0]), :]))
        at += block.shape[0]
    for col in range(0, train_buf.shape[1], unit):
        there = train_buf.at[:, pl.ds(col, unit)]
        copies.append((train.at[:, pl.ds(start + col, unit)], there))
    return [pltpu.make_async_copy(*copy, sems.at[i]) for i, copy in enumerate(copies)]


def scores_kernel(n_grp, n_ex, groups, unit, has_base, last, *refs):
    test, scale, train, *refs = refs
    blocks = []
    for start, width, count in groups:
        blocks.append([test.at[:, pl.ds(start, width)]] + refs[:count])
        refs = refs[count:]
    base, refs = (refs[0], refs[1:]) if has_base else (None, refs)
    out, refs = refs[0], refs[1:]
    kept, refs = (refs[0], refs[1:]) if last else (out, refs)
    pending = []
    for i, (start, width, _) in enumerate(groups):
        rows_buf, train_buf, sems = refs[3 * i : 3 * i + 3]
        pending.append(fetches(sems, blocks[i], train, rows_buf, train_buf, start, unit))
        for copy in pending[-1]:
            copy.start()
    total = None if base is None else base[...]
    for i, (start, width, _) in enumerate(groups):
        rows_buf, train_buf, _ = refs[3 * i : 3 * i + 3]
        count = len(blocks[i])
        for copy in pending[i][:count]:
            copy.wait()
        for step, col in enumerate(range(0, width, unit)):
            pending[i][count + step].wait()
            columns = scale[:, start + col : start + col + unit]
            here = slice(col, col + unit)
            precond = (rows_buf[:, here].astype(jnp.float32) * columns).astype(jnp.bfloat16)
            part = lax.dot_general(
                precond, train_buf[:, here], CONTRACT, preferred_element_type=jnp.float32
            )
            total = part if total is None else total + part
    kept[...] = total
    if last:
        ex, grp = lax.axis_index("ex"), lax.axis_index("grp")
        queries = test.shape[0]
        half = queries // n_grp
        for b in range(n_ex):
            t = lax.rem(ex + (n_ex - b), n_ex)
            for h in range(n_grp):
                place = jnp.where(t == 0, h, lax.rem(h + n_grp - grp, n_grp))
                at = pl.multiple_of(t * queries + place * half, half)
                to = b * queries + h * half
                out[to : to + half, :] = kept[pl.ds(at, half), :]


def scores(n_grp, n_ex, test, scale, train, unit, groups, base, last):
    docs = train.shape[0]
    queries = test.shape[0] * n_ex
    shape = jax.ShapeDtypeStruct((queries, docs), jnp.float32)
    hbm, vmem = pl.BlockSpec(memory_space=pltpu.HBM), pl.BlockSpec(memory_space=pltpu.VMEM)
    blocks = [block for _, _, received in groups for block in received]
    width = sum(w for _, w, _ in groups)
    scratch = [pltpu.VMEM(shape.shape, shape.dtype)] if last else []
    for _, w, received in groups:
        scratch += [
            pltpu.VMEM((queries, w), test.dtype),
            pltpu.VMEM((docs, w), train.dtype),
            pltpu.SemaphoreType.DMA((1 + len(received) + w // unit,)),
        ]
    kernel = functools.partial(
        scores_kernel, n_grp, n_ex, [(s, w, len(r)) for s, w, r in groups], unit, base is not None, last
    )
    return pl.pallas_call(
        kernel,
        out_shape=shape,
        in_specs=[hbm, vmem, hbm] + [hbm] * len(blocks) + ([] if base is None else [vmem]),
        out_specs=vmem,
        scratch_shapes=scratch,
        cost_estimate=pl.CostEstimate(
            flops=2 * queries * docs * width, bytes_accessed=2 * (queries + docs) * width, transcendentals=0
        ),
        compiler_params=pltpu.CompilerParams(vmem_limit_bytes=12 * 1024 * 1024),
    )(test, scale, train, *blocks, *([] if base is None else [base]))


def solution(mesh):
    n_grp, n_ex, n_feat = (mesh.shape[a] for a in ("grp", "ex", "feat"))
    assert n_grp <= 2

    def on_device(train, test, hess):
        docs, feats = train.shape
        queries = test.shape[0]
        half = queries // n_grp
        unit = feats // sum(CHUNKS)
        grp, feat = lax.axis_index("grp"), lax.axis_index("feat")
        ring = [(i, (i + 1) % n_ex) for i in range(n_ex)]
        hops, swaps = [], []

        def after(block, *waits):
            return lax.optimization_barrier((block, waits))[0] if waits else block

        def hop(block):
            hops.append(lax.ppermute(after(block, *hops[-2:-1], *swaps[-4:-3]), "ex", ring))
            return hops[-1]

        def swap(block):
            if n_grp == 1:
                return [block]
            swaps.append(lax.ppermute(after(block, *swaps[-2:-1]), "grp", [(0, 1), (1, 0)]))
            return [block, swaps[-1]]

        def sum_over_feat(sums):
            held = sums.reshape(n_feat, -1, docs)
            bit = 1
            while bit < n_feat:
                pairs = held.reshape((-1, 2) + held.shape[1:])
                mine = (feat // bit) % 2
                keep = lax.dynamic_index_in_dim(pairs, mine, 1, keepdims=False)
                away = lax.dynamic_index_in_dim(pairs, 1 - mine, 1, keepdims=False)
                held = keep + lax.ppermute(away, "feat", [(i, i ^ bit) for i in range(n_feat)])
                bit *= 2
            return held[0]

        def share(rows, start, width, other):
            columns = slice(start, start + width)
            if n_grp == 1:
                return rows[:, columns]
            return jnp.where(grp == other, rows[:half, columns], rows[half:, columns])

        scale = (1.0 / (hess + jnp.float32(0.1))).reshape(1, feats)
        widths = [width * unit for width in CHUNKS]
        starts = [sum(widths[:c]) for c in range(len(widths))]
        held = []
        for c, (start, width) in enumerate(zip(starts, widths)):
            rows = after(test, *held[-1:])
            mine = share(rows, start, width, 0)
            if c == len(widths) - 1 and n_grp > 1:
                mine = jnp.concatenate([mine, share(rows, start, width, 1)])
            held.append(mine)
        final, whole = n_ex - 1, len(widths) - 1
        order = [(t, c) for t in range(1, final) for c in range(whole)] + [(1, whole)]
        order += [(final, c) for c in range(whole - 1)] + [(t, whole) for t in range(2, final)]
        order += [(final, whole - 1), (final, whole)]

        got = [[] for _ in widths]
        for t, c in order:
            held[c] = hop(held[c])
            got[c] += [held[c]] if c == whole else swap(held[c])
        sums = None
        groups = list(zip(starts, widths, got))
        for group in [groups[c : c + 1] for c in range(whole - 1)] + [groups[whole - 1 :]]:
            sums = scores(n_grp, n_ex, test, scale, train, unit, group, sums, len(group) > 1)
        return sum_over_feat(sums).T

    return jax.shard_map(
        on_device,
        mesh=mesh,
        in_specs=(P(("grp", "ex"), "feat"), P("ex", "feat"), P("feat")),
        out_specs=P(("grp", "ex"), "feat"),
        check_vma=False,
    )
```

```python
import functools

import jax
import jax.numpy as jnp
from jax import lax
from jax.experimental import pallas as pl
from jax.experimental.pallas import tpu as pltpu
from jax.sharding import PartitionSpec as P

CONTRACT = (((1,), (1,)), ((), ()))
CHUNKS = (4, 4, 4, 3, 1)


def rounds(n_ex):
    if n_ex == 4:
        near, far = ([(i, i ^ x) for i in range(4)] for x in (1, 3))
        return [(0, near), (0, far), (2, near)], lambda ex, b: _select(ex ^ b, (0, 1, 3, 2))
    ring = [(i, (i + 1) % n_ex) for i in range(n_ex)]
    return [(t, ring) for t in range(n_ex - 1)], lambda ex, b: lax.rem(ex + (n_ex - b), n_ex)


def _select(index, values):
    found = jnp.int32(values[0])
    for i, value in enumerate(values[1:], 1):
        found = jnp.where(index == i, value, found)
    return found


def scores_kernel(n_grp, n_ex, groups, unit, has_base, last, *refs):
    test, scale, *refs = refs
    total = None
    for start, count in groups:
        blocks, train, refs = refs[:count], refs[count], refs[count + 1 :]
        for at in range(0, train.shape[1], unit):
            here, there = slice(at, at + unit), slice(start + at, start + at + unit)
            rows = jnp.concatenate([test[:, there]] + [r[:, here] for r in blocks], axis=0)
            precond = (rows.astype(jnp.float32) * scale[:, there]).astype(jnp.bfloat16)
            part = lax.dot_general(
                precond, train[:, here], CONTRACT, preferred_element_type=jnp.float32
            )
            total = part if total is None else total + part
    if has_base:
        total += refs[0][...]
    if not last:
        refs[-1][...] = total
        return
    out, kept = refs[-2:]
    kept[...] = total
    ex, grp = lax.axis_index("ex"), lax.axis_index("grp")
    queries = test.shape[0]
    half = queries // n_grp
    for b in range(n_ex):
        t = rounds(n_ex)[1](ex, b)
        for h in range(n_grp):
            place = jnp.where(t == 0, h, lax.rem(h + n_grp - grp, n_grp))
            at = pl.multiple_of(t * queries + place * half, half)
            to = b * queries + h * half
            out[to : to + half, :] = kept[pl.ds(at, half), :]


def scores(n_grp, n_ex, test, scale, unit, groups, base, last):
    docs = groups[0][2].shape[0]
    shape = (test.shape[0] * n_ex, docs)
    operands = [test, scale]
    for _, blocks, train in groups:
        operands += [*blocks, train]
    operands += [] if base is None else [base]
    width = sum(train.shape[1] for _, _, train in groups)
    return pl.pallas_call(
        functools.partial(
            scores_kernel, n_grp, n_ex, [(s, len(r)) for s, r, _ in groups], unit, base is not None, last
        ),
        out_shape=jax.ShapeDtypeStruct(shape, jnp.float32),
        in_specs=[pl.BlockSpec(memory_space=pltpu.VMEM)] * len(operands),
        out_specs=pl.BlockSpec(memory_space=pltpu.VMEM),
        scratch_shapes=[pltpu.VMEM(shape, jnp.float32)] if last else [],
        cost_estimate=pl.CostEstimate(
            flops=2 * shape[0] * docs * width,
            bytes_accessed=2 * (shape[0] + docs) * width,
            transcendentals=0,
        ),
        compiler_params=pltpu.CompilerParams(vmem_limit_bytes=12 * 1024 * 1024),
    )(*operands)


def solution(mesh):
    n_grp, n_ex, n_feat = (mesh.shape[a] for a in ("grp", "ex", "feat"))
    assert n_grp <= 2

    def on_device(train, test, hess):
        docs, feats = train.shape
        queries = test.shape[0]
        half = queries // n_grp
        unit = feats // sum(CHUNKS)
        grp, feat = lax.axis_index("grp"), lax.axis_index("feat")
        plan, _ = rounds(n_ex)
        hops, swaps = [], []

        def after(block, *waits):
            return lax.optimization_barrier((block, waits))[0] if waits else block

        def hop(block, pairs, *ahead):
            waits = [*hops[-2:-1], *swaps[-4:-3], *ahead]
            hops.append(lax.ppermute(after(block, *waits), "ex", pairs))
            return hops[-1]

        def swap(block):
            if n_grp == 1:
                return [block]
            swaps.append(lax.ppermute(after(block, *swaps[-2:-1]), "grp", [(0, 1), (1, 0)]))
            return [block, swaps[-1]]

        def sum_over_feat(sums):
            held = sums.reshape(n_feat, -1, docs)
            bit = 1
            while bit < n_feat:
                pairs = held.reshape((-1, 2) + held.shape[1:])
                mine = (feat // bit) % 2
                keep = lax.dynamic_index_in_dim(pairs, mine, 1, keepdims=False)
                away = lax.dynamic_index_in_dim(pairs, 1 - mine, 1, keepdims=False)
                held = keep + lax.ppermute(away, "feat", [(i, i ^ bit) for i in range(n_feat)])
                bit *= 2
            return held[0]

        def share(rows, start, width, other):
            columns = slice(start, start + width)
            if n_grp == 1:
                return rows[:, columns]
            return jnp.where(grp == other, rows[:half, columns], rows[half:, columns])

        scale = (1.0 / (hess + jnp.float32(0.1))).reshape(1, feats)
        widths = [width * unit for width in CHUNKS]
        starts = [sum(widths[:c]) for c in range(len(widths))]
        whole, final = len(widths) - 1, n_ex - 1
        held = []
        for c, (start, width) in enumerate(zip(starts, widths)):
            rows = after(test, *[h[0] for h in held[-1:]])
            mine = share(rows, start, width, 0)
            if c == whole and n_grp > 1:
                mine = jnp.concatenate([mine, share(rows, start, width, 1)])
            held.append({0: mine})
        trains = [train[:, start : start + width] for start, width in zip(starts, widths)]

        if n_ex == 4:
            order = [(0, 1), (0, 2)]
            for c in range(1, whole):
                order += [(c, 1), (c - 1, 3), (c, 2)]
            order += [(whole, 2), (whole - 1, 3), (whole, 1), (whole, 3)]
        else:
            order = [(c, t) for t in range(1, n_ex) for c in range(whole + 1)]

        got = [[None] * final for _ in widths]
        sums, made = None, []
        for j, (c, t) in enumerate(order):
            source, pairs = plan[t - 1]
            ahead = [m for at, m in made if at == j - 5]
            ahead += trains[whole - 1 :] if j == len(order) - 3 else []
            held[c][t] = hop(held[c][source], pairs, *ahead)
            got[c][t - 1] = [held[c][t]] if c == whole else swap(held[c][t])
            if t == final and c < whole - 1:
                group = (starts[c], sum(got[c], []), trains[c])
                sums = scores(n_grp, n_ex, test, scale, unit, [group], sums, False)
                made.append((j, sums))
        blocks = [sum(parts, []) for parts in got]
        groups = list(zip(starts, blocks, trains))[whole - 1 :]
        return sum_over_feat(scores(n_grp, n_ex, test, scale, unit, groups, sums, True)).T

    return jax.shard_map(
        on_device,
        mesh=mesh,
        in_specs=(P(("grp", "ex"), "feat"), P("ex", "feat"), P("feat")),
        out_specs=P(("grp", "ex"), "feat"),
        check_vma=False,
    )
```

```python
import functools

import jax
import jax.numpy as jnp
from jax import lax
from jax.experimental import pallas as pl
from jax.experimental.pallas import tpu as pltpu
from jax.sharding import PartitionSpec as P

CONTRACT = (((1,), (1,)), ((), ()))
CHUNKS = (4, 4, 4, 3, 1)


def product(rows, scale, train, unit):
    total = None
    for at in range(0, train.shape[1], unit):
        here = slice(at, at + unit)
        precond = (rows(here).astype(jnp.float32) * scale(here)).astype(jnp.bfloat16)
        part = lax.dot_general(
            precond, train[:, here], CONTRACT, preferred_element_type=jnp.float32
        )
        total = part if total is None else total + part
    return total


def own_kernel(starts, unit, test, scale, *refs):
    trains, out = refs[:-1], refs[-1]
    total = None
    for start, train in zip(starts, trains):
        column = lambda here: slice(start + here.start, start + here.stop)
        part = product(lambda here: test[:, column(here)], lambda here: scale[:, column(here)], train, unit)
        total = part if total is None else total + part
    out[...] = total


def arrived_rows(parts):
    return lambda here: jnp.concatenate([p[:, here] for p in parts], axis=0)


def part_kernel(start, unit, n_parts, has_base, *refs):
    parts, (scale, train) = refs[:n_parts], refs[n_parts : n_parts + 2]
    column = lambda here: scale[:, start + here.start : start + here.stop]
    total = product(arrived_rows(parts), column, train, unit)
    refs[-1][...] = total + refs[n_parts + 2][...] if has_base else total


def last_kernel(n_grp, n_ex, starts, unit, n_parts, *refs):
    parts, (scale, train), refs = refs[:n_parts], refs[n_parts : n_parts + 2], refs[n_parts + 2 :]
    wholes, (whole_train, *sums), (out, kept) = refs[: n_ex - 1], refs[n_ex - 1 : -2], refs[-2:]
    columns = lambda start: lambda here: scale[:, start + here.start : start + here.stop]
    total = product(arrived_rows(parts), columns(starts[0]), train, unit)
    queries = total.shape[0]
    half = queries // n_grp
    for t, value in enumerate(sums):
        value = value[...]
        if t > 0:
            value += product(arrived_rows([wholes[t - 1]]), columns(starts[1]), whole_train, unit)
        if t == n_ex - 1:
            value += total
        kept[t * queries : (t + 1) * queries, :] = value
    ex, grp = lax.axis_index("ex"), lax.axis_index("grp")
    for b in range(n_ex):
        t = lax.rem(ex + (n_ex - b), n_ex)
        for h in range(n_grp):
            place = jnp.where(t == 0, h, lax.rem(h + n_grp - grp, n_grp))
            at = pl.multiple_of(t * queries + place * half, half)
            to = b * queries + h * half
            out[to : to + half, :] = kept[pl.ds(at, half), :]


def call(kernel, rows, docs, width, operands, scratch=()):
    return pl.pallas_call(
        kernel,
        out_shape=jax.ShapeDtypeStruct((rows, docs), jnp.float32),
        in_specs=[pl.BlockSpec(memory_space=pltpu.VMEM)] * len(operands),
        out_specs=pl.BlockSpec(memory_space=pltpu.VMEM),
        scratch_shapes=scratch,
        cost_estimate=pl.CostEstimate(
            flops=2 * rows * docs * width, bytes_accessed=2 * (rows + docs) * width, transcendentals=0
        ),
        compiler_params=pltpu.CompilerParams(vmem_limit_bytes=16 * 1024 * 1024),
    )(*operands)


def solution(mesh):
    n_grp, n_ex, n_feat = (mesh.shape[a] for a in ("grp", "ex", "feat"))
    assert n_grp <= 2

    def on_device(train, test, hess):
        docs, feats = train.shape
        queries = test.shape[0]
        half = queries // n_grp
        unit = feats // sum(CHUNKS)
        grp, feat = lax.axis_index("grp"), lax.axis_index("feat")
        ring = [(i, (i + 1) % n_ex) for i in range(n_ex)]
        hops, swaps, made, first = [], [], [], []

        def after(block, *waits):
            return lax.optimization_barrier((block, waits))[0] if waits else block

        def hop(block):
            waits = hops[-2:-1] + swaps[-4:-3] + made[-5:-4] + (first if len(hops) == 3 else [])
            hops.append(lax.ppermute(after(block, *waits), "ex", ring))
            return hops[-1]

        def swap(block):
            if n_grp == 1:
                return [block]
            swaps.append(lax.ppermute(after(block, *swaps[-2:-1]), "grp", [(0, 1), (1, 0)]))
            return [block, swaps[-1]]

        def sum_over_feat(sums):
            held = sums.reshape(n_feat, -1, docs)
            bit = 1
            while bit < n_feat:
                pairs = held.reshape((-1, 2) + held.shape[1:])
                mine = (feat // bit) % 2
                keep = lax.dynamic_index_in_dim(pairs, mine, 1, keepdims=False)
                away = lax.dynamic_index_in_dim(pairs, 1 - mine, 1, keepdims=False)
                held = keep + lax.ppermute(away, "feat", [(i, i ^ bit) for i in range(n_feat)])
                bit *= 2
            return held[0]

        def share(rows, start, width, other=0):
            columns = slice(start, start + width)
            if n_grp == 1:
                return rows[:, columns]
            return jnp.where(grp == other, rows[:half, columns], rows[half:, columns])

        scale = (1.0 / (hess + jnp.float32(0.1))).reshape(1, feats)
        widths = [width * unit for width in CHUNKS]
        starts = [sum(widths[:c]) for c in range(len(widths))]
        held = []
        final, whole = n_ex - 1, len(widths) - 1
        for c, (start, width) in enumerate(zip(starts, widths)):
            rows = after(test, *held[-1:])
            mine = share(rows, start, width)
            if c == whole and n_grp > 1:
                mine = jnp.concatenate([mine, share(rows, start, width, 1)])
            held.append(mine)
        trains = [train[:, start : start + width] for start, width in zip(starts, widths)]
        own = call(
            functools.partial(own_kernel, starts, unit), queries, docs, feats, [test, scale, *trains]
        )
        first.append(own)
        order = [(t, c) for t in range(1, n_ex) for c in range(whole)]
        order[-whole + 1 : -whole + 1] = [(t, whole) for t in range(1, final - 1)]
        order += [(t, whole) for t in range(max(final - 1, 1), n_ex)]
        sums, wholes = [own] + [None] * final, []
        for t, c in order:
            held[c] = hop(held[c])
            if c == whole:
                wholes.append(held[c])
                continue
            parts = swap(held[c])
            operands = [*parts, scale, trains[c]]
            if (t, c) == (final, whole - 1):
                last = operands
                continue
            base = [] if sums[t] is None else [sums[t]]
            sums[t] = call(
                functools.partial(part_kernel, starts[c], unit, len(parts), len(base)),
                queries, docs, widths[c], operands + base,
            )
            made.append(sums[t])
        total = call(
            functools.partial(last_kernel, n_grp, n_ex, starts[-2:], unit, len(last) - 2),
            n_ex * queries, docs, sum(widths[-2:]), [*last, *wholes, trains[whole], *sums],
            [pltpu.VMEM((n_ex * queries, docs), jnp.float32)],
        )
        return sum_over_feat(total).T

    return jax.shard_map(
        on_device,
        mesh=mesh,
        in_specs=(P(("grp", "ex"), "feat"), P("ex", "feat"), P("feat")),
        out_specs=P(("grp", "ex"), "feat"),
        check_vma=False,
    )
```

```python
import functools

import jax
import jax.numpy as jnp
from jax import lax
from jax.experimental import pallas as pl
from jax.experimental.pallas import tpu as pltpu
from jax.sharding import PartitionSpec as P

CONTRACT = (((1,), (1,)), ((), ()))
CHUNKS = (4, 4, 4, 4)


def product(rows, scale, train, unit):
    total = None
    for at in range(0, train.shape[1], unit):
        here = slice(at, at + unit)
        precond = (rows(here).astype(jnp.float32) * scale(here)).astype(jnp.bfloat16)
        part = lax.dot_general(
            precond, train[:, here], CONTRACT, preferred_element_type=jnp.float32
        )
        total = part if total is None else total + part
    return total


def own_kernel(starts, unit, test, scale, *refs):
    trains, out = refs[:-1], refs[-1]
    total = None
    for start, train in zip(starts, trains):
        column = lambda here: slice(start + here.start, start + here.stop)
        part = product(lambda here: test[:, column(here)], lambda here: scale[:, column(here)], train, unit)
        total = part if total is None else total + part
    out[...] = total


def arrived_rows(parts):
    return lambda here: jnp.concatenate([p[:, here] for p in parts], axis=0)


def part_kernel(start, unit, n_parts, has_base, *refs):
    parts, (scale, train) = refs[:n_parts], refs[n_parts : n_parts + 2]
    column = lambda here: scale[:, start + here.start : start + here.stop]
    total = product(arrived_rows(parts), column, train, unit)
    refs[-1][...] = total + refs[n_parts + 2][...] if has_base else total


def last_kernel(n_grp, n_ex, start, unit, n_parts, *refs):
    parts, (scale, train) = refs[:n_parts], refs[n_parts : n_parts + 2]
    sums, (out, kept) = refs[n_parts + 2 : -2], refs[-2:]
    column = lambda here: scale[:, start + here.start : start + here.stop]
    total = product(arrived_rows(parts), column, train, unit) + sums[-1][...]
    queries = total.shape[0]
    half = queries // n_grp
    for t, value in enumerate([s[...] for s in sums[:-1]] + [total]):
        kept[t * queries : (t + 1) * queries, :] = value
    ex, grp = lax.axis_index("ex"), lax.axis_index("grp")
    for b in range(n_ex):
        t = lax.rem(ex + (n_ex - b), n_ex)
        for h in range(n_grp):
            place = jnp.where(t == 0, h, lax.rem(h + n_grp - grp, n_grp))
            at = pl.multiple_of(t * queries + place * half, half)
            to = b * queries + h * half
            out[to : to + half, :] = kept[pl.ds(at, half), :]


def call(kernel, rows, docs, width, operands, scratch=()):
    return pl.pallas_call(
        kernel,
        out_shape=jax.ShapeDtypeStruct((rows, docs), jnp.float32),
        in_specs=[pl.BlockSpec(memory_space=pltpu.VMEM)] * len(operands),
        out_specs=pl.BlockSpec(memory_space=pltpu.VMEM),
        scratch_shapes=scratch,
        cost_estimate=pl.CostEstimate(
            flops=2 * rows * docs * width, bytes_accessed=2 * (rows + docs) * width, transcendentals=0
        ),
        compiler_params=pltpu.CompilerParams(vmem_limit_bytes=16 * 1024 * 1024),
    )(*operands)


def solution(mesh):
    n_grp, n_ex, n_feat = (mesh.shape[a] for a in ("grp", "ex", "feat"))
    assert n_grp <= 2

    def on_device(train, test, hess):
        docs, feats = train.shape
        queries = test.shape[0]
        half = queries // n_grp
        unit = feats // sum(CHUNKS)
        grp, feat = lax.axis_index("grp"), lax.axis_index("feat")
        ring = [(i, (i + 1) % n_ex) for i in range(n_ex)]
        hops, swaps, made, first = [], [], [], []

        def after(block, *waits):
            return lax.optimization_barrier((block, waits))[0] if waits else block

        def hop(block):
            waits = hops[-2:-1] + swaps[-4:-3] + made[-5:-4] + (first if len(hops) == 3 else [])
            hops.append(lax.ppermute(after(block, *waits), "ex", ring))
            return hops[-1]

        def swap(block):
            if n_grp == 1:
                return [block]
            swaps.append(lax.ppermute(after(block, *swaps[-2:-1]), "grp", [(0, 1), (1, 0)]))
            return [block, swaps[-1]]

        def sum_over_feat(sums):
            held = sums.reshape(n_feat, -1, docs)
            bit = 1
            while bit < n_feat:
                pairs = held.reshape((-1, 2) + held.shape[1:])
                mine = (feat // bit) % 2
                keep = lax.dynamic_index_in_dim(pairs, mine, 1, keepdims=False)
                away = lax.dynamic_index_in_dim(pairs, 1 - mine, 1, keepdims=False)
                held = keep + lax.ppermute(away, "feat", [(i, i ^ bit) for i in range(n_feat)])
                bit *= 2
            return held[0]

        def share(rows, start, width):
            columns = slice(start, start + width)
            if n_grp == 1:
                return rows[:, columns]
            return jnp.where(grp == 0, rows[:half, columns], rows[half:, columns])

        scale = (1.0 / (hess + jnp.float32(0.1))).reshape(1, feats)
        widths = [width * unit for width in CHUNKS]
        starts = [sum(widths[:c]) for c in range(len(widths))]
        held = []
        for start, width in zip(starts, widths):
            held.append(share(after(test, *held[-1:]), start, width))
        trains = [train[:, start : start + width] for start, width in zip(starts, widths)]
        own = call(
            functools.partial(own_kernel, starts, unit), queries, docs, feats, [test, scale, *trains]
        )
        first.append(own)
        sums = [own]
        for t in range(1, n_ex):
            total = None
            for c, (start, width) in enumerate(zip(starts, widths)):
                held[c] = hop(held[c])
                parts = swap(held[c])
                operands = [*parts, scale, trains[c]]
                if t == n_ex - 1 and c == len(widths) - 1:
                    total = call(
                        functools.partial(last_kernel, n_grp, n_ex, start, unit, len(parts)),
                        n_ex * queries, docs, width, [*operands, *sums, total],
                        [pltpu.VMEM((n_ex * queries, docs), jnp.float32)],
                    )
                else:
                    total = call(
                        functools.partial(part_kernel, start, unit, len(parts), total is not None),
                        queries, docs, width, operands + ([] if total is None else [total]),
                    )
                made.append(total)
            sums.append(total)
        return sum_over_feat(sums[-1]).T


    return jax.shard_map(
        on_device,
        mesh=mesh,
        in_specs=(P(("grp", "ex"), "feat"), P("ex", "feat"), P("feat")),
        out_specs=P(("grp", "ex"), "feat"),
        check_vma=False,
    )
```

```python
import functools

import jax
import jax.numpy as jnp
from jax import lax
from jax.experimental import pallas as pl
from jax.experimental.pallas import tpu as pltpu
from jax.sharding import PartitionSpec as P

CONTRACT = (((1,), (1,)), ((), ()))
LANES = 128
CHUNKS, SHARE = 4, 15 / 64


def product(rows, scale, train, unit, width, skip=0):
    total = None
    for at in range(0, width, unit):
        here = slice(at, min(at + unit, width))
        precond = (rows(here).astype(jnp.float32) * scale(here)).astype(jnp.bfloat16)
        there = train[:, skip + here.start : skip + here.stop]
        part = lax.dot_general(precond, there, CONTRACT, preferred_element_type=jnp.float32)
        total = part if total is None else total + part
    return total


def own_kernel(starts, unit, test, scale, *refs):
    trains, out = refs[:-1], refs[-1]
    total = None
    for start, train in zip(starts, trains):
        column = lambda here: slice(start + here.start, start + here.stop)
        rows, scales = (lambda here, a=a: a[:, column(here)] for a in (test, scale))
        part = product(rows, scales, train, unit, train.shape[1])
        total = part if total is None else total + part
    out[...] = total


def arrived_rows(parts):
    return lambda here: jnp.concatenate([p[:, here] for p in parts], axis=0)


def part_kernel(start, unit, n_parts, has_base, *refs):
    parts, (scale, train) = refs[:n_parts], refs[n_parts : n_parts + 2]
    column = lambda here: scale[:, start + here.start : start + here.stop]
    total = product(arrived_rows(parts), column, train, unit, parts[0].shape[1])
    refs[-1][...] = total + refs[n_parts + 2][...] if has_base else total


def last_kernel(n_grp, n_ex, starts, unit, n_parts, *refs):
    parts, (scale, train), refs = refs[:n_parts], refs[n_parts : n_parts + 2], refs[n_parts + 2 :]
    wholes, sums, (out, kept) = refs[: n_ex - 1], refs[n_ex - 1 : -2], refs[-2:]
    width, left = parts[0].shape[1], wholes[0].shape[1]
    columns = lambda start: lambda here: scale[:, start + here.start : start + here.stop]
    total = product(arrived_rows(parts), columns(starts[0]), train, unit, width)
    queries = total.shape[0]
    half = queries // n_grp
    for t, value in enumerate(sums):
        value = value[...]
        if t > 0:
            rows = arrived_rows(wholes[t - 1 : t])
            value += product(rows, columns(starts[1]), train, unit, left, width)
        if t == n_ex - 1:
            value += total
        kept[t * queries : (t + 1) * queries, :] = value
    ex, grp = lax.axis_index("ex"), lax.axis_index("grp")
    for b in range(n_ex):
        t = lax.rem(ex + (n_ex - b), n_ex)
        for h in range(n_grp):
            place = jnp.where(t == 0, h, lax.rem(h + n_grp - grp, n_grp))
            at = pl.multiple_of(t * queries + place * half, half)
            to = b * queries + h * half
            out[to : to + half, :] = kept[pl.ds(at, half), :]


def call(kernel, rows, docs, width, operands, scratch=()):
    return pl.pallas_call(
        kernel,
        out_shape=jax.ShapeDtypeStruct((rows, docs), jnp.float32),
        in_specs=[pl.BlockSpec(memory_space=pltpu.VMEM)] * len(operands),
        out_specs=pl.BlockSpec(memory_space=pltpu.VMEM),
        scratch_shapes=scratch,
        cost_estimate=pl.CostEstimate(
            flops=2 * rows * docs * width, bytes_accessed=2 * (rows + docs) * width, transcendentals=0
        ),
        compiler_params=pltpu.CompilerParams(vmem_limit_bytes=16 * 1024 * 1024),
    )(*operands)


def solution(mesh):
    n_grp, n_ex, n_feat = (mesh.shape[a] for a in ("grp", "ex", "feat"))
    assert n_grp <= 2

    def on_device(train, test, hess):
        docs, feats = train.shape
        queries = test.shape[0]
        half = queries // n_grp
        unit = 8 * LANES
        width = int(feats * SHARE) // LANES * LANES
        grp, feat = lax.axis_index("grp"), lax.axis_index("feat")
        ring = [(i, (i + 1) % n_ex) for i in range(n_ex)]
        hops, swaps, made, first = [], [], [], []

        def after(block, *waits):
            return lax.optimization_barrier((block, waits))[0] if waits else block

        def hop(block, *ahead):
            waits = hops[-2:-1] + swaps[-4:-3] + made[-5:-4] + (first if len(hops) == 3 else [])
            hops.append(lax.ppermute(after(block, *waits, *ahead), "ex", ring))
            return hops[-1]

        def swap(block):
            if n_grp == 1:
                return [block]
            swaps.append(lax.ppermute(after(block, *swaps[-2:-1]), "grp", [(0, 1), (1, 0)]))
            return [block, swaps[-1]]

        def sum_over_feat(sums):
            held = sums.reshape(n_feat, -1, docs)
            bit = 1
            while bit < n_feat:
                pairs = held.reshape((-1, 2) + held.shape[1:])
                mine = (feat // bit) % 2
                keep = lax.dynamic_index_in_dim(pairs, mine, 1, keepdims=False)
                away = lax.dynamic_index_in_dim(pairs, 1 - mine, 1, keepdims=False)
                held = keep + lax.ppermute(away, "feat", [(i, i ^ bit) for i in range(n_feat)])
                bit *= 2
            return held[0]

        def share(rows, columns, other=0):
            if n_grp == 1:
                return rows[:, columns]
            return jnp.where(grp == other, rows[:half, columns], rows[half:, columns])

        scale = (1.0 / (hess + jnp.float32(0.1))).reshape(1, feats)
        starts = [c * width for c in range(CHUNKS)]
        rest = CHUNKS * width
        held = []
        for start in starts:
            held.append(share(after(test, *held[-1:]), slice(start, start + width)))
        late = after(test, *held[-1:])
        sides = [share(late, slice(rest, feats), other) for other in range(n_grp)]
        whole = [jnp.concatenate(sides, axis=0)]
        cuts = [*starts, feats]
        trains = [train[:, a:b] for a, b in zip(cuts[:-1], cuts[1:])]
        own = call(
            functools.partial(own_kernel, starts, unit), queries, docs, feats, [test, scale, *trains]
        )
        first.append(own)
        final = n_ex - 1
        sums = [own] + [None] * final
        def whole_hop(gate):
            whole.append(lax.ppermute(after(whole[-1], hops[gate]), "ex", ring))

        for t in range(1, n_ex):
            for c, start in enumerate(starts):
                held[c] = hop(held[c], *(whole[-1:] if t > 2 and c == 1 else []))
                if 1 < t < final and c == 1:
                    whole_hop(-2)
                parts = swap(held[c])
                operands = [*parts, scale, trains[c]]
                if (t, c) == (final, CHUNKS - 1):
                    continue
                base = [] if sums[t] is None else [sums[t]]
                sums[t] = call(
                    functools.partial(part_kernel, start, unit, len(parts), len(base)),
                    queries, docs, width, operands + base,
                )
                made.append(sums[t])
        while len(whole) < n_ex:
            whole_hop(-2)
        total = call(
            functools.partial(last_kernel, n_grp, n_ex, [starts[-1], rest], unit, len(operands) - 2),
            n_ex * queries, docs, feats - starts[-1], [*operands, *whole[1:], *sums],
            [pltpu.VMEM((n_ex * queries, docs), jnp.float32)],
        )
        return sum_over_feat(total).T

    return jax.shard_map(
        on_device,
        mesh=mesh,
        in_specs=(P(("grp", "ex"), "feat"), P("ex", "feat"), P("feat")),
        out_specs=P(("grp", "ex"), "feat"),
        check_vma=False,
    )
```

```python
import functools

import jax
import jax.numpy as jnp
from jax import lax
from jax.experimental import pallas as pl
from jax.experimental.pallas import tpu as pltpu
from jax.sharding import PartitionSpec as P

CONTRACT = (((1,), (1,)), ((), ()))
LANES = 128
QUARTERS, SHARE = 4, 15 / 16


def product(rows, scale, train, unit, width, skip=0):
    total = None
    for at in range(0, width, unit):
        here = slice(at, min(at + unit, width))
        precond = (rows(here).astype(jnp.float32) * scale(here)).astype(jnp.bfloat16)
        there = train[:, skip + here.start : skip + here.stop]
        part = lax.dot_general(precond, there, CONTRACT, preferred_element_type=jnp.float32)
        total = part if total is None else total + part
    return total


def own_kernel(starts, unit, test, scale, *refs):
    trains, out = refs[:-1], refs[-1]
    total = None
    for start, train in zip(starts, trains):
        column = lambda here: slice(start + here.start, start + here.stop)
        rows, scales = (lambda here, a=a: a[:, column(here)] for a in (test, scale))
        part = product(rows, scales, train, unit, train.shape[1])
        total = part if total is None else total + part
    out[...] = total


def arrived_rows(parts):
    return lambda here: jnp.concatenate([p[:, here] for p in parts], axis=0)


def part_kernel(start, unit, n_parts, has_base, *refs):
    parts, (scale, train) = refs[:n_parts], refs[n_parts : n_parts + 2]
    column = lambda here: scale[:, start + here.start : start + here.stop]
    total = product(arrived_rows(parts), column, train, unit, parts[0].shape[1])
    refs[-1][...] = total + refs[n_parts + 2][...] if has_base else total


def last_kernel(n_grp, n_ex, starts, unit, n_parts, *refs):
    parts, (scale, train, end_train), refs = refs[:n_parts], refs[n_parts : n_parts + 3], refs[n_parts + 3 :]
    wholes, sums, (out, kept) = refs[: n_ex - 1], refs[n_ex - 1 : -2], refs[-2:]
    width = parts[0].shape[1]
    column = lambda here: scale[:, starts[-1] + here.start : starts[-1] + here.stop]
    total = product(arrived_rows(parts), column, train, unit, width)
    queries = total.shape[0]
    half = queries // n_grp
    left = end_train.shape[1] // len(starts)
    block = jnp.concatenate([w[...] for w in wholes], axis=0)
    end_scale = jnp.concatenate([scale[:, s + width : s + width + left] for s in starts], axis=1)
    rest = product(lambda here: block[:, here], lambda here: end_scale[:, here], end_train, unit, len(starts) * left)
    for t, value in enumerate(sums):
        value = value[...]
        if t > 0:
            value += rest[(t - 1) * queries : t * queries]
        if t == n_ex - 1:
            value += total
        kept[t * queries : (t + 1) * queries, :] = value
    ex, grp = lax.axis_index("ex"), lax.axis_index("grp")
    for b in range(n_ex):
        t = lax.rem(ex + (n_ex - b), n_ex)
        for h in range(n_grp):
            place = jnp.where(t == 0, h, lax.rem(h + n_grp - grp, n_grp))
            at = pl.multiple_of(t * queries + place * half, half)
            to = b * queries + h * half
            out[to : to + half, :] = kept[pl.ds(at, half), :]


def call(kernel, rows, docs, width, operands, scratch=()):
    return pl.pallas_call(
        kernel,
        out_shape=jax.ShapeDtypeStruct((rows, docs), jnp.float32),
        in_specs=[pl.BlockSpec(memory_space=pltpu.VMEM)] * len(operands),
        out_specs=pl.BlockSpec(memory_space=pltpu.VMEM),
        scratch_shapes=scratch,
        cost_estimate=pl.CostEstimate(
            flops=2 * rows * docs * width, bytes_accessed=2 * (rows + docs) * width, transcendentals=0
        ),
        compiler_params=pltpu.CompilerParams(vmem_limit_bytes=16 * 1024 * 1024),
    )(*operands)


def solution(mesh):
    n_grp, n_ex, n_feat = (mesh.shape[a] for a in ("grp", "ex", "feat"))
    assert n_grp <= 2

    def on_device(train, test, hess):
        docs, feats = train.shape
        queries = test.shape[0]
        half = queries // n_grp
        unit = 8 * LANES
        quarter = feats // QUARTERS
        width = int(quarter * SHARE) // LANES * LANES
        grp, feat = lax.axis_index("grp"), lax.axis_index("feat")
        ring = [(i, (i + 1) % n_ex) for i in range(n_ex)]
        hops, swaps, made, first = [], [], [], []

        def after(block, *waits):
            return lax.optimization_barrier((block, waits))[0] if waits else block

        def hop(block, *ahead):
            waits = hops[-2:-1] + swaps[-4:-3] + made[-5:-4] + (first if len(hops) == 3 else [])
            hops.append(lax.ppermute(after(block, *waits, *ahead), "ex", ring))
            return hops[-1]

        def swap(block):
            if n_grp == 1:
                return [block]
            swaps.append(lax.ppermute(after(block, *swaps[-2:-1]), "grp", [(0, 1), (1, 0)]))
            return [block, swaps[-1]]

        def sum_over_feat(sums):
            held = sums.reshape(n_feat, -1, docs)
            bit = 1
            while bit < n_feat:
                pairs = held.reshape((-1, 2) + held.shape[1:])
                mine = (feat // bit) % 2
                keep = lax.dynamic_index_in_dim(pairs, mine, 1, keepdims=False)
                away = lax.dynamic_index_in_dim(pairs, 1 - mine, 1, keepdims=False)
                held = keep + lax.ppermute(away, "feat", [(i, i ^ bit) for i in range(n_feat)])
                bit *= 2
            return held[0]

        def share(rows, columns, other=0):
            if n_grp == 1:
                return rows[:, columns]
            return jnp.where(grp == other, rows[:half, columns], rows[half:, columns])

        scale = (1.0 / (hess + jnp.float32(0.1))).reshape(1, feats)
        starts = [c * quarter for c in range(QUARTERS)]
        held = []
        for start in starts:
            held.append(share(after(test, *held[-1:]), slice(start, start + width)))
        late = after(test, *held[-1:])
        ends = [slice(start + width, start + quarter) for start in starts]
        sides = [
            jnp.concatenate([share(late, end, other) for end in ends], axis=1) for other in range(n_grp)
        ]
        whole = [jnp.concatenate(sides, axis=0)]
        trains = [train[:, start : start + quarter] for start in starts]
        end_train = jnp.concatenate([train[:, end] for end in ends], axis=1)
        own = call(
            functools.partial(own_kernel, starts, unit), queries, docs, feats, [test, scale, *trains]
        )
        first.append(own)
        final = n_ex - 1
        sums = [own] + [None] * final
        def whole_hop(gate):
            whole.append(lax.ppermute(after(whole[-1], hops[gate]), "ex", ring))

        for t in range(1, n_ex):
            for c, start in enumerate(starts):
                ahead = whole[-1:] if t > 2 and c == 1 else [end_train] if (t, c) == (2, 2) else []
                held[c] = hop(held[c], *ahead)
                if 1 < t < final and c == 1:
                    whole_hop(-2)
                parts = swap(held[c])
                operands = [*parts, scale, trains[c]]
                if (t, c) == (final, QUARTERS - 1):
                    continue
                base = [] if sums[t] is None else [sums[t]]
                sums[t] = call(
                    functools.partial(part_kernel, start, unit, len(parts), len(base)),
                    queries, docs, width, operands + base,
                )
                made.append(sums[t])
        while len(whole) < n_ex:
            whole_hop(-2)
        total = call(
            functools.partial(last_kernel, n_grp, n_ex, starts, unit, len(operands) - 2),
            n_ex * queries, docs, 2 * width, [*operands, end_train, *whole[1:], *sums],
            [pltpu.VMEM((n_ex * queries, docs), jnp.float32)],
        )
        return sum_over_feat(total).T

    return jax.shard_map(
        on_device,
        mesh=mesh,
        in_specs=(P(("grp", "ex"), "feat"), P("ex", "feat"), P("feat")),
        out_specs=P(("grp", "ex"), "feat"),
        check_vma=False,
    )
```

```python
import functools

import jax
import jax.numpy as jnp
from jax import lax
from jax.experimental import pallas as pl
from jax.experimental.pallas import tpu as pltpu
from jax.sharding import PartitionSpec as P

CONTRACT = (((1,), (1,)), ((), ()))
LANES = 128
QUARTERS, SHARE = 4, 15 / 16


def product(rows, scale, train, unit, width, skip=0):
    total = None
    for at in range(0, width, unit):
        here = slice(at, min(at + unit, width))
        precond = (rows(here).astype(jnp.float32) * scale(here)).astype(jnp.bfloat16)
        there = train[:, skip + here.start : skip + here.stop]
        part = lax.dot_general(precond, there, CONTRACT, preferred_element_type=jnp.float32)
        total = part if total is None else total + part
    return total


def own_kernel(starts, unit, test, scale, *refs):
    trains, out = refs[:-1], refs[-1]
    total = None
    for start, train in zip(starts, trains):
        column = lambda here: slice(start + here.start, start + here.stop)
        rows, scales = (lambda here, a=a: a[:, column(here)] for a in (test, scale))
        part = product(rows, scales, train, unit, train.shape[1])
        total = part if total is None else total + part
    out[...] = total


def arrived_rows(parts):
    return lambda here: jnp.concatenate([p[:, here] for p in parts], axis=0)


def part_kernel(start, unit, n_parts, has_base, *refs):
    parts, (scale, train) = refs[:n_parts], refs[n_parts : n_parts + 2]
    column = lambda here: scale[:, start + here.start : start + here.stop]
    total = product(arrived_rows(parts), column, train, unit, parts[0].shape[1])
    refs[-1][...] = total + refs[n_parts + 2][...] if has_base else total


def last_kernel(n_grp, n_ex, starts, unit, n_parts, *refs):
    parts, (scale, train, end_train), refs = refs[:n_parts], refs[n_parts : n_parts + 3], refs[n_parts + 3 :]
    wholes, sums, (out, kept) = refs[: n_ex - 1], refs[n_ex - 1 : -2], refs[-2:]
    width = parts[0].shape[1]
    column = lambda here: scale[:, starts[-1] + here.start : starts[-1] + here.stop]
    total = product(arrived_rows(parts), column, train, unit, width)
    queries = total.shape[0]
    half = queries // n_grp
    left = end_train.shape[1] // len(starts)
    block = jnp.concatenate([w[...] for w in wholes], axis=0)
    end_scale = jnp.concatenate([scale[:, s + width : s + width + left] for s in starts], axis=1)
    rest = product(lambda here: block[:, here], lambda here: end_scale[:, here], end_train, unit, len(starts) * left)
    for t, value in enumerate(sums):
        value = value[...]
        if t > 0:
            value += rest[(t - 1) * queries : t * queries]
        if t == n_ex - 1:
            value += total
        kept[t * queries : (t + 1) * queries, :] = value
    ex, grp = lax.axis_index("ex"), lax.axis_index("grp")
    for b in range(n_ex):
        t = lax.rem(ex + (n_ex - b), n_ex)
        for h in range(n_grp):
            place = jnp.where(t == 0, h, lax.rem(h + n_grp - grp, n_grp))
            at = pl.multiple_of(t * queries + place * half, half)
            to = b * queries + h * half
            out[to : to + half, :] = kept[pl.ds(at, half), :]


def call(kernel, rows, docs, width, operands, scratch=()):
    return pl.pallas_call(
        kernel,
        out_shape=jax.ShapeDtypeStruct((rows, docs), jnp.float32),
        in_specs=[pl.BlockSpec(memory_space=pltpu.VMEM)] * len(operands),
        out_specs=pl.BlockSpec(memory_space=pltpu.VMEM),
        scratch_shapes=scratch,
        cost_estimate=pl.CostEstimate(
            flops=2 * rows * docs * width, bytes_accessed=2 * (rows + docs) * width, transcendentals=0
        ),
        compiler_params=pltpu.CompilerParams(vmem_limit_bytes=16 * 1024 * 1024),
    )(*operands)


def solution(mesh):
    n_grp, n_ex, n_feat = (mesh.shape[a] for a in ("grp", "ex", "feat"))
    assert n_grp <= 2

    def on_device(train, test, hess):
        docs, feats = train.shape
        queries = test.shape[0]
        half = queries // n_grp
        unit = 8 * LANES
        quarter = feats // QUARTERS
        width = int(quarter * SHARE) // LANES * LANES
        grp, feat = lax.axis_index("grp"), lax.axis_index("feat")
        ring = [(i, (i + 1) % n_ex) for i in range(n_ex)]
        hops, swaps, made, first = [], [], [], []

        def after(block, *waits):
            return lax.optimization_barrier((block, waits))[0] if waits else block

        def hop(block, *ahead):
            waits = hops[-2:-1] + swaps[-4:-3] + made[-4:-3] + (first if len(hops) == 3 else [])
            hops.append(lax.ppermute(after(block, *waits, *ahead), "ex", ring))
            return hops[-1]

        def swap(block):
            if n_grp == 1:
                return [block]
            waits = swaps[-2:-1]
            if len(swaps) > (n_ex - 2) * QUARTERS:
                waits += made[-3:-2]
            swaps.append(lax.ppermute(after(block, *waits), "grp", [(0, 1), (1, 0)]))
            return [block, swaps[-1]]

        def sum_over_feat(sums):
            held = sums.reshape(n_feat, -1, docs)
            bit = 1
            while bit < n_feat:
                pairs = held.reshape((-1, 2) + held.shape[1:])
                mine = (feat // bit) % 2
                keep = lax.dynamic_index_in_dim(pairs, mine, 1, keepdims=False)
                away = lax.dynamic_index_in_dim(pairs, 1 - mine, 1, keepdims=False)
                held = keep + lax.ppermute(away, "feat", [(i, i ^ bit) for i in range(n_feat)])
                bit *= 2
            return held[0]

        def share(rows, columns, other=0):
            if n_grp == 1:
                return rows[:, columns]
            return jnp.where(grp == other, rows[:half, columns], rows[half:, columns])

        scale = (1.0 / (hess + jnp.float32(0.1))).reshape(1, feats)
        starts = [c * quarter for c in range(QUARTERS)]
        held = []
        for start in starts:
            held.append(share(after(test, *held[-1:]), slice(start, start + width)))
        late = after(test, *held[-1:])
        ends = [slice(start + width, start + quarter) for start in starts]
        sides = [
            jnp.concatenate([share(late, end, other) for end in ends], axis=1) for other in range(n_grp)
        ]
        whole = [jnp.concatenate(sides, axis=0)]
        trains = [train[:, start : start + quarter] for start in starts]
        end_train = jnp.concatenate([train[:, end] for end in ends], axis=1)
        own = call(
            functools.partial(own_kernel, starts, unit), queries, docs, feats, [test, scale, *trains]
        )
        first.append(own)
        final = n_ex - 1
        sums = [own] + [None] * final
        def whole_hop(gate):
            whole.append(lax.ppermute(after(whole[-1], hops[gate]), "ex", ring))

        for t in range(1, n_ex):
            for c, start in enumerate(starts):
                ahead = whole[-1:] if t > 2 and c == 1 else [end_train] if (t, c) == (2, 2) else []
                held[c] = hop(held[c], *ahead)
                if 1 < t < final and c == 1:
                    whole_hop(-2)
                parts = swap(held[c])
                operands = [*parts, scale, trains[c]]
                if (t, c) == (final, QUARTERS - 1):
                    continue
                base = [] if sums[t] is None else [sums[t]]
                sums[t] = call(
                    functools.partial(part_kernel, start, unit, len(parts), len(base)),
                    queries, docs, width, operands + base,
                )
                made.append(sums[t])
        while len(whole) < n_ex:
            whole_hop(-2)
        total = call(
            functools.partial(last_kernel, n_grp, n_ex, starts, unit, len(operands) - 2),
            n_ex * queries, docs, 2 * width, [*operands, end_train, *whole[1:], *sums],
            [pltpu.VMEM((n_ex * queries, docs), jnp.float32)],
        )
        return sum_over_feat(total).T

    return jax.shard_map(
        on_device,
        mesh=mesh,
        in_specs=(P(("grp", "ex"), "feat"), P("ex", "feat"), P("feat")),
        out_specs=P(("grp", "ex"), "feat"),
        check_vma=False,
    )
```

```python
import functools

import jax
import jax.numpy as jnp
from jax import lax
from jax.experimental import pallas as pl
from jax.experimental.pallas import tpu as pltpu
from jax.sharding import PartitionSpec as P

CONTRACT = (((1,), (1,)), ((), ()))
LANES = 128
QUARTERS, SHARE = 4, 15 / 16


def product(rows, scale, train, unit, width, skip=0):
    total = None
    for at in range(0, width, unit):
        here = slice(at, min(at + unit, width))
        precond = (rows(here).astype(jnp.float32) * scale(here)).astype(jnp.bfloat16)
        there = train[:, skip + here.start : skip + here.stop]
        part = lax.dot_general(precond, there, CONTRACT, preferred_element_type=jnp.float32)
        total = part if total is None else total + part
    return total


def own_kernel(starts, unit, test, scale, *refs):
    trains, out = refs[:-1], refs[-1]
    total = None
    for start, train in zip(starts, trains):
        column = lambda here: slice(start + here.start, start + here.stop)
        rows, scales = (lambda here, a=a: a[:, column(here)] for a in (test, scale))
        part = product(rows, scales, train, unit, train.shape[1])
        total = part if total is None else total + part
    out[...] = total


def arrived_rows(parts):
    return lambda here: jnp.concatenate([p[:, here] for p in parts], axis=0)


def part_kernel(start, unit, n_parts, has_base, *refs):
    parts, (scale, train) = refs[:n_parts], refs[n_parts : n_parts + 2]
    column = lambda here: scale[:, start + here.start : start + here.stop]
    total = product(arrived_rows(parts), column, train, unit, parts[0].shape[1])
    refs[-1][...] = total + refs[n_parts + 2][...] if has_base else total


def last_kernel(n_grp, n_ex, n_feat, starts, unit, n_parts, *refs):
    parts, (scale, train, end_train), refs = refs[:n_parts], refs[n_parts : n_parts + 3], refs[n_parts + 3 :]
    wholes, sums, (out, kept) = refs[: n_ex - 1], refs[n_ex - 1 : -2], refs[-2:]
    width = parts[0].shape[1]
    column = lambda here: scale[:, starts[-1] + here.start : starts[-1] + here.stop]
    total = product(arrived_rows(parts), column, train, unit, width)
    queries = total.shape[0]
    half = queries // n_grp
    left = end_train.shape[1] // len(starts)
    block = jnp.concatenate([w[...] for w in wholes], axis=0)
    end_scale = jnp.concatenate([scale[:, s + width : s + width + left] for s in starts], axis=1)
    rest = product(lambda here: block[:, here], lambda here: end_scale[:, here], end_train, unit, len(starts) * left)
    for t, value in enumerate(sums):
        value = value[...]
        if t > 0:
            value += rest[(t - 1) * queries : t * queries]
        if t == n_ex - 1:
            value += total
        kept[t * queries : (t + 1) * queries, :] = value
    ex, grp, feat = (lax.axis_index(a) for a in ("ex", "grp", "feat"))
    units = n_ex * n_grp
    each = units // n_feat
    for to in range(units):
        unit_of = (feat ^ (to // each)) * each + to % each
        t = lax.rem(ex + (n_ex - lax.div(unit_of, n_grp)), n_ex)
        h = lax.rem(unit_of, n_grp)
        place = jnp.where(t == 0, h, lax.rem(h + n_grp - grp, n_grp))
        at = pl.multiple_of(t * queries + place * half, half)
        out[to * half : (to + 1) * half, :] = kept[pl.ds(at, half), :]


def call(kernel, rows, docs, width, operands, scratch=()):
    return pl.pallas_call(
        kernel,
        out_shape=jax.ShapeDtypeStruct((rows, docs), jnp.float32),
        in_specs=[pl.BlockSpec(memory_space=pltpu.VMEM)] * len(operands),
        out_specs=pl.BlockSpec(memory_space=pltpu.VMEM),
        scratch_shapes=scratch,
        cost_estimate=pl.CostEstimate(
            flops=2 * rows * docs * width, bytes_accessed=2 * (rows + docs) * width, transcendentals=0
        ),
        compiler_params=pltpu.CompilerParams(vmem_limit_bytes=16 * 1024 * 1024),
    )(*operands)


def solution(mesh):
    n_grp, n_ex, n_feat = (mesh.shape[a] for a in ("grp", "ex", "feat"))
    assert n_grp <= 2

    def on_device(train, test, hess):
        docs, feats = train.shape
        queries = test.shape[0]
        half = queries // n_grp
        unit = 8 * LANES
        quarter = feats // QUARTERS
        width = int(quarter * SHARE) // LANES * LANES
        first_grp = lax.axis_index("grp") == 0
        ring = [(i, (i + 1) % n_ex) for i in range(n_ex)]
        hops, swaps, made, first = [], [], [], []

        def after(block, *waits):
            return lax.optimization_barrier((block, waits))[0] if waits else block

        def hop(block, *ahead):
            waits = hops[-2:-1] + swaps[-4:-3] + made[-4:-3] + (first if len(hops) == 3 else [])
            hops.append(lax.ppermute(after(block, *waits, *ahead), "ex", ring))
            return hops[-1]

        def swap(block):
            if n_grp == 1:
                return [block]
            waits = swaps[-2:-1]
            if len(swaps) > (n_ex - 2) * QUARTERS:
                waits += made[-3:-2]
            swaps.append(lax.ppermute(after(block, *waits), "grp", [(0, 1), (1, 0)]))
            return [block, swaps[-1]]

        def sum_over_feat(sums):
            held = sums.reshape(n_feat, -1, docs)
            bit = 1
            while bit < n_feat:
                pairs = held.reshape((-1, 2) + held.shape[1:])
                partner = [(i, i ^ bit) for i in range(n_feat)]
                held = pairs[:, 0] + lax.ppermute(pairs[:, 1], "feat", partner)
                bit *= 2
            return held[0]

        def share(rows, columns, other=0):
            if n_grp == 1:
                return rows[:, columns]
            low, high = rows[:half, columns], rows[half:, columns]
            return jnp.where(first_grp, high, low) if other else jnp.where(first_grp, low, high)

        scale = (1.0 / (hess + jnp.float32(0.1))).reshape(1, feats)
        starts = [c * quarter for c in range(QUARTERS)]
        held = []
        for start in starts:
            held.append(share(after(test, *held[-1:]), slice(start, start + width)))
        late = after(test, *held[-1:])
        ends = [slice(start + width, start + quarter) for start in starts]
        sides = [
            jnp.concatenate([share(late, end, other) for end in ends], axis=1) for other in range(n_grp)
        ]
        whole = [jnp.concatenate(sides, axis=0)]
        trains = [train[:, start : start + quarter] for start in starts]
        end_train = jnp.concatenate([train[:, end] for end in ends], axis=1)
        own = call(
            functools.partial(own_kernel, starts, unit), queries, docs, feats, [test, scale, *trains]
        )
        first.append(own)
        final = n_ex - 1
        sums = [own] + [None] * final
        def whole_hop(gate):
            whole.append(lax.ppermute(after(whole[-1], hops[gate]), "ex", ring))

        for t in range(1, n_ex):
            for c, start in enumerate(starts):
                ahead = whole[-1:] if t > 2 and c == 1 else [end_train] if (t, c) == (2, 2) else []
                held[c] = hop(held[c], *ahead)
                if 1 < t < final and c == 1:
                    whole_hop(-2)
                parts = swap(held[c])
                operands = [*parts, scale, trains[c]]
                if (t, c) == (final, QUARTERS - 1):
                    continue
                base = [] if sums[t] is None else [sums[t]]
                sums[t] = call(
                    functools.partial(part_kernel, start, unit, len(parts), len(base)),
                    queries, docs, width, operands + base,
                )
                made.append(sums[t])
        while len(whole) < n_ex:
            whole_hop(-2)
        total = call(
            functools.partial(last_kernel, n_grp, n_ex, n_feat, starts, unit, len(operands) - 2),
            n_ex * queries, docs, 2 * width, [*operands, end_train, *whole[1:], *sums],
            [pltpu.VMEM((n_ex * queries, docs), jnp.float32)],
        )
        return sum_over_feat(total).T

    return jax.shard_map(
        on_device,
        mesh=mesh,
        in_specs=(P(("grp", "ex"), "feat"), P("ex", "feat"), P("feat")),
        out_specs=P(("grp", "ex"), "feat"),
        check_vma=False,
    )
```

```python
import functools

import jax
import jax.numpy as jnp
from jax import lax
from jax.experimental import pallas as pl
from jax.experimental.pallas import tpu as pltpu
from jax.sharding import PartitionSpec as P

CONTRACT = (((1,), (1,)), ((), ()))
LANES = 128
QUARTERS, SHARE = 4, 31 / 32


def product(rows, scale, train, unit, width, skip=0):
    total = None
    for at in range(0, width, unit):
        here = slice(at, min(at + unit, width))
        precond = (rows(here).astype(jnp.float32) * scale(here)).astype(jnp.bfloat16)
        there = train[:, skip + here.start : skip + here.stop]
        part = lax.dot_general(precond, there, CONTRACT, preferred_element_type=jnp.float32)
        total = part if total is None else total + part
    return total


def own_kernel(starts, unit, test, scale, *refs):
    trains, out = refs[:-1], refs[-1]
    total = None
    for start, train in zip(starts, trains):
        column = lambda here: slice(start + here.start, start + here.stop)
        rows, scales = (lambda here, a=a: a[:, column(here)] for a in (test, scale))
        part = product(rows, scales, train, unit, train.shape[1])
        total = part if total is None else total + part
    out[...] = total


def arrived_rows(parts):
    return lambda here: jnp.concatenate([p[:, here] for p in parts], axis=0)


def part_kernel(start, unit, n_parts, has_base, *refs):
    parts, (scale, train) = refs[:n_parts], refs[n_parts : n_parts + 2]
    column = lambda here: scale[:, start + here.start : start + here.stop]
    total = product(arrived_rows(parts), column, train, unit, parts[0].shape[1])
    refs[-1][...] = total + refs[n_parts + 2][...] if has_base else total


def last_kernel(n_grp, n_ex, n_feat, starts, unit, n_parts, *refs):
    parts, (scale, train, end_train), refs = refs[:n_parts], refs[n_parts : n_parts + 3], refs[n_parts + 3 :]
    wholes, sums, (out, kept) = refs[: n_ex - 1], refs[n_ex - 1 : -2], refs[-2:]
    width = parts[0].shape[1]
    column = lambda here: scale[:, starts[-1] + here.start : starts[-1] + here.stop]
    total = product(arrived_rows(parts), column, train, unit, width)
    queries = total.shape[0]
    half = queries // n_grp
    left = end_train.shape[1] // len(starts)
    block = jnp.concatenate([w[...] for w in wholes], axis=0)
    end_scale = jnp.concatenate([scale[:, s + width : s + width + left] for s in starts], axis=1)
    rest = product(lambda here: block[:, here], lambda here: end_scale[:, here], end_train, unit, len(starts) * left)
    for t, value in enumerate(sums):
        value = value[...]
        if t > 0:
            value += rest[(t - 1) * queries : t * queries]
        if t == n_ex - 1:
            value += total
        kept[t * queries : (t + 1) * queries, :] = value
    ex, grp, feat = (lax.axis_index(a) for a in ("ex", "grp", "feat"))
    units = n_ex * n_grp
    each = units // n_feat
    for to in range(units):
        unit_of = (feat ^ (to // each)) * each + to % each
        t = lax.rem(ex + (n_ex - lax.div(unit_of, n_grp)), n_ex)
        h = lax.rem(unit_of, n_grp)
        place = jnp.where(t == 0, h, lax.rem(h + n_grp - grp, n_grp))
        at = pl.multiple_of(t * queries + place * half, half)
        out[to * half : (to + 1) * half, :] = kept[pl.ds(at, half), :]


def call(kernel, rows, docs, width, operands, scratch=()):
    return pl.pallas_call(
        kernel,
        out_shape=jax.ShapeDtypeStruct((rows, docs), jnp.float32),
        in_specs=[pl.BlockSpec(memory_space=pltpu.VMEM)] * len(operands),
        out_specs=pl.BlockSpec(memory_space=pltpu.VMEM),
        scratch_shapes=scratch,
        cost_estimate=pl.CostEstimate(
            flops=2 * rows * docs * width, bytes_accessed=2 * (rows + docs) * width, transcendentals=0
        ),
        compiler_params=pltpu.CompilerParams(vmem_limit_bytes=16 * 1024 * 1024),
    )(*operands)


def solution(mesh):
    n_grp, n_ex, n_feat = (mesh.shape[a] for a in ("grp", "ex", "feat"))
    assert n_grp <= 2

    def on_device(train, test, hess):
        docs, feats = train.shape
        queries = test.shape[0]
        half = queries // n_grp
        unit = 8 * LANES
        quarter = feats // QUARTERS
        width = int(quarter * SHARE) // LANES * LANES
        first_grp = lax.axis_index("grp") == 0
        ring = [(i, (i + 1) % n_ex) for i in range(n_ex)]
        back = [(d, s) for s, d in ring]
        hops, swaps, made, first = [], [], [], []

        def after(block, *waits):
            return lax.optimization_barrier((block, waits))[0] if waits else block

        def hop(block, *ahead):
            waits = hops[-2:-1] + swaps[-4:-3] + made[-4:-3] + (first if len(hops) == 3 else [])
            hops.append(lax.ppermute(after(block, *waits, *ahead), "ex", ring))
            return hops[-1]

        def swap(block):
            if n_grp == 1:
                return [block]
            waits = swaps[-2:-1]
            if len(swaps) > (n_ex - 2) * QUARTERS:
                waits += made[-3:-2]
            swaps.append(lax.ppermute(after(block, *waits), "grp", [(0, 1), (1, 0)]))
            return [block, swaps[-1]]

        def sum_over_feat(sums):
            held = sums.reshape(n_feat, -1, docs)
            bit = 1
            while bit < n_feat:
                pairs = held.reshape((-1, 2) + held.shape[1:])
                partner = [(i, i ^ bit) for i in range(n_feat)]
                held = pairs[:, 0] + lax.ppermute(pairs[:, 1], "feat", partner)
                bit *= 2
            return held[0]

        def share(rows, columns, other=0):
            if n_grp == 1:
                return rows[:, columns]
            low, high = rows[:half, columns], rows[half:, columns]
            return jnp.where(first_grp, high, low) if other else jnp.where(first_grp, low, high)

        scale = (1.0 / (hess + jnp.float32(0.1))).reshape(1, feats)
        starts = [c * quarter for c in range(QUARTERS)]
        held = []
        for start in starts:
            held.append(share(after(test, *held[-1:]), slice(start, start + width)))
        late = after(test, *held[-1:])
        ends = [slice(start + width, start + quarter) for start in starts]
        sides = [
            jnp.concatenate([share(late, end, other) for end in ends], axis=1) for other in range(n_grp)
        ]
        whole = jnp.concatenate(sides, axis=0)
        trains = [train[:, start : start + quarter] for start in starts]
        end_train = jnp.concatenate([train[:, end] for end in ends], axis=1)
        own = call(
            functools.partial(own_kernel, starts, unit), queries, docs, feats, [test, scale, *trains]
        )
        first.append(own)
        final = n_ex - 1
        sums = [own] + [None] * final
        turns = []
        for away in range(1, n_ex // 2 + 1):
            turns += [(away, away - 1, ring), (n_ex - away, (n_ex + 1 - away) % n_ex, back)]
        turns = turns[: n_ex - 1]
        rest = {0: whole}
        latest = []

        def whole_hop(gate):
            to, source, pairs = turns.pop(0)
            rest[to] = lax.ppermute(after(rest[source], hops[gate]), "ex", pairs)
            latest[:] = [rest[to]]

        for t in range(1, n_ex):
            for c, start in enumerate(starts):
                ahead = latest if t > 2 and c == 1 else [end_train] if (t, c) == (2, 2) else []
                held[c] = hop(held[c], *ahead)
                if 1 < t < final and c == 1:
                    whole_hop(-2)
                parts = swap(held[c])
                operands = [*parts, scale, trains[c]]
                if (t, c) == (final, QUARTERS - 1):
                    continue
                base = [] if sums[t] is None else [sums[t]]
                sums[t] = call(
                    functools.partial(part_kernel, start, unit, len(parts), len(base)),
                    queries, docs, width, operands + base,
                )
                made.append(sums[t])
        while turns:
            whole_hop(-2)
        total = call(
            functools.partial(last_kernel, n_grp, n_ex, n_feat, starts, unit, len(operands) - 2),
            n_ex * queries, docs, 2 * width, [*operands, end_train, *(rest[t] for t in range(1, n_ex)), *sums],
            [pltpu.VMEM((n_ex * queries, docs), jnp.float32)],
        )
        return sum_over_feat(total).T

    return jax.shard_map(
        on_device,
        mesh=mesh,
        in_specs=(P(("grp", "ex"), "feat"), P("ex", "feat"), P("feat")),
        out_specs=P(("grp", "ex"), "feat"),
        check_vma=False,
    )
```

```python
import functools

import jax
import jax.numpy as jnp
from jax import lax
from jax.experimental import pallas as pl
from jax.experimental.pallas import tpu as pltpu
from jax.sharding import PartitionSpec as P

CONTRACT = (((1,), (1,)), ((), ()))
LANES = 128
CHUNKS = 4


def product(rows, scale, train, unit):
    width, total = train.shape[1], None
    for at in range(0, width, unit):
        here = slice(at, min(at + unit, width))
        precond = (rows(here).astype(jnp.float32) * scale(here)).astype(jnp.bfloat16)
        part = lax.dot_general(
            precond, train[:, here], CONTRACT, preferred_element_type=jnp.float32
        )
        total = part if total is None else total + part
    return total


def own_kernel(starts, unit, test, scale, *refs):
    trains, out = refs[:-1], refs[-1]
    total = None
    for start, train in zip(starts, trains):
        column = lambda here: slice(start + here.start, start + here.stop)
        rows, scales = (lambda here, a=a: a[:, column(here)] for a in (test, scale))
        part = product(rows, scales, train, unit)
        total = part if total is None else total + part
    out[...] = total


def arrived_rows(parts):
    return lambda here: jnp.concatenate([p[:, here] for p in parts], axis=0)


def part_kernel(start, unit, n_parts, has_base, *refs):
    parts, (scale, train) = refs[:n_parts], refs[n_parts : n_parts + 2]
    column = lambda here: scale[:, start + here.start : start + here.stop]
    total = product(arrived_rows(parts), column, train, unit)
    refs[-1][...] = total + refs[n_parts + 2][...] if has_base else total


def last_kernel(n_grp, n_ex, n_feat, start, unit, n_parts, *refs):
    parts, (scale, train) = refs[:n_parts], refs[n_parts : n_parts + 2]
    sums, (out, kept) = refs[n_parts + 2 : -2], refs[-2:]
    column = lambda here: scale[:, start + here.start : start + here.stop]
    total = product(arrived_rows(parts), column, train, unit) + sums[-1][...]
    queries = total.shape[0]
    half = queries // n_grp
    for t, value in enumerate([s[...] for s in sums[:-1]] + [total]):
        kept[t * queries : (t + 1) * queries, :] = value
    ex, grp, feat = (lax.axis_index(a) for a in ("ex", "grp", "feat"))
    units = n_ex * n_grp
    each = units // n_feat
    for to in range(units):
        unit_of = (feat ^ (to // each)) * each + to % each
        t = lax.rem(ex + (n_ex - lax.div(unit_of, n_grp)), n_ex)
        h = lax.rem(unit_of, n_grp)
        place = jnp.where(t == 0, h, lax.rem(h + n_grp - grp, n_grp))
        at = pl.multiple_of(t * queries + place * half, half)
        out[to * half : (to + 1) * half, :] = kept[pl.ds(at, half), :]


def call(kernel, rows, docs, width, operands, scratch=()):
    return pl.pallas_call(
        kernel,
        out_shape=jax.ShapeDtypeStruct((rows, docs), jnp.float32),
        in_specs=[pl.BlockSpec(memory_space=pltpu.VMEM)] * len(operands),
        out_specs=pl.BlockSpec(memory_space=pltpu.VMEM),
        scratch_shapes=scratch,
        cost_estimate=pl.CostEstimate(
            flops=2 * rows * docs * width, bytes_accessed=2 * (rows + docs) * width, transcendentals=0
        ),
        compiler_params=pltpu.CompilerParams(vmem_limit_bytes=16 * 1024 * 1024),
    )(*operands)


def solution(mesh):
    n_grp, n_ex, n_feat = (mesh.shape[a] for a in ("grp", "ex", "feat"))
    assert n_grp <= 2

    def on_device(train, test, hess):
        docs, feats = train.shape
        queries = test.shape[0]
        half = queries // n_grp
        unit = 8 * LANES
        lanes = feats // LANES
        cuts = [c * lanes // CHUNKS * LANES for c in range(CHUNKS + 1)]
        starts, columns = cuts[:-1], [slice(*ends) for ends in zip(cuts[:-1], cuts[1:])]
        first_grp = lax.axis_index("grp") == 0
        ring = [(i, (i + 1) % n_ex) for i in range(n_ex)]
        hops, swaps, made, first = [], [], [], []

        def after(block, *waits):
            return lax.optimization_barrier((block, waits))[0] if waits else block

        def hop(block):
            waits = hops[-2:-1] + swaps[-4:-3] + made[-4:-3] + (first if len(hops) == 3 else [])
            hops.append(lax.ppermute(after(block, *waits), "ex", ring))
            return hops[-1]

        def swap(block):
            if n_grp == 1:
                return [block]
            waits = swaps[-2:-1]
            if len(swaps) > (n_ex - 2) * CHUNKS:
                waits = swaps[-3:-2] + made[-3:-2]
            swaps.append(lax.ppermute(after(block, *waits), "grp", [(0, 1), (1, 0)]))
            return [block, swaps[-1]]

        def sum_over_feat(sums):
            held = sums.reshape(n_feat, -1, docs)
            bit = 1
            while bit < n_feat:
                pairs = held.reshape((-1, 2) + held.shape[1:])
                partner = [(i, i ^ bit) for i in range(n_feat)]
                held = pairs[:, 0] + lax.ppermute(pairs[:, 1], "feat", partner)
                bit *= 2
            return held[0]

        def share(rows, columns):
            if n_grp == 1:
                return rows[:, columns]
            return jnp.where(first_grp, rows[:half, columns], rows[half:, columns])

        scale = (1.0 / (hess + jnp.float32(0.1))).reshape(1, feats)
        held = []
        for here in columns:
            held.append(share(after(test, *held[-1:]), here))
        trains = [train[:, here] for here in columns]
        own = call(
            functools.partial(own_kernel, starts, unit), queries, docs, feats, [test, scale, *trains]
        )
        first.append(own)
        final = n_ex - 1
        sums = [own] + [None] * final
        for t in range(1, n_ex):
            for c, (start, here) in enumerate(zip(starts, columns)):
                held[c] = hop(held[c])
                parts = swap(held[c])
                operands = [*parts, scale, trains[c]]
                if (t, c) == (final, CHUNKS - 1):
                    continue
                base = [] if sums[t] is None else [sums[t]]
                sums[t] = call(
                    functools.partial(part_kernel, start, unit, len(parts), len(base)),
                    queries, docs, here.stop - here.start, operands + base,
                )
                made.append(sums[t])
        total = call(
            functools.partial(last_kernel, n_grp, n_ex, n_feat, start, unit, len(parts)),
            n_ex * queries, docs, here.stop - here.start, [*operands, *sums],
            [pltpu.VMEM((n_ex * queries, docs), jnp.float32)],
        )
        return sum_over_feat(total).T

    return jax.shard_map(
        on_device,
        mesh=mesh,
        in_specs=(P(("grp", "ex"), "feat"), P("ex", "feat"), P("feat")),
        out_specs=P(("grp", "ex"), "feat"),
        check_vma=False,
    )
```

```python
import functools

import jax
import jax.numpy as jnp
from jax import lax
from jax.experimental import pallas as pl
from jax.experimental.pallas import tpu as pltpu
from jax.sharding import PartitionSpec as P

CONTRACT = (((1,), (1,)), ((), ()))
LANES = 128
SHARES = (34, 34, 34, 26)
CHUNKS = len(SHARES)


def product(rows, scale, train, unit):
    width, total = train.shape[1], None
    for at in range(0, width, unit):
        here = slice(at, min(at + unit, width))
        precond = (rows(here).astype(jnp.float32) * scale(here)).astype(jnp.bfloat16)
        part = lax.dot_general(
            precond, train[:, here], CONTRACT, preferred_element_type=jnp.float32
        )
        total = part if total is None else total + part
    return total


def own_kernel(starts, unit, test, scale, *refs):
    trains, out = refs[:-1], refs[-1]
    total = None
    for start, train in zip(starts, trains):
        column = lambda here: slice(start + here.start, start + here.stop)
        rows, scales = (lambda here, a=a: a[:, column(here)] for a in (test, scale))
        part = product(rows, scales, train, unit)
        total = part if total is None else total + part
    out[...] = total


def arrived_rows(parts):
    return lambda here: jnp.concatenate([p[:, here] for p in parts], axis=0)


def part_kernel(start, unit, n_parts, has_base, *refs):
    parts, (scale, train) = refs[:n_parts], refs[n_parts : n_parts + 2]
    column = lambda here: scale[:, start + here.start : start + here.stop]
    total = product(arrived_rows(parts), column, train, unit)
    refs[-1][...] = total + refs[n_parts + 2][...] if has_base else total


def last_kernel(n_grp, n_ex, n_feat, start, unit, n_parts, *refs):
    parts, (scale, train) = refs[:n_parts], refs[n_parts : n_parts + 2]
    sums, (out, kept) = refs[n_parts + 2 : -2], refs[-2:]
    column = lambda here: scale[:, start + here.start : start + here.stop]
    total = product(arrived_rows(parts), column, train, unit) + sums[-1][...]
    queries = total.shape[0]
    half = queries // n_grp
    for t, value in enumerate([s[...] for s in sums[:-1]] + [total]):
        kept[t * queries : (t + 1) * queries, :] = value
    ex, grp, feat = (lax.axis_index(a) for a in ("ex", "grp", "feat"))
    units = n_ex * n_grp
    each = units // n_feat
    for to in range(units):
        unit_of = (feat ^ (to // each)) * each + to % each
        t = lax.rem(ex + (n_ex - lax.div(unit_of, n_grp)), n_ex)
        h = lax.rem(unit_of, n_grp)
        place = jnp.where(t == 0, h, lax.rem(h + n_grp - grp, n_grp))
        at = pl.multiple_of(t * queries + place * half, half)
        out[to * half : (to + 1) * half, :] = kept[pl.ds(at, half), :]


def call(kernel, rows, docs, width, operands, scratch=()):
    return pl.pallas_call(
        kernel,
        out_shape=jax.ShapeDtypeStruct((rows, docs), jnp.float32),
        in_specs=[pl.BlockSpec(memory_space=pltpu.VMEM)] * len(operands),
        out_specs=pl.BlockSpec(memory_space=pltpu.VMEM),
        scratch_shapes=scratch,
        cost_estimate=pl.CostEstimate(
            flops=2 * rows * docs * width, bytes_accessed=2 * (rows + docs) * width, transcendentals=0
        ),
        compiler_params=pltpu.CompilerParams(vmem_limit_bytes=16 * 1024 * 1024),
    )(*operands)


def solution(mesh):
    n_grp, n_ex, n_feat = (mesh.shape[a] for a in ("grp", "ex", "feat"))
    assert n_grp <= 2

    def on_device(train, test, hess):
        docs, feats = train.shape
        queries = test.shape[0]
        half = queries // n_grp
        unit = 8 * LANES
        lanes = feats // LANES
        cuts = [sum(SHARES[:c]) * lanes // sum(SHARES) * LANES for c in range(CHUNKS + 1)]
        starts, columns = cuts[:-1], [slice(*ends) for ends in zip(cuts[:-1], cuts[1:])]
        first_grp = lax.axis_index("grp") == 0
        ring = [(i, (i + 1) % n_ex) for i in range(n_ex)]
        hops, swaps, made, first = [], [], [], []

        def after(block, *waits):
            return lax.optimization_barrier((block, waits))[0] if waits else block

        def hop(block):
            waits = hops[-2:-1] + swaps[-4:-3] + made[-4:-3] + (first if len(hops) == 3 else [])
            hops.append(lax.ppermute(after(block, *waits), "ex", ring))
            return hops[-1]

        def swap(block):
            if n_grp == 1:
                return [block]
            waits = swaps[-2:-1]
            if len(swaps) > (n_ex - 2) * CHUNKS:
                waits = swaps[-3:-2] + made[-3:-2]
            swaps.append(lax.ppermute(after(block, *waits), "grp", [(0, 1), (1, 0)]))
            return [block, swaps[-1]]

        def sum_over_feat(sums):
            held = sums.reshape(n_feat, -1, docs)
            bit = 1
            while bit < n_feat:
                pairs = held.reshape((-1, 2) + held.shape[1:])
                partner = [(i, i ^ bit) for i in range(n_feat)]
                held = pairs[:, 0] + lax.ppermute(pairs[:, 1], "feat", partner)
                bit *= 2
            return held[0]

        def share(rows, columns):
            if n_grp == 1:
                return rows[:, columns]
            return jnp.where(first_grp, rows[:half, columns], rows[half:, columns])

        scale = (1.0 / (hess + jnp.float32(0.1))).reshape(1, feats)
        held = []
        for here in columns:
            held.append(share(after(test, *held[-1:]), here))
        trains = [train[:, here] for here in columns]
        own = call(
            functools.partial(own_kernel, starts, unit), queries, docs, feats, [test, scale, *trains]
        )
        first.append(own)
        final = n_ex - 1
        sums = [own] + [None] * final
        for t in range(1, n_ex):
            for c, (start, here) in enumerate(zip(starts, columns)):
                held[c] = hop(held[c])
                parts = swap(held[c])
                operands = [*parts, scale, trains[c]]
                if (t, c) == (final, CHUNKS - 1):
                    continue
                base = [] if sums[t] is None else [sums[t]]
                sums[t] = call(
                    functools.partial(part_kernel, start, unit, len(parts), len(base)),
                    queries, docs, here.stop - here.start, operands + base,
                )
                made.append(sums[t])
        total = call(
            functools.partial(last_kernel, n_grp, n_ex, n_feat, start, unit, len(parts)),
            n_ex * queries, docs, here.stop - here.start, [*operands, *sums],
            [pltpu.VMEM((n_ex * queries, docs), jnp.float32)],
        )
        return sum_over_feat(total).T

    return jax.shard_map(
        on_device,
        mesh=mesh,
        in_specs=(P(("grp", "ex"), "feat"), P("ex", "feat"), P("feat")),
        out_specs=P(("grp", "ex"), "feat"),
        check_vma=False,
    )
```

```python
import functools

import jax
import jax.numpy as jnp
from jax import lax
from jax.experimental import pallas as pl
from jax.experimental.pallas import tpu as pltpu
from jax.sharding import PartitionSpec as P

CONTRACT = (((1,), (1,)), ((), ()))
LANES = 128
CHUNKS = 4


def product(rows, scale, train, unit):
    width, total = train.shape[1], None
    for at in range(0, width, unit):
        here = slice(at, min(at + unit, width))
        precond = (rows(here).astype(jnp.float32) * scale(here)).astype(jnp.bfloat16)
        part = lax.dot_general(
            precond, train[:, here], CONTRACT, preferred_element_type=jnp.float32
        )
        total = part if total is None else total + part
    return total


def own_kernel(starts, unit, test, scale, *refs):
    trains, out = refs[:-1], refs[-1]
    total = None
    for start, train in zip(starts, trains):
        column = lambda here: slice(start + here.start, start + here.stop)
        rows, scales = (lambda here, a=a: a[:, column(here)] for a in (test, scale))
        part = product(rows, scales, train, unit)
        total = part if total is None else total + part
    out[...] = total


def arrived_rows(parts):
    return lambda here: jnp.concatenate([p[:, here] for p in parts], axis=0)


def part_kernel(start, unit, n_parts, has_base, *refs):
    parts, (scale, train) = refs[:n_parts], refs[n_parts : n_parts + 2]
    column = lambda here: scale[:, start + here.start : start + here.stop]
    total = product(arrived_rows(parts), column, train, unit)
    refs[-1][...] = total + refs[n_parts + 2][...] if has_base else total


def last_kernel(n_grp, n_ex, n_feat, start, unit, n_parts, *refs):
    parts, (scale, train) = refs[:n_parts], refs[n_parts : n_parts + 2]
    sums, (out, kept) = refs[n_parts + 2 : -2], refs[-2:]
    column = lambda here: scale[:, start + here.start : start + here.stop]
    total = product(arrived_rows(parts), column, train, unit) + sums[-1][...]
    queries = total.shape[0]
    half = queries // n_grp
    for t, value in enumerate([s[...] for s in sums[:-1]] + [total]):
        kept[t * queries : (t + 1) * queries, :] = value
    ex, grp, feat = (lax.axis_index(a) for a in ("ex", "grp", "feat"))
    units = n_ex * n_grp
    each = units // n_feat
    for to in range(units):
        unit_of = (feat ^ (to // each)) * each + to % each
        t = lax.rem(ex + (n_ex - lax.div(unit_of, n_grp)), n_ex)
        h = lax.rem(unit_of, n_grp)
        place = jnp.where(t == 0, h, lax.rem(h + n_grp - grp, n_grp))
        at = pl.multiple_of(t * queries + place * half, half)
        out[to * half : (to + 1) * half, :] = kept[pl.ds(at, half), :]


LINE, SHIP = (5, 5, 4), 2
KEPT = ((0, 1, 2, 3), (1, 0, 2, 3), (2, 3, 1, 0), (3, 2, 1, 0))


def line_rows(n_grp, n_feat, halved):
    ex, grp, feat = (lax.axis_index(a) for a in ("ex", "grp", "feat"))
    units = len(KEPT) * n_grp
    each = units // n_feat
    found = []
    for to in range(units):
        unit_of = (feat ^ (to // each)) * each + to % each
        block, h = lax.div(unit_of, n_grp), lax.rem(unit_of, n_grp)
        t = jnp.int32(0)
        for i, kept in enumerate(KEPT):
            for b in kept[1:]:
                t = jnp.where((ex == i) & (block == b), kept.index(b), t)
        place = jnp.where(t == 0, h, lax.rem(h + n_grp - grp, n_grp)) if halved else h
        found.append(t * n_grp + place)
    return found


def units_product(rows, scale, trains, unit, first, count):
    total = None
    for k in range(count):
        j = first + k
        column = scale[:, j * unit : (j + 1) * unit]
        precond = (rows(k).astype(jnp.float32) * column).astype(jnp.bfloat16)
        here = trains[j // 4][:, (j % 4) * unit : (j % 4 + 1) * unit]
        part = lax.dot_general(precond, here, CONTRACT, preferred_element_type=jnp.float32)
        total = part if total is None else total + part
    return total


def line_own_kernel(unit, test, scale, *refs):
    rows = lambda k: test[:, k * unit : (k + 1) * unit]
    refs[-1][...] = units_product(rows, scale, refs[:-1], unit, 0, sum(LINE))


def line_part_kernel(unit, first, count, quarters, n_parts, *refs):
    parts, scale = refs[:n_parts], refs[n_parts]
    trains = dict(zip(quarters, refs[n_parts + 1 :]))
    base = refs[n_parts + 1 + len(quarters) : -1]
    rows = lambda k: jnp.concatenate([p[:, k * unit : (k + 1) * unit] for p in parts], axis=0)
    total = units_product(rows, scale, trains, unit, first, count)
    refs[-1][...] = total + base[0][...] if base else total


def line_last_kernel(n_grp, n_feat, unit, first, count, quarters, n_parts, *refs):
    parts, scale = refs[:n_parts], refs[n_parts]
    trains = dict(zip(quarters, refs[n_parts + 1 :]))
    near, *sums = refs[n_parts + 1 + len(quarters) : -2]
    out, kept = refs[-2:]
    rows = lambda k: jnp.concatenate([p[:, k * unit : (k + 1) * unit] for p in parts], axis=0)
    total = units_product(rows, scale, trains, unit, first, count) + sums[-1][...]
    queries = total.shape[0]
    half = queries // n_grp
    for t, value in enumerate([s[...] for s in sums[:-1]] + [total]):
        kept[t * queries : (t + 1) * queries, :] = value
    for to, place in enumerate(line_rows(n_grp, n_feat, True)):
        at = pl.multiple_of(place * half, half)
        here = slice(to * half, (to + 1) * half)
        out[here, :] = kept[pl.ds(at, half), :] + near[here, :]


def crate_kernel(unit, n_grp, test, train, *outs):
    half = test.shape[0] // n_grp
    base = sum(LINE)
    blocks = []
    for h in range(n_grp):
        for x in range(SHIP):
            cols = slice((base + x) * unit, (base + x + 1) * unit)
            blocks.append(test[h * half : (h + 1) * half, cols])
    n_tests = len(blocks)
    for x in range(SHIP):
        at = ((base + x) % 4) * unit
        for g in range(train.shape[0] // half):
            blocks.append(train[g * half : (g + 1) * half, at : at + unit])
    for i, block in enumerate(blocks[:n_tests]):
        outs[-1][:, i * unit : (i + 1) * unit] = block
    for out in outs[:-1]:
        for i in range(out.shape[1] // unit):
            out[:, i * unit : (i + 1) * unit] = blocks.pop(0) if len(blocks) > 1 else blocks[0]


def shipped_kernel(n_grp, n_feat, unit, n_cargo, test, scale, train, other, *refs):
    cargo, (near, far, kept) = refs[:n_cargo], refs[n_cargo:]
    base = sum(LINE)
    half = test.shape[0] // n_grp
    blocks = [(c, i * unit) for c in cargo for i in range(c.shape[1] // unit)]
    tests, rows_of = blocks[: n_grp * SHIP], blocks[n_grp * SHIP :]
    groups = train.shape[0] // half
    sums = [None, None]
    for x in range(SHIP):
        parts = [test[:, (base + x) * unit : (base + x + 1) * unit]]
        for h in range(n_grp):
            ref, at = tests[h * SHIP + x]
            parts.append(ref[:, at : at + unit])
        for k in range(2):
            for h in range(n_grp):
                at = (h * SHIP + x) * unit
                parts.append(other[k * half : (k + 1) * half, at : at + unit])
        rows = jnp.concatenate(parts, axis=0)
        column = scale[:, (base + x) * unit : (base + x + 1) * unit]
        precond = (rows.astype(jnp.float32) * column).astype(jnp.bfloat16)
        at = ((base + x) % 4) * unit
        away = [ref[:, c : c + unit] for ref, c in rows_of[x * groups : (x + 1) * groups]]
        for i, docs in enumerate((train[:, at : at + unit], jnp.concatenate(away, axis=0))):
            part = lax.dot_general(precond, docs, CONTRACT, preferred_element_type=jnp.float32)
            sums[i] = part if sums[i] is None else sums[i] + part
    ex = lax.axis_index("ex")
    inner = (ex > 0) & (ex < len(KEPT) - 1)
    places = line_rows(n_grp, n_feat, False)
    for value, out in zip((jnp.where(inner, sums[0], 0.0), sums[1]), (near, far)):
        kept[...] = value
        for to, place in enumerate(places):
            at = pl.multiple_of(place * half, half)
            out[to * half : (to + 1) * half, :] = kept[pl.ds(at, half), :]


def call(kernel, rows, docs, width, operands, scratch=(), shapes=None):
    vmem = pl.BlockSpec(memory_space=pltpu.VMEM)
    return pl.pallas_call(
        kernel,
        out_shape=shapes or jax.ShapeDtypeStruct((rows, docs), jnp.float32),
        in_specs=[vmem] * len(operands),
        out_specs=[vmem] * len(shapes) if shapes else vmem,
        scratch_shapes=scratch,
        cost_estimate=pl.CostEstimate(
            flops=2 * rows * docs * width, bytes_accessed=2 * (rows + docs) * width, transcendentals=0
        ),
        compiler_params=pltpu.CompilerParams(vmem_limit_bytes=16 * 1024 * 1024),
    )(*operands)


def solution(mesh):
    n_grp, n_ex, n_feat = (mesh.shape[a] for a in ("grp", "ex", "feat"))
    assert n_grp <= 2

    def after(block, *waits):
        return lax.optimization_barrier((block, waits))[0] if waits else block

    def line(train, test, scale):
        docs, feats = train.shape
        queries = test.shape[0]
        half = queries // n_grp
        unit = feats // (sum(LINE) + SHIP)
        ex = lax.axis_index("ex")
        is_end, first_grp = (ex == 0) | (ex == n_ex - 1), lax.axis_index("grp") == 0
        test, is_end, first_grp = lax.optimization_barrier((test, is_end, first_grp))
        done, outs, swaps, middles, made = {}, [], [], [], []

        outer_pairs = [(i, i ^ 1) for i in range(n_ex)]
        middle_pairs = []
        for i in range(n_ex):
            for f in range(n_feat):
                to = (i, f ^ 1) if i in (0, n_ex - 1) else (n_ex - 1 - i, f)
                middle_pairs.append((i * n_feat + f, to[0] * n_feat + to[1]))

        def outer(name, block):
            waits = outs[-2:-1] + swaps[-4:-3] + made[-4:-3] + (first if len(outs) == 3 else [])
            outs.append(lax.ppermute(after(block, *waits), "ex", outer_pairs))
            done[name] = outs[-1]

        def middle(name, block):
            middles.append(lax.ppermute(after(block, *middles[-1:]), ("ex", "feat"), middle_pairs))
            done[name] = middles[-1]

        def swap(block):
            if n_grp == 1:
                return [block]
            waits = swaps[-2:-1]
            if len(swaps) > 2 * len(LINE):
                waits = swaps[-3:-2] + made[-3:-2]
            swaps.append(lax.ppermute(after(block, *waits), "grp", [(0, 1), (1, 0)]))
            return [block, swaps[-1]]

        def sum_over_feat(sums, *waits):
            held = sums.reshape(n_feat, -1, docs)
            bit = 1
            while bit < n_feat:
                pairs = held.reshape((-1, 2) + held.shape[1:])
                partner = [(i, i ^ bit) for i in range(n_feat)]
                send = after(pairs[:, 1], *waits)
                held, waits = pairs[:, 0] + lax.ppermute(send, "feat", partner), ()
                bit *= 2
            return held[0]

        def share(rows, start, count):
            here = slice(start * unit, (start + count) * unit)
            if n_grp == 1:
                return rows[:, here]
            return jnp.where(first_grp, rows[:half, here], rows[half:, here])

        firsts = [sum(LINE[:c]) for c in range(len(LINE))]
        columns = [slice(f * unit, (f + n) * unit) for f, n in zip(firsts, LINE)]
        mine = []
        for start, count in zip(firsts, LINE):
            mine.append(share(after(test, *mine[-1:]), start, count))
        every = share(after(test, mine[0]), 0, sum(LINE))
        trains = [train[:, q * 4 * unit : (q + 1) * 4 * unit] for q in range(4)]
        own = call(
            functools.partial(line_own_kernel, unit), queries, docs, feats, [test, scale, *trains]
        )
        first = [own]
        widths = [*LINE, *LINE[:2]]
        shapes = [jax.ShapeDtypeStruct((half, w * unit), test.dtype) for w in widths]
        shapes.append(jax.ShapeDtypeStruct((half, n_grp * SHIP * unit), test.dtype))
        *cargo, own_tests = call(
            functools.partial(crate_kernel, unit, n_grp), docs, SHIP * unit, 1,
            [test, trains[3]], shapes=shapes,
        )

        sums = [own, None, None, None]
        n = len(LINE)

        def finish(t, c, block):
            parts = swap(block)
            quarters = sorted({j // 4 for j in range(firsts[c], firsts[c] + LINE[c])})
            operands = [*parts, scale, *(trains[q] for q in quarters)]
            sizes = (unit, firsts[c], LINE[c], quarters, len(parts))
            if (t, c) == (3, n - 1):
                return sizes, operands
            base = [] if sums[t] is None else [sums[t]]
            kernel = functools.partial(line_part_kernel, *sizes)
            sums[t] = call(kernel, queries, docs, LINE[c] * unit, operands + base)
            made.append(sums[t])

        for c in range(n):
            outer(f"E1{c}", mine[c])
            if c == 0:
                middle("O1", every)
            finish(1, c, done[f"E1{c}"])
        middle("O20", done["E10"])
        for c in range(n):
            inner = done["O1"][:, columns[c]]
            outer(f"E2{c}", jnp.where(is_end, cargo[c], inner))
            if c == 0:
                middle("O21", jnp.concatenate([done["E11"], done["E12"]], axis=1))
            finish(2, c, jnp.where(is_end, done[f"E2{c}"], inner))
        end_tests = done["E20"][:, : own_tests.shape[1]]
        middle("OS", jnp.concatenate([own_tests, end_tests], axis=0))
        for c in range(n):
            inner = done["O20"] if c == 0 else done["O21"]
            if c > 0:
                inner = inner[:, columns[c].start - columns[1].start : columns[c].stop - columns[1].start]
            outer(f"E3{c}", jnp.where(is_end, cargo[3 + c], inner) if c < 2 else inner)
            last = finish(3, c, jnp.where(is_end, done[f"E3{c}"], inner))
        shape = jax.ShapeDtypeStruct((n_ex * queries, docs), jnp.float32)
        landed = [done[name] for name in ("E20", "E21", "E22", "E30", "E31")]
        near, far = call(
            functools.partial(shipped_kernel, n_grp, n_feat, unit, len(landed)),
            n_ex * queries, docs, 2 * SHIP * unit,
            [test, scale, trains[3], done["OS"], *landed],
            [pltpu.VMEM(shape.shape, jnp.float32)], shapes=[shape, shape],
        )
        back = lax.ppermute(sum_over_feat(far), "ex", outer_pairs)
        sizes, operands = last
        total = call(
            functools.partial(line_last_kernel, n_grp, n_feat, *sizes),
            n_ex * queries, docs, LINE[-1] * unit, [*operands, near, *sums],
            [pltpu.VMEM(shape.shape, jnp.float32)],
        )
        out = sum_over_feat(total, back) + jnp.where(is_end, back, 0.0)
        return out.T

    def on_device(train, test, hess):
        docs, feats = train.shape
        queries = test.shape[0]
        half = queries // n_grp
        unit = 8 * LANES
        lanes = feats // LANES
        cuts = [c * lanes // CHUNKS * LANES for c in range(CHUNKS + 1)]
        starts, columns = cuts[:-1], [slice(*ends) for ends in zip(cuts[:-1], cuts[1:])]
        first_grp = lax.axis_index("grp") == 0
        ring = [(i, (i + 1) % n_ex) for i in range(n_ex)]
        hops, swaps, made, first = [], [], [], []

        def after(block, *waits):
            return lax.optimization_barrier((block, waits))[0] if waits else block

        def hop(block):
            waits = hops[-2:-1] + swaps[-4:-3] + made[-4:-3] + (first if len(hops) == 3 else [])
            hops.append(lax.ppermute(after(block, *waits), "ex", ring))
            return hops[-1]

        def swap(block):
            if n_grp == 1:
                return [block]
            waits = swaps[-2:-1]
            if len(swaps) > (n_ex - 2) * CHUNKS:
                waits = swaps[-3:-2] + made[-3:-2]
            swaps.append(lax.ppermute(after(block, *waits), "grp", [(0, 1), (1, 0)]))
            return [block, swaps[-1]]

        def sum_over_feat(sums):
            held = sums.reshape(n_feat, -1, docs)
            bit = 1
            while bit < n_feat:
                pairs = held.reshape((-1, 2) + held.shape[1:])
                partner = [(i, i ^ bit) for i in range(n_feat)]
                held = pairs[:, 0] + lax.ppermute(pairs[:, 1], "feat", partner)
                bit *= 2
            return held[0]

        def share(rows, columns):
            if n_grp == 1:
                return rows[:, columns]
            return jnp.where(first_grp, rows[:half, columns], rows[half:, columns])

        scale = (1.0 / (hess + jnp.float32(0.1))).reshape(1, feats)
        if n_ex == len(KEPT):
            return line(train, test, scale)
        held = []
        for here in columns:
            held.append(share(after(test, *held[-1:]), here))
        trains = [train[:, here] for here in columns]
        own = call(
            functools.partial(own_kernel, starts, unit), queries, docs, feats, [test, scale, *trains]
        )
        first.append(own)
        final = n_ex - 1
        sums = [own] + [None] * final
        for t in range(1, n_ex):
            for c, (start, here) in enumerate(zip(starts, columns)):
                held[c] = hop(held[c])
                parts = swap(held[c])
                operands = [*parts, scale, trains[c]]
                if (t, c) == (final, CHUNKS - 1):
                    continue
                base = [] if sums[t] is None else [sums[t]]
                sums[t] = call(
                    functools.partial(part_kernel, start, unit, len(parts), len(base)),
                    queries, docs, here.stop - here.start, operands + base,
                )
                made.append(sums[t])
        total = call(
            functools.partial(last_kernel, n_grp, n_ex, n_feat, start, unit, len(parts)),
            n_ex * queries, docs, here.stop - here.start, [*operands, *sums],
            [pltpu.VMEM((n_ex * queries, docs), jnp.float32)],
        )
        return sum_over_feat(total).T

    return jax.shard_map(
        on_device,
        mesh=mesh,
        in_specs=(P(("grp", "ex"), "feat"), P("ex", "feat"), P("feat")),
        out_specs=P(("grp", "ex"), "feat"),
        check_vma=False,
    )
```

```python
import functools

import jax
import jax.numpy as jnp
from jax import lax
from jax.experimental import pallas as pl
from jax.experimental.pallas import tpu as pltpu
from jax.sharding import PartitionSpec as P

CONTRACT = (((1,), (1,)), ((), ()))
LANES = 128
CHUNKS = 4


def product(rows, scale, train, unit):
    width, total = train.shape[1], None
    for at in range(0, width, unit):
        here = slice(at, min(at + unit, width))
        precond = (rows(here).astype(jnp.float32) * scale(here)).astype(jnp.bfloat16)
        part = lax.dot_general(
            precond, train[:, here], CONTRACT, preferred_element_type=jnp.float32
        )
        total = part if total is None else total + part
    return total


def own_kernel(starts, unit, test, scale, *refs):
    trains, out = refs[:-1], refs[-1]
    total = None
    for start, train in zip(starts, trains):
        column = lambda here: slice(start + here.start, start + here.stop)
        rows, scales = (lambda here, a=a: a[:, column(here)] for a in (test, scale))
        part = product(rows, scales, train, unit)
        total = part if total is None else total + part
    out[...] = total


def arrived_rows(parts):
    return lambda here: jnp.concatenate([p[:, here] for p in parts], axis=0)


def part_kernel(start, unit, n_parts, has_base, *refs):
    parts, (scale, train) = refs[:n_parts], refs[n_parts : n_parts + 2]
    column = lambda here: scale[:, start + here.start : start + here.stop]
    total = product(arrived_rows(parts), column, train, unit)
    refs[-1][...] = total + refs[n_parts + 2][...] if has_base else total


def last_kernel(n_grp, n_ex, n_feat, start, unit, n_parts, *refs):
    parts, (scale, train) = refs[:n_parts], refs[n_parts : n_parts + 2]
    sums, (out, kept) = refs[n_parts + 2 : -2], refs[-2:]
    column = lambda here: scale[:, start + here.start : start + here.stop]
    total = product(arrived_rows(parts), column, train, unit) + sums[-1][...]
    queries = total.shape[0]
    half = queries // n_grp
    for t, value in enumerate([s[...] for s in sums[:-1]] + [total]):
        kept[t * queries : (t + 1) * queries, :] = value
    ex, grp, feat = (lax.axis_index(a) for a in ("ex", "grp", "feat"))
    units = n_ex * n_grp
    each = units // n_feat
    for to in range(units):
        unit_of = (feat ^ (to // each)) * each + to % each
        t = lax.rem(ex + (n_ex - lax.div(unit_of, n_grp)), n_ex)
        h = lax.rem(unit_of, n_grp)
        place = jnp.where(t == 0, h, lax.rem(h + n_grp - grp, n_grp))
        at = pl.multiple_of(t * queries + place * half, half)
        out[to * half : (to + 1) * half, :] = kept[pl.ds(at, half), :]


LINE, SHIP = (5, 5, 5), 1
KEPT = ((0, 1, 2, 3), (1, 0, 2, 3), (2, 3, 1, 0), (3, 2, 1, 0))


def line_rows(n_grp, n_feat, halved):
    ex, grp, feat = (lax.axis_index(a) for a in ("ex", "grp", "feat"))
    units = len(KEPT) * n_grp
    each = units // n_feat
    found = []
    for to in range(units):
        unit_of = (feat ^ (to // each)) * each + to % each
        block, h = lax.div(unit_of, n_grp), lax.rem(unit_of, n_grp)
        t = jnp.int32(0)
        for i, kept in enumerate(KEPT):
            for b in kept[1:]:
                t = jnp.where((ex == i) & (block == b), kept.index(b), t)
        place = jnp.where(t == 0, h, lax.rem(h + n_grp - grp, n_grp)) if halved else h
        found.append(t * n_grp + place)
    return found


def units_product(rows, scale, trains, unit, first, count):
    total = None
    for k in range(count):
        j = first + k
        column = scale[:, j * unit : (j + 1) * unit]
        precond = (rows(k).astype(jnp.float32) * column).astype(jnp.bfloat16)
        here = trains[j // 4][:, (j % 4) * unit : (j % 4 + 1) * unit]
        part = lax.dot_general(precond, here, CONTRACT, preferred_element_type=jnp.float32)
        total = part if total is None else total + part
    return total


def line_own_kernel(unit, test, scale, *refs):
    rows = lambda k: test[:, k * unit : (k + 1) * unit]
    refs[-1][...] = units_product(rows, scale, refs[:-1], unit, 0, sum(LINE))


def line_part_kernel(unit, first, count, quarters, n_parts, *refs):
    parts, scale = refs[:n_parts], refs[n_parts]
    trains = dict(zip(quarters, refs[n_parts + 1 :]))
    base = refs[n_parts + 1 + len(quarters) : -1]
    rows = lambda k: jnp.concatenate([p[:, k * unit : (k + 1) * unit] for p in parts], axis=0)
    total = units_product(rows, scale, trains, unit, first, count)
    refs[-1][...] = total + base[0][...] if base else total


def line_last_kernel(n_grp, n_feat, unit, first, count, quarters, n_parts, *refs):
    parts, scale = refs[:n_parts], refs[n_parts]
    trains = dict(zip(quarters, refs[n_parts + 1 :]))
    near, *sums = refs[n_parts + 1 + len(quarters) : -2]
    out, kept = refs[-2:]
    rows = lambda k: jnp.concatenate([p[:, k * unit : (k + 1) * unit] for p in parts], axis=0)
    total = units_product(rows, scale, trains, unit, first, count) + sums[-1][...]
    queries = total.shape[0]
    half = queries // n_grp
    for t, value in enumerate([s[...] for s in sums[:-1]] + [total]):
        kept[t * queries : (t + 1) * queries, :] = value
    for to, place in enumerate(line_rows(n_grp, n_feat, True)):
        at = pl.multiple_of(place * half, half)
        here = slice(to * half, (to + 1) * half)
        out[here, :] = kept[pl.ds(at, half), :] + near[here, :]


def crate_kernel(unit, n_grp, test, train, *outs):
    half = test.shape[0] // n_grp
    base = sum(LINE)
    blocks = []
    for h in range(n_grp):
        for x in range(SHIP):
            cols = slice((base + x) * unit, (base + x + 1) * unit)
            blocks.append(test[h * half : (h + 1) * half, cols])
    n_tests = len(blocks)
    for x in range(SHIP):
        at = ((base + x) % 4) * unit
        for g in range(train.shape[0] // half):
            blocks.append(train[g * half : (g + 1) * half, at : at + unit])
    for i, block in enumerate(blocks[:n_tests]):
        outs[-1][:, i * unit : (i + 1) * unit] = block
    for out in outs[:-1]:
        for i in range(out.shape[1] // unit):
            out[:, i * unit : (i + 1) * unit] = blocks.pop(0) if len(blocks) > 1 else blocks[0]


def shipped_kernel(n_grp, n_feat, unit, n_cargo, test, scale, train, other, *refs):
    cargo, (near, far, kept) = refs[:n_cargo], refs[n_cargo:]
    base = sum(LINE)
    half = test.shape[0] // n_grp
    blocks = [(c, i * unit) for c in cargo for i in range(c.shape[1] // unit)]
    tests, rows_of = blocks[: n_grp * SHIP], blocks[n_grp * SHIP :]
    groups = train.shape[0] // half
    sums = [None, None]
    for x in range(SHIP):
        parts = [test[:, (base + x) * unit : (base + x + 1) * unit]]
        for h in range(n_grp):
            ref, at = tests[h * SHIP + x]
            parts.append(ref[:, at : at + unit])
        for k in range(2):
            for h in range(n_grp):
                at = (h * SHIP + x) * unit
                parts.append(other[k * half : (k + 1) * half, at : at + unit])
        rows = jnp.concatenate(parts, axis=0)
        column = scale[:, (base + x) * unit : (base + x + 1) * unit]
        precond = (rows.astype(jnp.float32) * column).astype(jnp.bfloat16)
        at = ((base + x) % 4) * unit
        away = [ref[:, c : c + unit] for ref, c in rows_of[x * groups : (x + 1) * groups]]
        for i, docs in enumerate((train[:, at : at + unit], jnp.concatenate(away, axis=0))):
            part = lax.dot_general(precond, docs, CONTRACT, preferred_element_type=jnp.float32)
            sums[i] = part if sums[i] is None else sums[i] + part
    ex = lax.axis_index("ex")
    inner = (ex > 0) & (ex < len(KEPT) - 1)
    places = line_rows(n_grp, n_feat, False)
    for value, out in zip((jnp.where(inner, sums[0], 0.0), sums[1]), (near, far)):
        kept[...] = value
        for to, place in enumerate(places):
            at = pl.multiple_of(place * half, half)
            out[to * half : (to + 1) * half, :] = kept[pl.ds(at, half), :]


def call(kernel, rows, docs, width, operands, scratch=(), shapes=None):
    vmem = pl.BlockSpec(memory_space=pltpu.VMEM)
    return pl.pallas_call(
        kernel,
        out_shape=shapes or jax.ShapeDtypeStruct((rows, docs), jnp.float32),
        in_specs=[vmem] * len(operands),
        out_specs=[vmem] * len(shapes) if shapes else vmem,
        scratch_shapes=scratch,
        cost_estimate=pl.CostEstimate(
            flops=2 * rows * docs * width, bytes_accessed=2 * (rows + docs) * width, transcendentals=0
        ),
        compiler_params=pltpu.CompilerParams(vmem_limit_bytes=16 * 1024 * 1024),
    )(*operands)


def solution(mesh):
    n_grp, n_ex, n_feat = (mesh.shape[a] for a in ("grp", "ex", "feat"))
    assert n_grp <= 2

    def after(block, *waits):
        return lax.optimization_barrier((block, waits))[0] if waits else block

    def line(train, test, scale):
        docs, feats = train.shape
        queries = test.shape[0]
        half = queries // n_grp
        unit = feats // (sum(LINE) + SHIP)
        ex = lax.axis_index("ex")
        is_end, first_grp = (ex == 0) | (ex == n_ex - 1), lax.axis_index("grp") == 0
        test, is_end, first_grp = lax.optimization_barrier((test, is_end, first_grp))
        done, outs, swaps, middles, made = {}, [], [], [], []

        outer_pairs = [(i, i ^ 1) for i in range(n_ex)]
        middle_pairs = []
        for i in range(n_ex):
            for f in range(n_feat):
                to = (i, f ^ 1) if i in (0, n_ex - 1) else (n_ex - 1 - i, f)
                middle_pairs.append((i * n_feat + f, to[0] * n_feat + to[1]))

        def outer(name, block):
            waits = outs[-2:-1] + swaps[-3:-2] + made[-4:-3] + (first if len(outs) == 3 else [])
            outs.append(lax.ppermute(after(block, *waits), "ex", outer_pairs))
            done[name] = outs[-1]

        def middle(name, block):
            middles.append(lax.ppermute(after(block, *middles[-1:]), ("ex", "feat"), middle_pairs))
            done[name] = middles[-1]

        def swap(block):
            if n_grp == 1:
                return [block]
            waits = swaps[-2:-1]
            if len(swaps) > 2 * len(LINE):
                waits = swaps[-3:-2] + made[-3:-2]
            swaps.append(lax.ppermute(after(block, *waits), "grp", [(0, 1), (1, 0)]))
            return [block, swaps[-1]]

        def sum_over_feat(sums, *waits):
            held = sums.reshape(n_feat, -1, docs)
            bit = 1
            while bit < n_feat:
                pairs = held.reshape((-1, 2) + held.shape[1:])
                partner = [(i, i ^ bit) for i in range(n_feat)]
                send = after(pairs[:, 1], *waits)
                held, waits = pairs[:, 0] + lax.ppermute(send, "feat", partner), ()
                bit *= 2
            return held[0]

        def share(rows, start, count):
            here = slice(start * unit, (start + count) * unit)
            if n_grp == 1:
                return rows[:, here]
            return jnp.where(first_grp, rows[:half, here], rows[half:, here])

        firsts = [sum(LINE[:c]) for c in range(len(LINE))]
        columns = [slice(f * unit, (f + n) * unit) for f, n in zip(firsts, LINE)]
        mine = []
        for start, count in zip(firsts, LINE):
            mine.append(share(after(test, *mine[-1:]), start, count))
        trains = [train[:, q * 4 * unit : (q + 1) * 4 * unit] for q in range(4)]
        own = call(
            functools.partial(line_own_kernel, unit), queries, docs, feats, [test, scale, *trains]
        )
        first = [own]
        widths = LINE[:2]
        shapes = [jax.ShapeDtypeStruct((half, w * unit), test.dtype) for w in widths]
        shapes.append(jax.ShapeDtypeStruct((half, n_grp * SHIP * unit), test.dtype))
        *cargo, own_tests = call(
            functools.partial(crate_kernel, unit, n_grp), docs, SHIP * unit, 1,
            [test, trains[3]], shapes=shapes,
        )

        sums = [own, None, None, None]
        n = len(LINE)

        def finish(t, c, block):
            parts = swap(block)
            quarters = sorted({j // 4 for j in range(firsts[c], firsts[c] + LINE[c])})
            operands = [*parts, scale, *(trains[q] for q in quarters)]
            sizes = (unit, firsts[c], LINE[c], quarters, len(parts))
            if (t, c) == (3, n - 1):
                return sizes, operands
            base = [] if sums[t] is None else [sums[t]]
            kernel = functools.partial(line_part_kernel, *sizes)
            sums[t] = call(kernel, queries, docs, LINE[c] * unit, operands + base)
            made.append(sums[t])

        for c in range(n):
            outer(f"E1{c}", mine[c])
            middle(f"O1{c}", mine[c])
            finish(1, c, done[f"E1{c}"])
        for c in range(n):
            inner = done[f"O1{c}"]
            outer(f"E2{c}", jnp.where(is_end, cargo[c], inner) if c < len(cargo) else inner)
            middle(f"O2{c}", done[f"E1{c}"])
            finish(2, c, jnp.where(is_end, done[f"E2{c}"], inner))
        end_tests = done["E20"][:, : own_tests.shape[1]]
        middle("OS", jnp.concatenate([own_tests, end_tests], axis=0))
        for c in range(n):
            inner = done[f"O2{c}"]
            outer(f"E3{c}", inner)
            last = finish(3, c, jnp.where(is_end, done[f"E3{c}"], inner))
        shape = jax.ShapeDtypeStruct((n_ex * queries, docs), jnp.float32)
        landed = [done["E20"], done["E21"]]
        near, far = call(
            functools.partial(shipped_kernel, n_grp, n_feat, unit, len(landed)),
            n_ex * queries, docs, 2 * SHIP * unit,
            [test, scale, trains[3], done["OS"], *landed],
            [pltpu.VMEM(shape.shape, jnp.float32)], shapes=[shape, shape],
        )
        back = lax.ppermute(sum_over_feat(far), "ex", outer_pairs)
        sizes, operands = last
        total = call(
            functools.partial(line_last_kernel, n_grp, n_feat, *sizes),
            n_ex * queries, docs, LINE[-1] * unit, [*operands, near, *sums],
            [pltpu.VMEM(shape.shape, jnp.float32)],
        )
        out = sum_over_feat(total, back) + jnp.where(is_end, back, 0.0)
        return out.T

    def on_device(train, test, hess):
        docs, feats = train.shape
        queries = test.shape[0]
        half = queries // n_grp
        unit = 8 * LANES
        lanes = feats // LANES
        cuts = [c * lanes // CHUNKS * LANES for c in range(CHUNKS + 1)]
        starts, columns = cuts[:-1], [slice(*ends) for ends in zip(cuts[:-1], cuts[1:])]
        first_grp = lax.axis_index("grp") == 0
        ring = [(i, (i + 1) % n_ex) for i in range(n_ex)]
        hops, swaps, made, first = [], [], [], []

        def after(block, *waits):
            return lax.optimization_barrier((block, waits))[0] if waits else block

        def hop(block):
            waits = hops[-2:-1] + swaps[-4:-3] + made[-4:-3] + (first if len(hops) == 3 else [])
            hops.append(lax.ppermute(after(block, *waits), "ex", ring))
            return hops[-1]

        def swap(block):
            if n_grp == 1:
                return [block]
            waits = swaps[-2:-1]
            if len(swaps) > (n_ex - 2) * CHUNKS:
                waits = swaps[-3:-2] + made[-3:-2]
            swaps.append(lax.ppermute(after(block, *waits), "grp", [(0, 1), (1, 0)]))
            return [block, swaps[-1]]

        def sum_over_feat(sums):
            held = sums.reshape(n_feat, -1, docs)
            bit = 1
            while bit < n_feat:
                pairs = held.reshape((-1, 2) + held.shape[1:])
                partner = [(i, i ^ bit) for i in range(n_feat)]
                held = pairs[:, 0] + lax.ppermute(pairs[:, 1], "feat", partner)
                bit *= 2
            return held[0]

        def share(rows, columns):
            if n_grp == 1:
                return rows[:, columns]
            return jnp.where(first_grp, rows[:half, columns], rows[half:, columns])

        scale = (1.0 / (hess + jnp.float32(0.1))).reshape(1, feats)
        if n_ex == len(KEPT):
            return line(train, test, scale)
        held = []
        for here in columns:
            held.append(share(after(test, *held[-1:]), here))
        trains = [train[:, here] for here in columns]
        own = call(
            functools.partial(own_kernel, starts, unit), queries, docs, feats, [test, scale, *trains]
        )
        first.append(own)
        final = n_ex - 1
        sums = [own] + [None] * final
        for t in range(1, n_ex):
            for c, (start, here) in enumerate(zip(starts, columns)):
                held[c] = hop(held[c])
                parts = swap(held[c])
                operands = [*parts, scale, trains[c]]
                if (t, c) == (final, CHUNKS - 1):
                    continue
                base = [] if sums[t] is None else [sums[t]]
                sums[t] = call(
                    functools.partial(part_kernel, start, unit, len(parts), len(base)),
                    queries, docs, here.stop - here.start, operands + base,
                )
                made.append(sums[t])
        total = call(
            functools.partial(last_kernel, n_grp, n_ex, n_feat, start, unit, len(parts)),
            n_ex * queries, docs, here.stop - here.start, [*operands, *sums],
            [pltpu.VMEM((n_ex * queries, docs), jnp.float32)],
        )
        return sum_over_feat(total).T

    return jax.shard_map(
        on_device,
        mesh=mesh,
        in_specs=(P(("grp", "ex"), "feat"), P("ex", "feat"), P("feat")),
        out_specs=P(("grp", "ex"), "feat"),
        check_vma=False,
    )
```

```python
import functools

import jax
import jax.numpy as jnp
from jax import lax
from jax.experimental import pallas as pl
from jax.experimental.pallas import tpu as pltpu
from jax.sharding import PartitionSpec as P

CONTRACT = (((1,), (1,)), ((), ()))
LANES = 128
CHUNKS = 4


def product(rows, scale, train, unit):
    width, total = train.shape[1], None
    for at in range(0, width, unit):
        here = slice(at, min(at + unit, width))
        precond = (rows(here).astype(jnp.float32) * scale(here)).astype(jnp.bfloat16)
        part = lax.dot_general(
            precond, train[:, here], CONTRACT, preferred_element_type=jnp.float32
        )
        total = part if total is None else total + part
    return total


def own_kernel(starts, unit, test, scale, *refs):
    trains, out = refs[:-1], refs[-1]
    total = None
    for start, train in zip(starts, trains):
        column = lambda here: slice(start + here.start, start + here.stop)
        rows, scales = (lambda here, a=a: a[:, column(here)] for a in (test, scale))
        part = product(rows, scales, train, unit)
        total = part if total is None else total + part
    out[...] = total


def arrived_rows(parts):
    return lambda here: jnp.concatenate([p[:, here] for p in parts], axis=0)


def part_kernel(start, unit, n_parts, has_base, *refs):
    parts, (scale, train) = refs[:n_parts], refs[n_parts : n_parts + 2]
    column = lambda here: scale[:, start + here.start : start + here.stop]
    total = product(arrived_rows(parts), column, train, unit)
    refs[-1][...] = total + refs[n_parts + 2][...] if has_base else total


def last_kernel(n_grp, n_ex, n_feat, start, unit, n_parts, *refs):
    parts, (scale, train) = refs[:n_parts], refs[n_parts : n_parts + 2]
    sums, (out, kept) = refs[n_parts + 2 : -2], refs[-2:]
    column = lambda here: scale[:, start + here.start : start + here.stop]
    total = product(arrived_rows(parts), column, train, unit) + sums[-1][...]
    queries = total.shape[0]
    half = queries // n_grp
    for t, value in enumerate([s[...] for s in sums[:-1]] + [total]):
        kept[t * queries : (t + 1) * queries, :] = value
    ex, grp, feat = (lax.axis_index(a) for a in ("ex", "grp", "feat"))
    units = n_ex * n_grp
    each = units // n_feat
    for to in range(units):
        unit_of = (feat ^ (to // each)) * each + to % each
        t = lax.rem(ex + (n_ex - lax.div(unit_of, n_grp)), n_ex)
        h = lax.rem(unit_of, n_grp)
        place = jnp.where(t == 0, h, lax.rem(h + n_grp - grp, n_grp))
        at = pl.multiple_of(t * queries + place * half, half)
        out[to * half : (to + 1) * half, :] = kept[pl.ds(at, half), :]


LINE, SHIP = (5, 5, 5), 1
KEPT = ((0, 1, 2, 3), (1, 0, 2, 3), (2, 3, 1, 0), (3, 2, 1, 0))


def line_rows(n_grp, n_feat, halved):
    ex, grp, feat = (lax.axis_index(a) for a in ("ex", "grp", "feat"))
    units = len(KEPT) * n_grp
    each = units // n_feat
    found = []
    for to in range(units):
        unit_of = (feat ^ (to // each)) * each + to % each
        block, h = lax.div(unit_of, n_grp), lax.rem(unit_of, n_grp)
        t = jnp.int32(0)
        for i, kept in enumerate(KEPT):
            for b in kept[1:]:
                t = jnp.where((ex == i) & (block == b), kept.index(b), t)
        place = jnp.where(t == 0, h, lax.rem(h + n_grp - grp, n_grp)) if halved else h
        found.append(t * n_grp + place)
    return found


def units_product(rows, scale, trains, unit, first, count):
    total = None
    for k in range(count):
        j = first + k
        column = scale[:, j * unit : (j + 1) * unit]
        precond = (rows(k).astype(jnp.float32) * column).astype(jnp.bfloat16)
        here = trains[j // 4][:, (j % 4) * unit : (j % 4 + 1) * unit]
        part = lax.dot_general(precond, here, CONTRACT, preferred_element_type=jnp.float32)
        total = part if total is None else total + part
    return total


def line_own_kernel(unit, test, scale, *refs):
    rows = lambda k: test[:, k * unit : (k + 1) * unit]
    refs[-1][...] = units_product(rows, scale, refs[:-1], unit, 0, sum(LINE))


def line_part_kernel(unit, first, count, quarters, n_parts, *refs):
    parts, scale = refs[:n_parts], refs[n_parts]
    trains = dict(zip(quarters, refs[n_parts + 1 :]))
    base = refs[n_parts + 1 + len(quarters) : -1]
    rows = lambda k: jnp.concatenate([p[:, k * unit : (k + 1) * unit] for p in parts], axis=0)
    total = units_product(rows, scale, trains, unit, first, count)
    refs[-1][...] = total + base[0][...] if base else total


def line_last_kernel(n_grp, n_feat, unit, first, count, quarters, n_parts, *refs):
    parts, scale = refs[:n_parts], refs[n_parts]
    trains = dict(zip(quarters, refs[n_parts + 1 :]))
    near, *sums = refs[n_parts + 1 + len(quarters) : -2]
    out, kept = refs[-2:]
    rows = lambda k: jnp.concatenate([p[:, k * unit : (k + 1) * unit] for p in parts], axis=0)
    total = units_product(rows, scale, trains, unit, first, count) + sums[-1][...]
    queries = total.shape[0]
    half = queries // n_grp
    for t, value in enumerate([s[...] for s in sums[:-1]] + [total]):
        kept[t * queries : (t + 1) * queries, :] = value
    for to, place in enumerate(line_rows(n_grp, n_feat, True)):
        at = pl.multiple_of(place * half, half)
        here = slice(to * half, (to + 1) * half)
        out[here, :] = kept[pl.ds(at, half), :] + near[here, :]


def crate_kernel(unit, n_grp, test, train, *outs):
    half = test.shape[0] // n_grp
    base = sum(LINE)
    blocks = []
    for h in range(n_grp):
        for x in range(SHIP):
            cols = slice((base + x) * unit, (base + x + 1) * unit)
            blocks.append(test[h * half : (h + 1) * half, cols])
    n_tests = len(blocks)
    for x in range(SHIP):
        at = ((base + x) % 4) * unit
        for g in range(train.shape[0] // half):
            blocks.append(train[g * half : (g + 1) * half, at : at + unit])
    for i, block in enumerate(blocks[:n_tests]):
        outs[-1][:, i * unit : (i + 1) * unit] = block
    for out in outs[:-1]:
        for i in range(out.shape[1] // unit):
            out[:, i * unit : (i + 1) * unit] = blocks.pop(0) if len(blocks) > 1 else blocks[0]


def shipped_kernel(n_grp, n_feat, unit, n_cargo, test, scale, train, other, *refs):
    cargo, (near, far, kept) = refs[:n_cargo], refs[n_cargo:]
    base = sum(LINE)
    half = test.shape[0] // n_grp
    blocks = [(c, i * unit) for c in cargo for i in range(c.shape[1] // unit)]
    tests, rows_of = blocks[: n_grp * SHIP], blocks[n_grp * SHIP :]
    groups = train.shape[0] // half
    sums = [None, None]
    for x in range(SHIP):
        parts = [test[:, (base + x) * unit : (base + x + 1) * unit]]
        for h in range(n_grp):
            ref, at = tests[h * SHIP + x]
            parts.append(ref[:, at : at + unit])
        for k in range(2):
            for h in range(n_grp):
                at = (h * SHIP + x) * unit
                parts.append(other[k * half : (k + 1) * half, at : at + unit])
        rows = jnp.concatenate(parts, axis=0)
        column = scale[:, (base + x) * unit : (base + x + 1) * unit]
        precond = (rows.astype(jnp.float32) * column).astype(jnp.bfloat16)
        at = ((base + x) % 4) * unit
        away = [ref[:, c : c + unit] for ref, c in rows_of[x * groups : (x + 1) * groups]]
        for i, docs in enumerate((train[:, at : at + unit], jnp.concatenate(away, axis=0))):
            part = lax.dot_general(precond, docs, CONTRACT, preferred_element_type=jnp.float32)
            sums[i] = part if sums[i] is None else sums[i] + part
    ex = lax.axis_index("ex")
    inner = (ex > 0) & (ex < len(KEPT) - 1)
    places = line_rows(n_grp, n_feat, False)
    for value, out in zip((jnp.where(inner, sums[0], 0.0), sums[1]), (near, far)):
        kept[...] = value
        for to, place in enumerate(places):
            at = pl.multiple_of(place * half, half)
            out[to * half : (to + 1) * half, :] = kept[pl.ds(at, half), :]


def call(kernel, rows, docs, width, operands, scratch=(), shapes=None):
    vmem = pl.BlockSpec(memory_space=pltpu.VMEM)
    return pl.pallas_call(
        kernel,
        out_shape=shapes or jax.ShapeDtypeStruct((rows, docs), jnp.float32),
        in_specs=[vmem] * len(operands),
        out_specs=[vmem] * len(shapes) if shapes else vmem,
        scratch_shapes=scratch,
        cost_estimate=pl.CostEstimate(
            flops=2 * rows * docs * width, bytes_accessed=2 * (rows + docs) * width, transcendentals=0
        ),
        compiler_params=pltpu.CompilerParams(vmem_limit_bytes=16 * 1024 * 1024),
    )(*operands)


def solution(mesh):
    n_grp, n_ex, n_feat = (mesh.shape[a] for a in ("grp", "ex", "feat"))
    assert n_grp <= 2

    def after(block, *waits):
        return lax.optimization_barrier((block, waits))[0] if waits else block

    def line(train, test, scale):
        docs, feats = train.shape
        queries = test.shape[0]
        half = queries // n_grp
        unit = feats // (sum(LINE) + SHIP)
        ex = lax.axis_index("ex")
        is_end, first_grp = (ex == 0) | (ex == n_ex - 1), lax.axis_index("grp") == 0
        test, is_end, first_grp = lax.optimization_barrier((test, is_end, first_grp))
        done, outs, swaps, middles, made = {}, [], [], [], []

        outer_pairs = [(i, i ^ 1) for i in range(n_ex)]
        middle_pairs = []
        for i in range(n_ex):
            for f in range(n_feat):
                to = (i, f ^ 1) if i in (0, n_ex - 1) else (n_ex - 1 - i, f)
                middle_pairs.append((i * n_feat + f, to[0] * n_feat + to[1]))

        def outer(name, block):
            waits = outs[-2:-1] + swaps[-4:-3] + made[-4:-3] + (first if len(outs) == 3 else [])
            outs.append(lax.ppermute(after(block, *waits), "ex", outer_pairs))
            done[name] = outs[-1]

        def middle(name, block):
            middles.append(lax.ppermute(after(block, *middles[-1:], *swaps[-2:-1]), ("ex", "feat"), middle_pairs))
            done[name] = middles[-1]

        def swap(block):
            if n_grp == 1:
                return [block]
            waits = swaps[-2:-1]
            if len(swaps) > 2 * len(LINE):
                waits = swaps[-3:-2] + made[-3:-2]
            swaps.append(lax.ppermute(after(block, *waits), "grp", [(0, 1), (1, 0)]))
            return [block, swaps[-1]]

        def sum_over_feat(sums, *waits):
            held = sums.reshape(n_feat, -1, docs)
            bit = 1
            while bit < n_feat:
                pairs = held.reshape((-1, 2) + held.shape[1:])
                partner = [(i, i ^ bit) for i in range(n_feat)]
                send = after(pairs[:, 1], *waits)
                held, waits = pairs[:, 0] + lax.ppermute(send, "feat", partner), ()
                bit *= 2
            return held[0]

        def share(rows, start, count):
            here = slice(start * unit, (start + count) * unit)
            if n_grp == 1:
                return rows[:, here]
            return jnp.where(first_grp, rows[:half, here], rows[half:, here])

        firsts = [sum(LINE[:c]) for c in range(len(LINE))]
        columns = [slice(f * unit, (f + n) * unit) for f, n in zip(firsts, LINE)]
        mine = []
        for start, count in zip(firsts, LINE):
            mine.append(share(after(test, *mine[-1:]), start, count))
        trains = [train[:, q * 4 * unit : (q + 1) * 4 * unit] for q in range(4)]
        own = call(
            functools.partial(line_own_kernel, unit), queries, docs, feats, [test, scale, *trains]
        )
        first = [own]
        widths = LINE[:2]
        shapes = [jax.ShapeDtypeStruct((half, w * unit), test.dtype) for w in widths]
        shapes.append(jax.ShapeDtypeStruct((half, n_grp * SHIP * unit), test.dtype))
        *cargo, own_tests = call(
            functools.partial(crate_kernel, unit, n_grp), docs, SHIP * unit, 1,
            [test, trains[3]], shapes=shapes,
        )

        sums = [own, None, None, None]
        n = len(LINE)

        def finish(t, c, block):
            parts = swap(block)
            quarters = sorted({j // 4 for j in range(firsts[c], firsts[c] + LINE[c])})
            operands = [*parts, scale, *(trains[q] for q in quarters)]
            sizes = (unit, firsts[c], LINE[c], quarters, len(parts))
            if (t, c) == (3, n - 1):
                return sizes, operands
            base = [] if sums[t] is None else [sums[t]]
            kernel = functools.partial(line_part_kernel, *sizes)
            sums[t] = call(kernel, queries, docs, LINE[c] * unit, operands + base)
            made.append(sums[t])

        for c in range(n):
            outer(f"E1{c}", mine[c])
            middle(f"O1{c}", mine[c])
            finish(1, c, done[f"E1{c}"])
        for c in range(n):
            inner = done[f"O1{c}"]
            outer(f"E2{c}", jnp.where(is_end, cargo[c], inner) if c < len(cargo) else inner)
            middle(f"O2{c}", done[f"E1{c}"])
            finish(2, c, jnp.where(is_end, done[f"E2{c}"], inner))
        end_tests = done["E20"][:, : own_tests.shape[1]]
        middle("OS", jnp.concatenate([own_tests, end_tests], axis=0))
        for c in range(n):
            inner = done[f"O2{c}"]
            outer(f"E3{c}", inner)
            last = finish(3, c, jnp.where(is_end, done[f"E3{c}"], inner))
        shape = jax.ShapeDtypeStruct((n_ex * queries, docs), jnp.float32)
        landed = [done["E20"], done["E21"]]
        near, far = call(
            functools.partial(shipped_kernel, n_grp, n_feat, unit, len(landed)),
            n_ex * queries, docs, 2 * SHIP * unit,
            [test, scale, trains[3], done["OS"], *landed],
            [pltpu.VMEM(shape.shape, jnp.float32)], shapes=[shape, shape],
        )
        back = lax.ppermute(sum_over_feat(far), "ex", outer_pairs)
        sizes, operands = last
        total = call(
            functools.partial(line_last_kernel, n_grp, n_feat, *sizes),
            n_ex * queries, docs, LINE[-1] * unit, [*operands, near, *sums],
            [pltpu.VMEM(shape.shape, jnp.float32)],
        )
        out = sum_over_feat(total, back) + jnp.where(is_end, back, 0.0)
        return out.T

    def on_device(train, test, hess):
        docs, feats = train.shape
        queries = test.shape[0]
        half = queries // n_grp
        unit = 8 * LANES
        lanes = feats // LANES
        cuts = [c * lanes // CHUNKS * LANES for c in range(CHUNKS + 1)]
        starts, columns = cuts[:-1], [slice(*ends) for ends in zip(cuts[:-1], cuts[1:])]
        first_grp = lax.axis_index("grp") == 0
        ring = [(i, (i + 1) % n_ex) for i in range(n_ex)]
        hops, swaps, made, first = [], [], [], []

        def after(block, *waits):
            return lax.optimization_barrier((block, waits))[0] if waits else block

        def hop(block):
            waits = hops[-2:-1] + swaps[-4:-3] + made[-4:-3] + (first if len(hops) == 3 else [])
            hops.append(lax.ppermute(after(block, *waits), "ex", ring))
            return hops[-1]

        def swap(block):
            if n_grp == 1:
                return [block]
            waits = swaps[-2:-1]
            if len(swaps) > (n_ex - 2) * CHUNKS:
                waits = swaps[-3:-2] + made[-3:-2]
            swaps.append(lax.ppermute(after(block, *waits), "grp", [(0, 1), (1, 0)]))
            return [block, swaps[-1]]

        def sum_over_feat(sums):
            held = sums.reshape(n_feat, -1, docs)
            bit = 1
            while bit < n_feat:
                pairs = held.reshape((-1, 2) + held.shape[1:])
                partner = [(i, i ^ bit) for i in range(n_feat)]
                held = pairs[:, 0] + lax.ppermute(pairs[:, 1], "feat", partner)
                bit *= 2
            return held[0]

        def share(rows, columns):
            if n_grp == 1:
                return rows[:, columns]
            return jnp.where(first_grp, rows[:half, columns], rows[half:, columns])

        scale = (1.0 / (hess + jnp.float32(0.1))).reshape(1, feats)
        if n_ex == len(KEPT):
            return line(train, test, scale)
        held = []
        for here in columns:
            held.append(share(after(test, *held[-1:]), here))
        trains = [train[:, here] for here in columns]
        own = call(
            functools.partial(own_kernel, starts, unit), queries, docs, feats, [test, scale, *trains]
        )
        first.append(own)
        final = n_ex - 1
        sums = [own] + [None] * final
        for t in range(1, n_ex):
            for c, (start, here) in enumerate(zip(starts, columns)):
                held[c] = hop(held[c])
                parts = swap(held[c])
                operands = [*parts, scale, trains[c]]
                if (t, c) == (final, CHUNKS - 1):
                    continue
                base = [] if sums[t] is None else [sums[t]]
                sums[t] = call(
                    functools.partial(part_kernel, start, unit, len(parts), len(base)),
                    queries, docs, here.stop - here.start, operands + base,
                )
                made.append(sums[t])
        total = call(
            functools.partial(last_kernel, n_grp, n_ex, n_feat, start, unit, len(parts)),
            n_ex * queries, docs, here.stop - here.start, [*operands, *sums],
            [pltpu.VMEM((n_ex * queries, docs), jnp.float32)],
        )
        return sum_over_feat(total).T

    return jax.shard_map(
        on_device,
        mesh=mesh,
        in_specs=(P(("grp", "ex"), "feat"), P("ex", "feat"), P("feat")),
        out_specs=P(("grp", "ex"), "feat"),
        check_vma=False,
    )
```

```python
import functools

import jax
import jax.numpy as jnp
from jax import lax
from jax.experimental import pallas as pl
from jax.experimental.pallas import tpu as pltpu
from jax.sharding import PartitionSpec as P

CONTRACT = (((1,), (1,)), ((), ()))
LANES = 128
CHUNKS = 4


def product(rows, scale, train, unit):
    width, total = train.shape[1], None
    for at in range(0, width, unit):
        here = slice(at, min(at + unit, width))
        precond = (rows(here).astype(jnp.float32) * scale(here)).astype(jnp.bfloat16)
        part = lax.dot_general(
            precond, train[:, here], CONTRACT, preferred_element_type=jnp.float32
        )
        total = part if total is None else total + part
    return total


def own_kernel(starts, unit, test, scale, *refs):
    trains, out = refs[:-1], refs[-1]
    total = None
    for start, train in zip(starts, trains):
        column = lambda here: slice(start + here.start, start + here.stop)
        rows, scales = (lambda here, a=a: a[:, column(here)] for a in (test, scale))
        part = product(rows, scales, train, unit)
        total = part if total is None else total + part
    out[...] = total


def arrived_rows(parts):
    return lambda here: jnp.concatenate([p[:, here] for p in parts], axis=0)


def part_kernel(start, unit, n_parts, has_base, *refs):
    parts, (scale, train) = refs[:n_parts], refs[n_parts : n_parts + 2]
    column = lambda here: scale[:, start + here.start : start + here.stop]
    total = product(arrived_rows(parts), column, train, unit)
    refs[-1][...] = total + refs[n_parts + 2][...] if has_base else total


def last_kernel(n_grp, n_ex, n_feat, start, unit, n_parts, *refs):
    parts, (scale, train) = refs[:n_parts], refs[n_parts : n_parts + 2]
    sums, (out, kept) = refs[n_parts + 2 : -2], refs[-2:]
    column = lambda here: scale[:, start + here.start : start + here.stop]
    total = product(arrived_rows(parts), column, train, unit) + sums[-1][...]
    queries = total.shape[0]
    half = queries // n_grp
    for t, value in enumerate([s[...] for s in sums[:-1]] + [total]):
        kept[t * queries : (t + 1) * queries, :] = value
    ex, grp, feat = (lax.axis_index(a) for a in ("ex", "grp", "feat"))
    units = n_ex * n_grp
    each = units // n_feat
    for to in range(units):
        unit_of = (feat ^ (to // each)) * each + to % each
        t = lax.rem(ex + (n_ex - lax.div(unit_of, n_grp)), n_ex)
        h = lax.rem(unit_of, n_grp)
        place = jnp.where(t == 0, h, lax.rem(h + n_grp - grp, n_grp))
        at = pl.multiple_of(t * queries + place * half, half)
        out[to * half : (to + 1) * half, :] = kept[pl.ds(at, half), :]


LINE, SHIP = (5, 5, 5), 1
KEPT = ((0, 1, 2, 3), (1, 0, 2, 3), (2, 3, 1, 0), (3, 2, 1, 0))


def line_rows(n_grp, n_feat, halved):
    ex, grp, feat = (lax.axis_index(a) for a in ("ex", "grp", "feat"))
    units = len(KEPT) * n_grp
    each = units // n_feat
    found = []
    for to in range(units):
        unit_of = (feat ^ (to // each)) * each + to % each
        block, h = lax.div(unit_of, n_grp), lax.rem(unit_of, n_grp)
        t = jnp.int32(0)
        for i, kept in enumerate(KEPT):
            for b in kept[1:]:
                t = jnp.where((ex == i) & (block == b), kept.index(b), t)
        place = jnp.where(t == 0, h, lax.rem(h + n_grp - grp, n_grp)) if halved else h
        found.append(t * n_grp + place)
    return found


def units_product(rows, scale, trains, unit, first, count):
    total = None
    for k in range(count):
        j = first + k
        column = scale[:, j * unit : (j + 1) * unit]
        precond = (rows(k).astype(jnp.float32) * column).astype(jnp.bfloat16)
        here = trains[j // 4][:, (j % 4) * unit : (j % 4 + 1) * unit]
        part = lax.dot_general(precond, here, CONTRACT, preferred_element_type=jnp.float32)
        total = part if total is None else total + part
    return total


def line_own_kernel(unit, test, scale, *refs):
    rows = lambda k: test[:, k * unit : (k + 1) * unit]
    refs[-1][...] = units_product(rows, scale, refs[:-1], unit, 0, sum(LINE))


def line_part_kernel(unit, first, count, quarters, n_parts, *refs):
    parts, scale = refs[:n_parts], refs[n_parts]
    trains = dict(zip(quarters, refs[n_parts + 1 :]))
    base = refs[n_parts + 1 + len(quarters) : -1]
    rows = lambda k: jnp.concatenate([p[:, k * unit : (k + 1) * unit] for p in parts], axis=0)
    total = units_product(rows, scale, trains, unit, first, count)
    refs[-1][...] = total + base[0][...] if base else total


def line_last_kernel(n_grp, n_feat, unit, first, count, quarters, n_parts, *refs):
    parts, scale = refs[:n_parts], refs[n_parts]
    trains = dict(zip(quarters, refs[n_parts + 1 :]))
    near, *sums = refs[n_parts + 1 + len(quarters) : -2]
    out, kept = refs[-2:]
    rows = lambda k: jnp.concatenate([p[:, k * unit : (k + 1) * unit] for p in parts], axis=0)
    total = units_product(rows, scale, trains, unit, first, count) + sums[-1][...]
    queries = total.shape[0]
    half = queries // n_grp
    for t, value in enumerate([s[...] for s in sums[:-1]] + [total]):
        kept[t * queries : (t + 1) * queries, :] = value
    for to, place in enumerate(line_rows(n_grp, n_feat, True)):
        at = pl.multiple_of(place * half, half)
        here = slice(to * half, (to + 1) * half)
        out[here, :] = kept[pl.ds(at, half), :] + near[here, :]


def crate_kernel(unit, n_grp, test, train, *outs):
    half = test.shape[0] // n_grp
    base = sum(LINE)
    blocks = []
    for h in range(n_grp):
        for x in range(SHIP):
            cols = slice((base + x) * unit, (base + x + 1) * unit)
            blocks.append(test[h * half : (h + 1) * half, cols])
    n_tests = len(blocks)
    for x in range(SHIP):
        at = ((base + x) % 4) * unit
        for g in range(train.shape[0] // half):
            blocks.append(train[g * half : (g + 1) * half, at : at + unit])
    for i, block in enumerate(blocks[:n_tests]):
        outs[-1][:, i * unit : (i + 1) * unit] = block
    for out in outs[:-1]:
        for i in range(out.shape[1] // unit):
            out[:, i * unit : (i + 1) * unit] = blocks.pop(0) if len(blocks) > 1 else blocks[0]


def shipped_kernel(n_grp, n_feat, unit, n_cargo, test, scale, train, other, *refs):
    cargo, (near, far, kept) = refs[:n_cargo], refs[n_cargo:]
    base = sum(LINE)
    half = test.shape[0] // n_grp
    blocks = [(c, i * unit) for c in cargo for i in range(c.shape[1] // unit)]
    tests, rows_of = blocks[: n_grp * SHIP], blocks[n_grp * SHIP :]
    groups = train.shape[0] // half
    sums = [None, None]
    for x in range(SHIP):
        parts = [test[:, (base + x) * unit : (base + x + 1) * unit]]
        for h in range(n_grp):
            ref, at = tests[h * SHIP + x]
            parts.append(ref[:, at : at + unit])
        for k in range(2):
            for h in range(n_grp):
                at = (h * SHIP + x) * unit
                parts.append(other[k * half : (k + 1) * half, at : at + unit])
        rows = jnp.concatenate(parts, axis=0)
        column = scale[:, (base + x) * unit : (base + x + 1) * unit]
        precond = (rows.astype(jnp.float32) * column).astype(jnp.bfloat16)
        at = ((base + x) % 4) * unit
        away = [ref[:, c : c + unit] for ref, c in rows_of[x * groups : (x + 1) * groups]]
        for i, docs in enumerate((train[:, at : at + unit], jnp.concatenate(away, axis=0))):
            part = lax.dot_general(precond, docs, CONTRACT, preferred_element_type=jnp.float32)
            sums[i] = part if sums[i] is None else sums[i] + part
    ex = lax.axis_index("ex")
    inner = (ex > 0) & (ex < len(KEPT) - 1)
    places = line_rows(n_grp, n_feat, False)
    for value, out in zip((jnp.where(inner, sums[0], 0.0), sums[1]), (near, far)):
        kept[...] = value
        for to, place in enumerate(places):
            at = pl.multiple_of(place * half, half)
            out[to * half : (to + 1) * half, :] = kept[pl.ds(at, half), :]


def call(kernel, rows, docs, width, operands, scratch=(), shapes=None):
    vmem = pl.BlockSpec(memory_space=pltpu.VMEM)
    return pl.pallas_call(
        kernel,
        out_shape=shapes or jax.ShapeDtypeStruct((rows, docs), jnp.float32),
        in_specs=[vmem] * len(operands),
        out_specs=[vmem] * len(shapes) if shapes else vmem,
        scratch_shapes=scratch,
        cost_estimate=pl.CostEstimate(
            flops=2 * rows * docs * width, bytes_accessed=2 * (rows + docs) * width, transcendentals=0
        ),
        compiler_params=pltpu.CompilerParams(vmem_limit_bytes=16 * 1024 * 1024),
    )(*operands)


def solution(mesh):
    n_grp, n_ex, n_feat = (mesh.shape[a] for a in ("grp", "ex", "feat"))
    assert n_grp <= 2

    def after(block, *waits):
        return lax.optimization_barrier((block, waits))[0] if waits else block

    def line(train, test, scale):
        docs, feats = train.shape
        queries = test.shape[0]
        half = queries // n_grp
        unit = feats // (sum(LINE) + SHIP)
        ex = lax.axis_index("ex")
        is_end, first_grp = (ex == 0) | (ex == n_ex - 1), lax.axis_index("grp") == 0
        test, is_end, first_grp = lax.optimization_barrier((test, is_end, first_grp))
        done, outs, swaps, middles, made = {}, [], [], [], []

        outer_pairs = [(i, i ^ 1) for i in range(n_ex)]
        middle_pairs = []
        for i in range(n_ex):
            for f in range(n_feat):
                to = (i, f ^ 1) if i in (0, n_ex - 1) else (n_ex - 1 - i, f)
                middle_pairs.append((i * n_feat + f, to[0] * n_feat + to[1]))

        def outer(name, block):
            waits = outs[-2:-1] + swaps[-4:-3] + made[-4:-3] + (first if len(outs) == 4 else [])
            outs.append(lax.ppermute(after(block, *waits), "ex", outer_pairs))
            done[name] = outs[-1]

        def middle(name, block):
            middles.append(lax.ppermute(after(block, *middles[-1:], *swaps[-2:-1]), ("ex", "feat"), middle_pairs))
            done[name] = middles[-1]

        def swap(block):
            if n_grp == 1:
                return [block]
            waits = swaps[-2:-1]
            if len(swaps) > 2 * len(LINE):
                waits = swaps[-3:-2] + made[-3:-2]
            swaps.append(lax.ppermute(after(block, *waits), "grp", [(0, 1), (1, 0)]))
            return [block, swaps[-1]]

        def sum_over_feat(sums, *waits):
            held = sums.reshape(n_feat, -1, docs)
            bit = 1
            while bit < n_feat:
                pairs = held.reshape((-1, 2) + held.shape[1:])
                partner = [(i, i ^ bit) for i in range(n_feat)]
                send = after(pairs[:, 1], *waits)
                held, waits = pairs[:, 0] + lax.ppermute(send, "feat", partner), ()
                bit *= 2
            return held[0]

        def share(rows, start, count):
            here = slice(start * unit, (start + count) * unit)
            if n_grp == 1:
                return rows[:, here]
            return jnp.where(first_grp, rows[:half, here], rows[half:, here])

        firsts = [sum(LINE[:c]) for c in range(len(LINE))]
        columns = [slice(f * unit, (f + n) * unit) for f, n in zip(firsts, LINE)]
        mine = []
        for start, count in zip(firsts, LINE):
            mine.append(share(after(test, *mine[-1:]), start, count))
        trains = [train[:, q * 4 * unit : (q + 1) * 4 * unit] for q in range(4)]
        widths = LINE[:2]
        shapes = [jax.ShapeDtypeStruct((half, w * unit), test.dtype) for w in widths]
        shapes.append(jax.ShapeDtypeStruct((half, n_grp * SHIP * unit), test.dtype))
        *cargo, own_tests = call(
            functools.partial(crate_kernel, unit, n_grp), docs, SHIP * unit, 1,
            [test, trains[3]], shapes=shapes,
        )

        first, sums = [], [None] * n_ex
        n = len(LINE)

        def finish(t, c, block):
            parts = swap(block)
            quarters = sorted({j // 4 for j in range(firsts[c], firsts[c] + LINE[c])})
            operands = [*parts, scale, *(trains[q] for q in quarters)]
            sizes = (unit, firsts[c], LINE[c], quarters, len(parts))
            if (t, c) == (3, n - 1):
                return sizes, operands
            base = [] if sums[t] is None else [sums[t]]
            kernel = functools.partial(line_part_kernel, *sizes)
            sums[t] = call(kernel, queries, docs, LINE[c] * unit, operands + base)
            made.append(sums[t])

        for c in range(n):
            outer(f"E1{c}", mine[c])
            middle(f"O1{c}", mine[c])
            if c == 0:
                late = after(test, done["E10"])
                sums[0] = call(
                    functools.partial(line_own_kernel, unit), queries, docs, feats, [late, scale, *trains]
                )
                first.append(sums[0])
            finish(1, c, done[f"E1{c}"])
        for c in range(n):
            inner = done[f"O1{c}"]
            outer(f"E2{c}", jnp.where(is_end, cargo[c], inner) if c < len(cargo) else inner)
            middle(f"O2{c}", done[f"E1{c}"])
            finish(2, c, jnp.where(is_end, done[f"E2{c}"], inner))
        end_tests = done["E20"][:, : own_tests.shape[1]]
        middle("OS", jnp.concatenate([own_tests, end_tests], axis=0))
        for c in range(n):
            inner = done[f"O2{c}"]
            outer(f"E3{c}", inner)
            last = finish(3, c, jnp.where(is_end, done[f"E3{c}"], inner))
        shape = jax.ShapeDtypeStruct((n_ex * queries, docs), jnp.float32)
        landed = [done["E20"], done["E21"]]
        near, far = call(
            functools.partial(shipped_kernel, n_grp, n_feat, unit, len(landed)),
            n_ex * queries, docs, 2 * SHIP * unit,
            [test, scale, trains[3], done["OS"], *landed],
            [pltpu.VMEM(shape.shape, jnp.float32)], shapes=[shape, shape],
        )
        back = lax.ppermute(sum_over_feat(far), "ex", outer_pairs)
        sizes, operands = last
        total = call(
            functools.partial(line_last_kernel, n_grp, n_feat, *sizes),
            n_ex * queries, docs, LINE[-1] * unit, [*operands, near, *sums],
            [pltpu.VMEM(shape.shape, jnp.float32)],
        )
        out = sum_over_feat(total, back) + jnp.where(is_end, back, 0.0)
        return out.T

    def on_device(train, test, hess):
        docs, feats = train.shape
        queries = test.shape[0]
        half = queries // n_grp
        unit = 8 * LANES
        lanes = feats // LANES
        cuts = [c * lanes // CHUNKS * LANES for c in range(CHUNKS + 1)]
        starts, columns = cuts[:-1], [slice(*ends) for ends in zip(cuts[:-1], cuts[1:])]
        first_grp = lax.axis_index("grp") == 0
        ring = [(i, (i + 1) % n_ex) for i in range(n_ex)]
        hops, swaps, made, first = [], [], [], []

        def after(block, *waits):
            return lax.optimization_barrier((block, waits))[0] if waits else block

        def hop(block):
            waits = hops[-2:-1] + swaps[-4:-3] + made[-4:-3] + (first if len(hops) == 3 else [])
            hops.append(lax.ppermute(after(block, *waits), "ex", ring))
            return hops[-1]

        def swap(block):
            if n_grp == 1:
                return [block]
            waits = swaps[-2:-1]
            if len(swaps) > (n_ex - 2) * CHUNKS:
                waits = swaps[-3:-2] + made[-3:-2]
            swaps.append(lax.ppermute(after(block, *waits), "grp", [(0, 1), (1, 0)]))
            return [block, swaps[-1]]

        def sum_over_feat(sums):
            held = sums.reshape(n_feat, -1, docs)
            bit = 1
            while bit < n_feat:
                pairs = held.reshape((-1, 2) + held.shape[1:])
                partner = [(i, i ^ bit) for i in range(n_feat)]
                held = pairs[:, 0] + lax.ppermute(pairs[:, 1], "feat", partner)
                bit *= 2
            return held[0]

        def share(rows, columns):
            if n_grp == 1:
                return rows[:, columns]
            return jnp.where(first_grp, rows[:half, columns], rows[half:, columns])

        scale = (1.0 / (hess + jnp.float32(0.1))).reshape(1, feats)
        if n_ex == len(KEPT):
            return line(train, test, scale)
        held = []
        for here in columns:
            held.append(share(after(test, *held[-1:]), here))
        trains = [train[:, here] for here in columns]
        own = call(
            functools.partial(own_kernel, starts, unit), queries, docs, feats, [test, scale, *trains]
        )
        first.append(own)
        final = n_ex - 1
        sums = [own] + [None] * final
        for t in range(1, n_ex):
            for c, (start, here) in enumerate(zip(starts, columns)):
                held[c] = hop(held[c])
                parts = swap(held[c])
                operands = [*parts, scale, trains[c]]
                if (t, c) == (final, CHUNKS - 1):
                    continue
                base = [] if sums[t] is None else [sums[t]]
                sums[t] = call(
                    functools.partial(part_kernel, start, unit, len(parts), len(base)),
                    queries, docs, here.stop - here.start, operands + base,
                )
                made.append(sums[t])
        total = call(
            functools.partial(last_kernel, n_grp, n_ex, n_feat, start, unit, len(parts)),
            n_ex * queries, docs, here.stop - here.start, [*operands, *sums],
            [pltpu.VMEM((n_ex * queries, docs), jnp.float32)],
        )
        return sum_over_feat(total).T

    return jax.shard_map(
        on_device,
        mesh=mesh,
        in_specs=(P(("grp", "ex"), "feat"), P("ex", "feat"), P("feat")),
        out_specs=P(("grp", "ex"), "feat"),
        check_vma=False,
    )
```

```python
import functools

import jax
import jax.numpy as jnp
from jax import lax
from jax.experimental import pallas as pl
from jax.experimental.pallas import tpu as pltpu
from jax.sharding import PartitionSpec as P

CONTRACT = (((1,), (1,)), ((), ()))
LANES = 128
CHUNKS = 4


def product(rows, scale, train, unit):
    width, total = train.shape[1], None
    for at in range(0, width, unit):
        here = slice(at, min(at + unit, width))
        precond = (rows(here).astype(jnp.float32) * scale(here)).astype(jnp.bfloat16)
        part = lax.dot_general(
            precond, train[:, here], CONTRACT, preferred_element_type=jnp.float32
        )
        total = part if total is None else total + part
    return total


def own_kernel(starts, unit, test, scale, *refs):
    trains, out = refs[:-1], refs[-1]
    total = None
    for start, train in zip(starts, trains):
        column = lambda here: slice(start + here.start, start + here.stop)
        rows, scales = (lambda here, a=a: a[:, column(here)] for a in (test, scale))
        part = product(rows, scales, train, unit)
        total = part if total is None else total + part
    out[...] = total


def arrived_rows(parts):
    return lambda here: jnp.concatenate([p[:, here] for p in parts], axis=0)


def part_kernel(start, unit, n_parts, has_base, *refs):
    parts, (scale, train) = refs[:n_parts], refs[n_parts : n_parts + 2]
    column = lambda here: scale[:, start + here.start : start + here.stop]
    total = product(arrived_rows(parts), column, train, unit)
    refs[-1][...] = total + refs[n_parts + 2][...] if has_base else total


def last_kernel(n_grp, n_ex, n_feat, start, unit, n_parts, *refs):
    parts, (scale, train) = refs[:n_parts], refs[n_parts : n_parts + 2]
    sums, (out, kept) = refs[n_parts + 2 : -2], refs[-2:]
    column = lambda here: scale[:, start + here.start : start + here.stop]
    total = product(arrived_rows(parts), column, train, unit) + sums[-1][...]
    queries = total.shape[0]
    half = queries // n_grp
    for t, value in enumerate([s[...] for s in sums[:-1]] + [total]):
        kept[t * queries : (t + 1) * queries, :] = value
    ex, grp, feat = (lax.axis_index(a) for a in ("ex", "grp", "feat"))
    units = n_ex * n_grp
    each = units // n_feat
    for to in range(units):
        unit_of = (feat ^ (to // each)) * each + to % each
        t = lax.rem(ex + (n_ex - lax.div(unit_of, n_grp)), n_ex)
        h = lax.rem(unit_of, n_grp)
        place = jnp.where(t == 0, h, lax.rem(h + n_grp - grp, n_grp))
        at = pl.multiple_of(t * queries + place * half, half)
        out[to * half : (to + 1) * half, :] = kept[pl.ds(at, half), :]


LINE, SHIP = (5, 5, 5), 1
KEPT = ((0, 1, 2, 3), (1, 0, 2, 3), (2, 3, 1, 0), (3, 2, 1, 0))


def line_rows(n_grp, n_feat, halved):
    ex, grp, feat = (lax.axis_index(a) for a in ("ex", "grp", "feat"))
    units = len(KEPT) * n_grp
    each = units // n_feat
    found = []
    for to in range(units):
        unit_of = (feat ^ (to // each)) * each + to % each
        block, h = lax.div(unit_of, n_grp), lax.rem(unit_of, n_grp)
        t = jnp.int32(0)
        for i, kept in enumerate(KEPT):
            for b in kept[1:]:
                t = jnp.where((ex == i) & (block == b), kept.index(b), t)
        place = jnp.where(t == 0, h, lax.rem(h + n_grp - grp, n_grp)) if halved else h
        found.append(t * n_grp + place)
    return found


def units_product(rows, scale, trains, unit, first, count):
    total = None
    for k in range(count):
        j = first + k
        column = scale[:, j * unit : (j + 1) * unit]
        precond = (rows(k).astype(jnp.float32) * column).astype(jnp.bfloat16)
        here = trains[j // 4][:, (j % 4) * unit : (j % 4 + 1) * unit]
        part = lax.dot_general(precond, here, CONTRACT, preferred_element_type=jnp.float32)
        total = part if total is None else total + part
    return total


def line_own_kernel(unit, test, scale, *refs):
    rows = lambda k: test[:, k * unit : (k + 1) * unit]
    refs[-1][...] = units_product(rows, scale, refs[:-1], unit, 0, sum(LINE))


def line_part_kernel(unit, first, count, quarters, n_parts, *refs):
    parts, scale = refs[:n_parts], refs[n_parts]
    trains = dict(zip(quarters, refs[n_parts + 1 :]))
    base = refs[n_parts + 1 + len(quarters) : -1]
    rows = lambda k: jnp.concatenate([p[:, k * unit : (k + 1) * unit] for p in parts], axis=0)
    total = units_product(rows, scale, trains, unit, first, count)
    refs[-1][...] = total + base[0][...] if base else total


def line_last_kernel(n_grp, n_feat, unit, first, count, quarters, n_parts, *refs):
    parts, scale = refs[:n_parts], refs[n_parts]
    trains = dict(zip(quarters, refs[n_parts + 1 :]))
    near, *sums = refs[n_parts + 1 + len(quarters) : -2]
    out, kept = refs[-2:]
    rows = lambda k: jnp.concatenate([p[:, k * unit : (k + 1) * unit] for p in parts], axis=0)
    total = units_product(rows, scale, trains, unit, first, count) + sums[-1][...]
    queries = total.shape[0]
    half = queries // n_grp
    for t, value in enumerate([s[...] for s in sums[:-1]] + [total]):
        kept[t * queries : (t + 1) * queries, :] = value
    for to, place in enumerate(line_rows(n_grp, n_feat, True)):
        at = pl.multiple_of(place * half, half)
        here = slice(to * half, (to + 1) * half)
        out[here, :] = kept[pl.ds(at, half), :] + near[here, :]


def crate_kernel(unit, n_grp, test, train, *outs):
    half = test.shape[0] // n_grp
    base = sum(LINE)
    blocks = []
    for h in range(n_grp):
        for x in range(SHIP):
            cols = slice((base + x) * unit, (base + x + 1) * unit)
            blocks.append(test[h * half : (h + 1) * half, cols])
    n_tests = len(blocks)
    for x in range(SHIP):
        at = ((base + x) % 4) * unit
        for g in range(train.shape[0] // half):
            blocks.append(train[g * half : (g + 1) * half, at : at + unit])
    for i, block in enumerate(blocks[:n_tests]):
        outs[-1][:, i * unit : (i + 1) * unit] = block
    for out in outs[:-1]:
        for i in range(out.shape[1] // unit):
            out[:, i * unit : (i + 1) * unit] = blocks.pop(0) if len(blocks) > 1 else blocks[0]


def shipped_kernel(n_grp, n_feat, unit, n_cargo, test, scale, train, other, *refs):
    cargo, (near, far, kept) = refs[:n_cargo], refs[n_cargo:]
    base = sum(LINE)
    half = test.shape[0] // n_grp
    blocks = [(c, i * unit) for c in cargo for i in range(c.shape[1] // unit)]
    tests, rows_of = blocks[: n_grp * SHIP], blocks[n_grp * SHIP :]
    groups = train.shape[0] // half
    sums = [None, None]
    for x in range(SHIP):
        parts = [test[:, (base + x) * unit : (base + x + 1) * unit]]
        for h in range(n_grp):
            ref, at = tests[h * SHIP + x]
            parts.append(ref[:, at : at + unit])
        for k in range(2):
            for h in range(n_grp):
                at = (h * SHIP + x) * unit
                parts.append(other[k * half : (k + 1) * half, at : at + unit])
        rows = jnp.concatenate(parts, axis=0)
        column = scale[:, (base + x) * unit : (base + x + 1) * unit]
        precond = (rows.astype(jnp.float32) * column).astype(jnp.bfloat16)
        at = ((base + x) % 4) * unit
        away = [ref[:, c : c + unit] for ref, c in rows_of[x * groups : (x + 1) * groups]]
        for i, docs in enumerate((train[:, at : at + unit], jnp.concatenate(away, axis=0))):
            part = lax.dot_general(precond, docs, CONTRACT, preferred_element_type=jnp.float32)
            sums[i] = part if sums[i] is None else sums[i] + part
    ex = lax.axis_index("ex")
    inner = (ex > 0) & (ex < len(KEPT) - 1)
    places = line_rows(n_grp, n_feat, False)
    for value, out in zip((jnp.where(inner, sums[0], 0.0), sums[1]), (near, far)):
        kept[...] = value
        for to, place in enumerate(places):
            at = pl.multiple_of(place * half, half)
            out[to * half : (to + 1) * half, :] = kept[pl.ds(at, half), :]


def call(kernel, rows, docs, width, operands, scratch=(), shapes=None):
    vmem = pl.BlockSpec(memory_space=pltpu.VMEM)
    return pl.pallas_call(
        kernel,
        out_shape=shapes or jax.ShapeDtypeStruct((rows, docs), jnp.float32),
        in_specs=[vmem] * len(operands),
        out_specs=[vmem] * len(shapes) if shapes else vmem,
        scratch_shapes=scratch,
        cost_estimate=pl.CostEstimate(
            flops=2 * rows * docs * width, bytes_accessed=2 * (rows + docs) * width, transcendentals=0
        ),
        compiler_params=pltpu.CompilerParams(vmem_limit_bytes=16 * 1024 * 1024),
    )(*operands)


def solution(mesh):
    n_grp, n_ex, n_feat = (mesh.shape[a] for a in ("grp", "ex", "feat"))
    assert n_grp <= 2

    def after(block, *waits):
        return lax.optimization_barrier((block, waits))[0] if waits else block

    def line(train, test, scale):
        docs, feats = train.shape
        queries = test.shape[0]
        half = queries // n_grp
        unit = feats // (sum(LINE) + SHIP)
        ex = lax.axis_index("ex")
        is_end, first_grp = (ex == 0) | (ex == n_ex - 1), lax.axis_index("grp") == 0
        test, is_end, first_grp = lax.optimization_barrier((test, is_end, first_grp))
        done, outs, swaps, middles, made = {}, [], [], [], []

        outer_pairs = [(i, i ^ 1) for i in range(n_ex)]
        middle_pairs = []
        for i in range(n_ex):
            for f in range(n_feat):
                to = (i, f ^ 1) if i in (0, n_ex - 1) else (n_ex - 1 - i, f)
                middle_pairs.append((i * n_feat + f, to[0] * n_feat + to[1]))

        def outer(name, block, *ahead):
            waits = [*ahead] + outs[-2:-1] + swaps[-4:-3] + made[-4:-3] + (first if len(outs) == 4 else [])
            outs.append(lax.ppermute(after(block, *waits), "ex", outer_pairs))
            done[name] = outs[-1]

        def middle(name, block):
            middles.append(lax.ppermute(after(block, *middles[-1:]), ("ex", "feat"), middle_pairs))
            done[name] = middles[-1]

        def swap(block):
            if n_grp == 1:
                return [block]
            waits = swaps[-2:-1]
            if len(swaps) > 2 * len(LINE):
                waits = swaps[-3:-2] + made[-3:-2]
            swaps.append(lax.ppermute(after(block, *waits), "grp", [(0, 1), (1, 0)]))
            return [block, swaps[-1]]

        def sum_over_feat(sums, *waits):
            held = sums.reshape(n_feat, -1, docs)
            bit = 1
            while bit < n_feat:
                pairs = held.reshape((-1, 2) + held.shape[1:])
                partner = [(i, i ^ bit) for i in range(n_feat)]
                send = after(pairs[:, 1], *waits)
                held, waits = pairs[:, 0] + lax.ppermute(send, "feat", partner), ()
                bit *= 2
            return held[0]

        def share(rows, start, count):
            here = slice(start * unit, (start + count) * unit)
            if n_grp == 1:
                return rows[:, here]
            return jnp.where(first_grp, rows[:half, here], rows[half:, here])

        firsts = [sum(LINE[:c]) for c in range(len(LINE))]
        columns = [slice(f * unit, (f + n) * unit) for f, n in zip(firsts, LINE)]
        mine = []
        for start, count in zip(firsts, LINE):
            mine.append(share(after(test, *mine[-1:]), start, count))
        trains = [train[:, q * 4 * unit : (q + 1) * 4 * unit] for q in range(4)]
        widths = LINE[:2]
        shapes = [jax.ShapeDtypeStruct((half, w * unit), test.dtype) for w in widths]
        shapes.append(jax.ShapeDtypeStruct((half, n_grp * SHIP * unit), test.dtype))
        *cargo, own_tests = call(
            functools.partial(crate_kernel, unit, n_grp), docs, SHIP * unit, 1,
            [test, trains[3]], shapes=shapes,
        )

        first, sums = [], [None] * n_ex
        n = len(LINE)

        def finish(t, c, block):
            parts = swap(block)
            quarters = sorted({j // 4 for j in range(firsts[c], firsts[c] + LINE[c])})
            operands = [*parts, scale, *(trains[q] for q in quarters)]
            sizes = (unit, firsts[c], LINE[c], quarters, len(parts))
            if (t, c) == (3, n - 1):
                return sizes, operands
            base = [] if sums[t] is None else [sums[t]]
            kernel = functools.partial(line_part_kernel, *sizes)
            sums[t] = call(kernel, queries, docs, LINE[c] * unit, operands + base)
            made.append(sums[t])

        for c in range(n):
            outer(f"E1{c}", mine[c])
            middle(f"O1{c}", mine[c])
            if c == 0:
                late = after(test, done["E10"])
                sums[0] = call(
                    functools.partial(line_own_kernel, unit), queries, docs, feats, [late, scale, *trains]
                )
                first.append(sums[0])
            finish(1, c, done[f"E1{c}"])
        for c in range(n):
            inner = done[f"O1{c}"]
            ahead = done[f"O1{c + 1}"] if c + 1 < n else done["O20"]
            outer(f"E2{c}", jnp.where(is_end, cargo[c], inner) if c < len(cargo) else inner, ahead)
            middle(f"O2{c}", done[f"E1{c}"])
            finish(2, c, jnp.where(is_end, done[f"E2{c}"], inner))
        end_tests = done["E20"][:, : own_tests.shape[1]]
        middle("OS", jnp.concatenate([own_tests, end_tests], axis=0))
        for c in range(n):
            inner = done[f"O2{c}"]
            outer(f"E3{c}", inner, *([done[f"O2{c + 1}"]] if c + 1 < n else []))
            last = finish(3, c, jnp.where(is_end, done[f"E3{c}"], inner))
        shape = jax.ShapeDtypeStruct((n_ex * queries, docs), jnp.float32)
        landed = [done["E20"], done["E21"]]
        near, far = call(
            functools.partial(shipped_kernel, n_grp, n_feat, unit, len(landed)),
            n_ex * queries, docs, 2 * SHIP * unit,
            [test, scale, trains[3], done["OS"], *landed],
            [pltpu.VMEM(shape.shape, jnp.float32)], shapes=[shape, shape],
        )
        back = lax.ppermute(sum_over_feat(far), "ex", outer_pairs)
        sizes, operands = last
        total = call(
            functools.partial(line_last_kernel, n_grp, n_feat, *sizes),
            n_ex * queries, docs, LINE[-1] * unit, [*operands, near, *sums],
            [pltpu.VMEM(shape.shape, jnp.float32)],
        )
        out = sum_over_feat(total, back) + jnp.where(is_end, back, 0.0)
        return out.T

    def on_device(train, test, hess):
        docs, feats = train.shape
        queries = test.shape[0]
        half = queries // n_grp
        unit = 8 * LANES
        lanes = feats // LANES
        cuts = [c * lanes // CHUNKS * LANES for c in range(CHUNKS + 1)]
        starts, columns = cuts[:-1], [slice(*ends) for ends in zip(cuts[:-1], cuts[1:])]
        first_grp = lax.axis_index("grp") == 0
        ring = [(i, (i + 1) % n_ex) for i in range(n_ex)]
        hops, swaps, made, first = [], [], [], []

        def after(block, *waits):
            return lax.optimization_barrier((block, waits))[0] if waits else block

        def hop(block):
            waits = hops[-2:-1] + swaps[-4:-3] + made[-4:-3] + (first if len(hops) == 3 else [])
            hops.append(lax.ppermute(after(block, *waits), "ex", ring))
            return hops[-1]

        def swap(block):
            if n_grp == 1:
                return [block]
            waits = swaps[-2:-1]
            if len(swaps) > (n_ex - 2) * CHUNKS:
                waits = swaps[-3:-2] + made[-3:-2]
            swaps.append(lax.ppermute(after(block, *waits), "grp", [(0, 1), (1, 0)]))
            return [block, swaps[-1]]

        def sum_over_feat(sums):
            held = sums.reshape(n_feat, -1, docs)
            bit = 1
            while bit < n_feat:
                pairs = held.reshape((-1, 2) + held.shape[1:])
                partner = [(i, i ^ bit) for i in range(n_feat)]
                held = pairs[:, 0] + lax.ppermute(pairs[:, 1], "feat", partner)
                bit *= 2
            return held[0]

        def share(rows, columns):
            if n_grp == 1:
                return rows[:, columns]
            return jnp.where(first_grp, rows[:half, columns], rows[half:, columns])

        scale = (1.0 / (hess + jnp.float32(0.1))).reshape(1, feats)
        if n_ex == len(KEPT):
            return line(train, test, scale)
        held = []
        for here in columns:
            held.append(share(after(test, *held[-1:]), here))
        trains = [train[:, here] for here in columns]
        own = call(
            functools.partial(own_kernel, starts, unit), queries, docs, feats, [test, scale, *trains]
        )
        first.append(own)
        final = n_ex - 1
        sums = [own] + [None] * final
        for t in range(1, n_ex):
            for c, (start, here) in enumerate(zip(starts, columns)):
                held[c] = hop(held[c])
                parts = swap(held[c])
                operands = [*parts, scale, trains[c]]
                if (t, c) == (final, CHUNKS - 1):
                    continue
                base = [] if sums[t] is None else [sums[t]]
                sums[t] = call(
                    functools.partial(part_kernel, start, unit, len(parts), len(base)),
                    queries, docs, here.stop - here.start, operands + base,
                )
                made.append(sums[t])
        total = call(
            functools.partial(last_kernel, n_grp, n_ex, n_feat, start, unit, len(parts)),
            n_ex * queries, docs, here.stop - here.start, [*operands, *sums],
            [pltpu.VMEM((n_ex * queries, docs), jnp.float32)],
        )
        return sum_over_feat(total).T

    return jax.shard_map(
        on_device,
        mesh=mesh,
        in_specs=(P(("grp", "ex"), "feat"), P("ex", "feat"), P("feat")),
        out_specs=P(("grp", "ex"), "feat"),
        check_vma=False,
    )
```

```python
import functools

import jax
import jax.numpy as jnp
from jax import lax
from jax.experimental import pallas as pl
from jax.experimental.pallas import tpu as pltpu
from jax.sharding import PartitionSpec as P

CONTRACT = (((1,), (1,)), ((), ()))
LANES = 128
CHUNKS = 4


def product(rows, scale, train, unit):
    width, total = train.shape[1], None
    for at in range(0, width, unit):
        here = slice(at, min(at + unit, width))
        precond = (rows(here).astype(jnp.float32) * scale(here)).astype(jnp.bfloat16)
        part = lax.dot_general(
            precond, train[:, here], CONTRACT, preferred_element_type=jnp.float32
        )
        total = part if total is None else total + part
    return total


def own_kernel(starts, unit, test, scale, *refs):
    trains, out = refs[:-1], refs[-1]
    total = None
    for start, train in zip(starts, trains):
        column = lambda here: slice(start + here.start, start + here.stop)
        rows, scales = (lambda here, a=a: a[:, column(here)] for a in (test, scale))
        part = product(rows, scales, train, unit)
        total = part if total is None else total + part
    out[...] = total


def arrived_rows(parts):
    return lambda here: jnp.concatenate([p[:, here] for p in parts], axis=0)


def part_kernel(start, unit, n_parts, has_base, *refs):
    parts, (scale, train) = refs[:n_parts], refs[n_parts : n_parts + 2]
    column = lambda here: scale[:, start + here.start : start + here.stop]
    total = product(arrived_rows(parts), column, train, unit)
    refs[-1][...] = total + refs[n_parts + 2][...] if has_base else total


def last_kernel(n_grp, n_ex, n_feat, start, unit, n_parts, *refs):
    parts, (scale, train) = refs[:n_parts], refs[n_parts : n_parts + 2]
    sums, (out, kept) = refs[n_parts + 2 : -2], refs[-2:]
    column = lambda here: scale[:, start + here.start : start + here.stop]
    total = product(arrived_rows(parts), column, train, unit) + sums[-1][...]
    queries = total.shape[0]
    half = queries // n_grp
    for t, value in enumerate([s[...] for s in sums[:-1]] + [total]):
        kept[t * queries : (t + 1) * queries, :] = value
    ex, grp, feat = (lax.axis_index(a) for a in ("ex", "grp", "feat"))
    units = n_ex * n_grp
    each = units // n_feat
    for to in range(units):
        unit_of = (feat ^ (to // each)) * each + to % each
        t = lax.rem(ex + (n_ex - lax.div(unit_of, n_grp)), n_ex)
        h = lax.rem(unit_of, n_grp)
        place = jnp.where(t == 0, h, lax.rem(h + n_grp - grp, n_grp))
        at = pl.multiple_of(t * queries + place * half, half)
        out[to * half : (to + 1) * half, :] = kept[pl.ds(at, half), :]


LINE, SHIP = (5, 5, 5), 1
KEPT = ((0, 1, 2, 3), (1, 0, 2, 3), (2, 3, 1, 0), (3, 2, 1, 0))


def line_rows(n_grp, n_feat, halved):
    ex, grp, feat = (lax.axis_index(a) for a in ("ex", "grp", "feat"))
    units = len(KEPT) * n_grp
    each = units // n_feat
    found = []
    for to in range(units):
        unit_of = (feat ^ (to // each)) * each + to % each
        block, h = lax.div(unit_of, n_grp), lax.rem(unit_of, n_grp)
        t = jnp.int32(0)
        for i, kept in enumerate(KEPT):
            for b in kept[1:]:
                t = jnp.where((ex == i) & (block == b), kept.index(b), t)
        place = jnp.where(t == 0, h, lax.rem(h + n_grp - grp, n_grp)) if halved else h
        found.append(t * n_grp + place)
    return found


def units_product(rows, scale, trains, unit, first, count):
    total = None
    for k in range(count):
        j = first + k
        column = scale[:, j * unit : (j + 1) * unit]
        precond = (rows(k).astype(jnp.float32) * column).astype(jnp.bfloat16)
        here = trains[j // 4][:, (j % 4) * unit : (j % 4 + 1) * unit]
        part = lax.dot_general(precond, here, CONTRACT, preferred_element_type=jnp.float32)
        total = part if total is None else total + part
    return total


def line_own_kernel(unit, test, scale, *refs):
    rows = lambda k: test[:, k * unit : (k + 1) * unit]
    refs[-1][...] = units_product(rows, scale, refs[:-1], unit, 0, sum(LINE))


def line_part_kernel(unit, first, count, quarters, n_parts, *refs):
    parts, scale = refs[:n_parts], refs[n_parts]
    trains = dict(zip(quarters, refs[n_parts + 1 :]))
    base = refs[n_parts + 1 + len(quarters) : -1]
    rows = lambda k: jnp.concatenate([p[:, k * unit : (k + 1) * unit] for p in parts], axis=0)
    total = units_product(rows, scale, trains, unit, first, count)
    refs[-1][...] = total + base[0][...] if base else total


def line_last_kernel(n_grp, n_feat, unit, first, count, quarters, n_parts, *refs):
    parts, scale = refs[:n_parts], refs[n_parts]
    trains = dict(zip(quarters, refs[n_parts + 1 :]))
    near, *sums = refs[n_parts + 1 + len(quarters) : -2]
    out, kept = refs[-2:]
    rows = lambda k: jnp.concatenate([p[:, k * unit : (k + 1) * unit] for p in parts], axis=0)
    total = units_product(rows, scale, trains, unit, first, count) + sums[-1][...]
    queries = total.shape[0]
    half = queries // n_grp
    for t, value in enumerate([s[...] for s in sums[:-1]] + [total]):
        kept[t * queries : (t + 1) * queries, :] = value
    for to, place in enumerate(line_rows(n_grp, n_feat, True)):
        at = pl.multiple_of(place * half, half)
        here = slice(to * half, (to + 1) * half)
        out[here, :] = kept[pl.ds(at, half), :] + near[here, :]


def crate_kernel(unit, n_grp, test, train, *outs):
    half = test.shape[0] // n_grp
    base = sum(LINE)
    blocks = []
    for h in range(n_grp):
        for x in range(SHIP):
            cols = slice((base + x) * unit, (base + x + 1) * unit)
            blocks.append(test[h * half : (h + 1) * half, cols])
    n_tests = len(blocks)
    for x in range(SHIP):
        at = ((base + x) % 4) * unit
        for g in range(train.shape[0] // half):
            blocks.append(train[g * half : (g + 1) * half, at : at + unit])
    for i, block in enumerate(blocks[:n_tests]):
        outs[-1][:, i * unit : (i + 1) * unit] = block
    for out in outs[:-1]:
        for i in range(out.shape[1] // unit):
            out[:, i * unit : (i + 1) * unit] = blocks.pop(0) if len(blocks) > 1 else blocks[0]


def shipped_kernel(n_grp, n_feat, unit, n_cargo, test, scale, train, other, *refs):
    cargo, (near, far, kept) = refs[:n_cargo], refs[n_cargo:]
    base = sum(LINE)
    half = test.shape[0] // n_grp
    blocks = [(c, i * unit) for c in cargo for i in range(c.shape[1] // unit)]
    tests, rows_of = blocks[: n_grp * SHIP], blocks[n_grp * SHIP :]
    groups = train.shape[0] // half
    sums = [None, None]
    for x in range(SHIP):
        parts = [test[:, (base + x) * unit : (base + x + 1) * unit]]
        for h in range(n_grp):
            ref, at = tests[h * SHIP + x]
            parts.append(ref[:, at : at + unit])
        for k in range(2):
            for h in range(n_grp):
                at = (h * SHIP + x) * unit
                parts.append(other[k * half : (k + 1) * half, at : at + unit])
        rows = jnp.concatenate(parts, axis=0)
        column = scale[:, (base + x) * unit : (base + x + 1) * unit]
        precond = (rows.astype(jnp.float32) * column).astype(jnp.bfloat16)
        at = ((base + x) % 4) * unit
        away = [ref[:, c : c + unit] for ref, c in rows_of[x * groups : (x + 1) * groups]]
        for i, docs in enumerate((train[:, at : at + unit], jnp.concatenate(away, axis=0))):
            part = lax.dot_general(precond, docs, CONTRACT, preferred_element_type=jnp.float32)
            sums[i] = part if sums[i] is None else sums[i] + part
    ex = lax.axis_index("ex")
    inner = (ex > 0) & (ex < len(KEPT) - 1)
    places = line_rows(n_grp, n_feat, False)
    for value, out in zip((jnp.where(inner, sums[0], 0.0), sums[1]), (near, far)):
        kept[...] = value
        for to, place in enumerate(places):
            at = pl.multiple_of(place * half, half)
            out[to * half : (to + 1) * half, :] = kept[pl.ds(at, half), :]


def call(kernel, rows, docs, width, operands, scratch=(), shapes=None):
    vmem = pl.BlockSpec(memory_space=pltpu.VMEM)
    return pl.pallas_call(
        kernel,
        out_shape=shapes or jax.ShapeDtypeStruct((rows, docs), jnp.float32),
        in_specs=[vmem] * len(operands),
        out_specs=[vmem] * len(shapes) if shapes else vmem,
        scratch_shapes=scratch,
        cost_estimate=pl.CostEstimate(
            flops=2 * rows * docs * width, bytes_accessed=2 * (rows + docs) * width, transcendentals=0
        ),
        compiler_params=pltpu.CompilerParams(vmem_limit_bytes=16 * 1024 * 1024),
    )(*operands)


def solution(mesh):
    n_grp, n_ex, n_feat = (mesh.shape[a] for a in ("grp", "ex", "feat"))
    assert n_grp <= 2

    def after(block, *waits):
        return lax.optimization_barrier((block, waits))[0] if waits else block

    def line(train, test, scale):
        docs, feats = train.shape
        queries = test.shape[0]
        half = queries // n_grp
        unit = feats // (sum(LINE) + SHIP)
        ex = lax.axis_index("ex")
        is_end, first_grp = (ex == 0) | (ex == n_ex - 1), lax.axis_index("grp") == 0
        test, is_end, first_grp = lax.optimization_barrier((test, is_end, first_grp))
        done, outs, swaps, middles, made = {}, [], [], [], []

        outer_pairs = [(i, i ^ 1) for i in range(n_ex)]
        middle_pairs = []
        for i in range(n_ex):
            for f in range(n_feat):
                to = (i, f) if i in (0, n_ex - 1) else (n_ex - 1 - i, f)
                middle_pairs.append((i * n_feat + f, to[0] * n_feat + to[1]))

        def outer(name, block):
            waits = outs[-2:-1] + swaps[-4:-3] + made[-4:-3] + (first if len(outs) == 4 else [])
            outs.append(lax.ppermute(after(block, *waits), "ex", outer_pairs))
            done[name] = outs[-1]

        def middle(name, block):
            middles.append(lax.ppermute(after(block, *middles[-1:], *swaps[-2:-1]), ("ex", "feat"), middle_pairs))
            done[name] = middles[-1]

        def swap(block):
            if n_grp == 1:
                return [block]
            waits = swaps[-2:-1]
            if len(swaps) > 2 * len(LINE):
                waits = swaps[-3:-2] + made[-3:-2]
            swaps.append(lax.ppermute(after(block, *waits), "grp", [(0, 1), (1, 0)]))
            return [block, swaps[-1]]

        def sum_over_feat(sums, *waits):
            held = sums.reshape(n_feat, -1, docs)
            bit = 1
            while bit < n_feat:
                pairs = held.reshape((-1, 2) + held.shape[1:])
                partner = [(i, i ^ bit) for i in range(n_feat)]
                send = after(pairs[:, 1], *waits)
                held, waits = pairs[:, 0] + lax.ppermute(send, "feat", partner), ()
                bit *= 2
            return held[0]

        def share(rows, start, count):
            here = slice(start * unit, (start + count) * unit)
            if n_grp == 1:
                return rows[:, here]
            return jnp.where(first_grp, rows[:half, here], rows[half:, here])

        firsts = [sum(LINE[:c]) for c in range(len(LINE))]
        columns = [slice(f * unit, (f + n) * unit) for f, n in zip(firsts, LINE)]
        mine = []
        for start, count in zip(firsts, LINE):
            mine.append(share(after(test, *mine[-1:]), start, count))
        trains = [train[:, q * 4 * unit : (q + 1) * 4 * unit] for q in range(4)]
        widths = LINE[:2]
        shapes = [jax.ShapeDtypeStruct((half, w * unit), test.dtype) for w in widths]
        shapes.append(jax.ShapeDtypeStruct((half, n_grp * SHIP * unit), test.dtype))
        *cargo, own_tests = call(
            functools.partial(crate_kernel, unit, n_grp), docs, SHIP * unit, 1,
            [test, trains[3]], shapes=shapes,
        )

        first, sums = [], [None] * n_ex
        n = len(LINE)

        def finish(t, c, block):
            parts = swap(block)
            quarters = sorted({j // 4 for j in range(firsts[c], firsts[c] + LINE[c])})
            operands = [*parts, scale, *(trains[q] for q in quarters)]
            sizes = (unit, firsts[c], LINE[c], quarters, len(parts))
            if (t, c) == (3, n - 1):
                return sizes, operands
            base = [] if sums[t] is None else [sums[t]]
            kernel = functools.partial(line_part_kernel, *sizes)
            sums[t] = call(kernel, queries, docs, LINE[c] * unit, operands + base)
            made.append(sums[t])

        for c in range(n):
            outer(f"E1{c}", mine[c])
            middle(f"O1{c}", mine[c])
            if c == 0:
                late = after(test, done["E10"])
                sums[0] = call(
                    functools.partial(line_own_kernel, unit), queries, docs, feats, [late, scale, *trains]
                )
                first.append(sums[0])
            finish(1, c, done[f"E1{c}"])
        for c in range(n):
            inner = done[f"O1{c}"]
            outer(f"E2{c}", jnp.where(is_end, cargo[c], inner) if c < len(cargo) else inner)
            middle(f"O2{c}", done[f"E1{c}"])
            finish(2, c, jnp.where(is_end, done[f"E2{c}"], inner))
        end_tests = done["E20"][:, : own_tests.shape[1]]
        middle("OS", jnp.concatenate([own_tests, end_tests], axis=0))
        for c in range(n):
            inner = done[f"O2{c}"]
            outer(f"E3{c}", inner)
            last = finish(3, c, jnp.where(is_end, done[f"E3{c}"], inner))
        shape = jax.ShapeDtypeStruct((n_ex * queries, docs), jnp.float32)
        landed = [done["E20"], done["E21"]]
        near, far = call(
            functools.partial(shipped_kernel, n_grp, n_feat, unit, len(landed)),
            n_ex * queries, docs, 2 * SHIP * unit,
            [test, scale, trains[3], done["OS"], *landed],
            [pltpu.VMEM(shape.shape, jnp.float32)], shapes=[shape, shape],
        )
        back = lax.ppermute(sum_over_feat(far), "ex", outer_pairs)
        sizes, operands = last
        total = call(
            functools.partial(line_last_kernel, n_grp, n_feat, *sizes),
            n_ex * queries, docs, LINE[-1] * unit, [*operands, near, *sums],
            [pltpu.VMEM(shape.shape, jnp.float32)],
        )
        out = sum_over_feat(total, back) + jnp.where(is_end, back, 0.0)
        return out.T

    def on_device(train, test, hess):
        docs, feats = train.shape
        queries = test.shape[0]
        half = queries // n_grp
        unit = 8 * LANES
        lanes = feats // LANES
        cuts = [c * lanes // CHUNKS * LANES for c in range(CHUNKS + 1)]
        starts, columns = cuts[:-1], [slice(*ends) for ends in zip(cuts[:-1], cuts[1:])]
        first_grp = lax.axis_index("grp") == 0
        ring = [(i, (i + 1) % n_ex) for i in range(n_ex)]
        hops, swaps, made, first = [], [], [], []

        def after(block, *waits):
            return lax.optimization_barrier((block, waits))[0] if waits else block

        def hop(block):
            waits = hops[-2:-1] + swaps[-4:-3] + made[-4:-3] + (first if len(hops) == 3 else [])
            hops.append(lax.ppermute(after(block, *waits), "ex", ring))
            return hops[-1]

        def swap(block):
            if n_grp == 1:
                return [block]
            waits = swaps[-2:-1]
            if len(swaps) > (n_ex - 2) * CHUNKS:
                waits = swaps[-3:-2] + made[-3:-2]
            swaps.append(lax.ppermute(after(block, *waits), "grp", [(0, 1), (1, 0)]))
            return [block, swaps[-1]]

        def sum_over_feat(sums):
            held = sums.reshape(n_feat, -1, docs)
            bit = 1
            while bit < n_feat:
                pairs = held.reshape((-1, 2) + held.shape[1:])
                partner = [(i, i ^ bit) for i in range(n_feat)]
                held = pairs[:, 0] + lax.ppermute(pairs[:, 1], "feat", partner)
                bit *= 2
            return held[0]

        def share(rows, columns):
            if n_grp == 1:
                return rows[:, columns]
            return jnp.where(first_grp, rows[:half, columns], rows[half:, columns])

        scale = (1.0 / (hess + jnp.float32(0.1))).reshape(1, feats)
        if n_ex == len(KEPT):
            return line(train, test, scale)
        held = []
        for here in columns:
            held.append(share(after(test, *held[-1:]), here))
        trains = [train[:, here] for here in columns]
        own = call(
            functools.partial(own_kernel, starts, unit), queries, docs, feats, [test, scale, *trains]
        )
        first.append(own)
        final = n_ex - 1
        sums = [own] + [None] * final
        for t in range(1, n_ex):
            for c, (start, here) in enumerate(zip(starts, columns)):
                held[c] = hop(held[c])
                parts = swap(held[c])
                operands = [*parts, scale, trains[c]]
                if (t, c) == (final, CHUNKS - 1):
                    continue
                base = [] if sums[t] is None else [sums[t]]
                sums[t] = call(
                    functools.partial(part_kernel, start, unit, len(parts), len(base)),
                    queries, docs, here.stop - here.start, operands + base,
                )
                made.append(sums[t])
        total = call(
            functools.partial(last_kernel, n_grp, n_ex, n_feat, start, unit, len(parts)),
            n_ex * queries, docs, here.stop - here.start, [*operands, *sums],
            [pltpu.VMEM((n_ex * queries, docs), jnp.float32)],
        )
        return sum_over_feat(total).T

    return jax.shard_map(
        on_device,
        mesh=mesh,
        in_specs=(P(("grp", "ex"), "feat"), P("ex", "feat"), P("feat")),
        out_specs=P(("grp", "ex"), "feat"),
        check_vma=False,
    )
```

```python
import functools

import jax
import jax.numpy as jnp
from jax import lax
from jax.experimental import pallas as pl
from jax.experimental.pallas import tpu as pltpu
from jax.sharding import PartitionSpec as P

CONTRACT = (((1,), (1,)), ((), ()))
LANES = 128
CHUNKS = 5


def product(rows, scale, train, unit):
    width, total = train.shape[1], None
    for at in range(0, width, unit):
        here = slice(at, min(at + unit, width))
        precond = (rows(here).astype(jnp.float32) * scale(here)).astype(jnp.bfloat16)
        part = lax.dot_general(
            precond, train[:, here], CONTRACT, preferred_element_type=jnp.float32
        )
        total = part if total is None else total + part
    return total


def own_kernel(starts, unit, test, scale, *refs):
    trains, out = refs[:-1], refs[-1]
    total = None
    for start, train in zip(starts, trains):
        column = lambda here: slice(start + here.start, start + here.stop)
        rows, scales = (lambda here, a=a: a[:, column(here)] for a in (test, scale))
        part = product(rows, scales, train, unit)
        total = part if total is None else total + part
    out[...] = total


def arrived_rows(parts):
    return lambda here: jnp.concatenate([p[:, here] for p in parts], axis=0)


def part_kernel(start, unit, n_parts, has_base, *refs):
    parts, (scale, train) = refs[:n_parts], refs[n_parts : n_parts + 2]
    column = lambda here: scale[:, start + here.start : start + here.stop]
    total = product(arrived_rows(parts), column, train, unit)
    refs[-1][...] = total + refs[n_parts + 2][...] if has_base else total


def last_kernel(n_grp, n_ex, n_feat, start, unit, n_parts, *refs):
    parts, (scale, train) = refs[:n_parts], refs[n_parts : n_parts + 2]
    sums, (out, kept) = refs[n_parts + 2 : -2], refs[-2:]
    column = lambda here: scale[:, start + here.start : start + here.stop]
    total = product(arrived_rows(parts), column, train, unit) + sums[-1][...]
    queries = total.shape[0]
    half = queries // n_grp
    for t, value in enumerate([s[...] for s in sums[:-1]] + [total]):
        kept[t * queries : (t + 1) * queries, :] = value
    ex, grp, feat = (lax.axis_index(a) for a in ("ex", "grp", "feat"))
    units = n_ex * n_grp
    each = units // n_feat
    for to in range(units):
        unit_of = (feat ^ (to // each)) * each + to % each
        t = lax.rem(ex + (n_ex - lax.div(unit_of, n_grp)), n_ex)
        h = lax.rem(unit_of, n_grp)
        place = jnp.where(t == 0, h, lax.rem(h + n_grp - grp, n_grp))
        at = pl.multiple_of(t * queries + place * half, half)
        out[to * half : (to + 1) * half, :] = kept[pl.ds(at, half), :]


def call(kernel, rows, docs, width, operands, scratch=()):
    return pl.pallas_call(
        kernel,
        out_shape=jax.ShapeDtypeStruct((rows, docs), jnp.float32),
        in_specs=[pl.BlockSpec(memory_space=pltpu.VMEM)] * len(operands),
        out_specs=pl.BlockSpec(memory_space=pltpu.VMEM),
        scratch_shapes=scratch,
        cost_estimate=pl.CostEstimate(
            flops=2 * rows * docs * width, bytes_accessed=2 * (rows + docs) * width, transcendentals=0
        ),
        compiler_params=pltpu.CompilerParams(vmem_limit_bytes=16 * 1024 * 1024),
    )(*operands)


def solution(mesh):
    n_grp, n_ex, n_feat = (mesh.shape[a] for a in ("grp", "ex", "feat"))
    assert n_grp <= 2

    def on_device(train, test, hess):
        docs, feats = train.shape
        queries = test.shape[0]
        half = queries // n_grp
        unit = 8 * LANES
        lanes = feats // LANES
        cuts = [c * lanes // CHUNKS * LANES for c in range(CHUNKS + 1)]
        starts, columns = cuts[:-1], [slice(*ends) for ends in zip(cuts[:-1], cuts[1:])]
        first_grp = lax.axis_index("grp") == 0
        ring = [(i, (i + 1) % n_ex) for i in range(n_ex)]
        hops, swaps, made, first = [], [], [], []

        def after(block, *waits):
            return lax.optimization_barrier((block, waits))[0] if waits else block

        def hop(block):
            waits = hops[-2:-1] + swaps[-4:-3] + made[-4:-3] + (first if len(hops) == 3 else [])
            hops.append(lax.ppermute(after(block, *waits), "ex", ring))
            return hops[-1]

        def swap(block):
            if n_grp == 1:
                return [block]
            waits = swaps[-2:-1]
            if len(swaps) > (n_ex - 2) * CHUNKS:
                waits = swaps[-3:-2] + made[-3:-2]
            swaps.append(lax.ppermute(after(block, *waits), "grp", [(0, 1), (1, 0)]))
            return [block, swaps[-1]]

        def sum_over_feat(sums):
            held = sums.reshape(n_feat, -1, docs)
            bit = 1
            while bit < n_feat:
                pairs = held.reshape((-1, 2) + held.shape[1:])
                partner = [(i, i ^ bit) for i in range(n_feat)]
                held = pairs[:, 0] + lax.ppermute(pairs[:, 1], "feat", partner)
                bit *= 2
            return held[0]

        def share(rows, columns):
            if n_grp == 1:
                return rows[:, columns]
            return jnp.where(first_grp, rows[:half, columns], rows[half:, columns])

        scale = (1.0 / (hess + jnp.float32(0.1))).reshape(1, feats)
        held = []
        for here in columns:
            held.append(share(after(test, *held[-1:]), here))
        trains = [train[:, here] for here in columns]
        own = call(
            functools.partial(own_kernel, starts, unit), queries, docs, feats, [test, scale, *trains]
        )
        first.append(own)
        final = n_ex - 1
        sums = [own] + [None] * final
        for t in range(1, n_ex):
            for c, (start, here) in enumerate(zip(starts, columns)):
                held[c] = hop(held[c])
                parts = swap(held[c])
                operands = [*parts, scale, trains[c]]
                if (t, c) == (final, CHUNKS - 1):
                    continue
                base = [] if sums[t] is None else [sums[t]]
                sums[t] = call(
                    functools.partial(part_kernel, start, unit, len(parts), len(base)),
                    queries, docs, here.stop - here.start, operands + base,
                )
                made.append(sums[t])
        total = call(
            functools.partial(last_kernel, n_grp, n_ex, n_feat, start, unit, len(parts)),
            n_ex * queries, docs, here.stop - here.start, [*operands, *sums],
            [pltpu.VMEM((n_ex * queries, docs), jnp.float32)],
        )
        return sum_over_feat(total).T

    return jax.shard_map(
        on_device,
        mesh=mesh,
        in_specs=(P(("grp", "ex"), "feat"), P("ex", "feat"), P("feat")),
        out_specs=P(("grp", "ex"), "feat"),
        check_vma=False,
    )
```

```python
import functools

import jax
import jax.numpy as jnp
from jax import lax
from jax.experimental import pallas as pl
from jax.experimental.pallas import tpu as pltpu
from jax.sharding import PartitionSpec as P

CONTRACT = (((1,), (1,)), ((), ()))
LANES = 128
CHUNKS = 4


def product(rows, scale, train, unit):
    width, total = train.shape[1], None
    for at in range(0, width, unit):
        here = slice(at, min(at + unit, width))
        precond = (rows(here).astype(jnp.float32) * scale(here)).astype(jnp.bfloat16)
        part = lax.dot_general(
            precond, train[:, here], CONTRACT, preferred_element_type=jnp.float32
        )
        total = part if total is None else total + part
    return total


def own_kernel(starts, unit, test, scale, *refs):
    trains, out = refs[:-1], refs[-1]
    total = None
    for start, train in zip(starts, trains):
        column = lambda here: slice(start + here.start, start + here.stop)
        rows, scales = (lambda here, a=a: a[:, column(here)] for a in (test, scale))
        part = product(rows, scales, train, unit)
        total = part if total is None else total + part
    out[...] = total


def arrived_rows(parts):
    return lambda here: jnp.concatenate([p[:, here] for p in parts], axis=0)


def part_kernel(start, unit, n_parts, has_base, *refs):
    parts, (scale, train) = refs[:n_parts], refs[n_parts : n_parts + 2]
    column = lambda here: scale[:, start + here.start : start + here.stop]
    total = product(arrived_rows(parts), column, train, unit)
    refs[-1][...] = total + refs[n_parts + 2][...] if has_base else total


def last_kernel(n_grp, n_ex, n_feat, start, unit, n_parts, *refs):
    parts, (scale, train) = refs[:n_parts], refs[n_parts : n_parts + 2]
    sums, (out, kept) = refs[n_parts + 2 : -2], refs[-2:]
    column = lambda here: scale[:, start + here.start : start + here.stop]
    size = parts[0].shape[1]
    blocks = n_parts // (train.shape[1] // size)

    def rows(here):
        piece, at = here.start // size, here.start % size
        block = parts[piece * blocks : (piece + 1) * blocks]
        return jnp.concatenate([p[:, at : at + here.stop - here.start] for p in block], axis=0)

    total = product(rows, column, train, min(unit, size)) + sums[-1][...]
    queries = total.shape[0]
    half = queries // n_grp
    for t, value in enumerate([s[...] for s in sums[:-1]] + [total]):
        kept[t * queries : (t + 1) * queries, :] = value
    ex, grp, feat = (lax.axis_index(a) for a in ("ex", "grp", "feat"))
    units = n_ex * n_grp
    each = units // n_feat
    for to in range(units):
        unit_of = (feat ^ (to // each)) * each + to % each
        t = lax.rem(ex + (n_ex - lax.div(unit_of, n_grp)), n_ex)
        h = lax.rem(unit_of, n_grp)
        place = jnp.where(t == 0, h, lax.rem(h + n_grp - grp, n_grp))
        at = pl.multiple_of(t * queries + place * half, half)
        out[to * half : (to + 1) * half, :] = kept[pl.ds(at, half), :]


def call(kernel, rows, docs, width, operands, scratch=()):
    return pl.pallas_call(
        kernel,
        out_shape=jax.ShapeDtypeStruct((rows, docs), jnp.float32),
        in_specs=[pl.BlockSpec(memory_space=pltpu.VMEM)] * len(operands),
        out_specs=pl.BlockSpec(memory_space=pltpu.VMEM),
        scratch_shapes=scratch,
        cost_estimate=pl.CostEstimate(
            flops=2 * rows * docs * width, bytes_accessed=2 * (rows + docs) * width, transcendentals=0
        ),
        compiler_params=pltpu.CompilerParams(vmem_limit_bytes=16 * 1024 * 1024),
    )(*operands)


def solution(mesh):
    n_grp, n_ex, n_feat = (mesh.shape[a] for a in ("grp", "ex", "feat"))
    assert n_grp <= 2

    def on_device(train, test, hess):
        docs, feats = train.shape
        queries = test.shape[0]
        half = queries // n_grp
        unit = 8 * LANES
        lanes = feats // LANES
        cuts = [c * lanes // CHUNKS * LANES for c in range(CHUNKS + 1)]
        starts, columns = cuts[:-1], [slice(*ends) for ends in zip(cuts[:-1], cuts[1:])]
        first_grp = lax.axis_index("grp") == 0
        ring = [(i, (i + 1) % n_ex) for i in range(n_ex)]
        hops, swaps, made, first = [], [], [], []

        def after(block, *waits):
            return lax.optimization_barrier((block, waits))[0] if waits else block

        def hop(block):
            waits = hops[-2:-1] + swaps[-4:-3] + made[-4:-3] + (first if len(hops) == 3 else [])
            hops.append(lax.ppermute(after(block, *waits), "ex", ring))
            return hops[-1]

        def swap(block):
            if n_grp == 1:
                return [block]
            waits = swaps[-2:-1]
            if len(swaps) > (n_ex - 2) * CHUNKS:
                waits = swaps[-3:-2] + made[-3:-2]
            swaps.append(lax.ppermute(after(block, *waits), "grp", [(0, 1), (1, 0)]))
            return [block, swaps[-1]]

        def sum_over_feat(sums):
            held = sums.reshape(n_feat, -1, docs)
            bit = 1
            while bit < n_feat:
                pairs = held.reshape((-1, 2) + held.shape[1:])
                partner = [(i, i ^ bit) for i in range(n_feat)]
                held = pairs[:, 0] + lax.ppermute(pairs[:, 1], "feat", partner)
                bit *= 2
            return held[0]

        def share(rows, columns):
            if n_grp == 1:
                return rows[:, columns]
            return jnp.where(first_grp, rows[:half, columns], rows[half:, columns])

        scale = (1.0 / (hess + jnp.float32(0.1))).reshape(1, feats)
        held = []
        for here in columns:
            held.append(share(after(test, *held[-1:]), here))
        trains = [train[:, here] for here in columns]
        own = call(
            functools.partial(own_kernel, starts, unit), queries, docs, feats, [test, scale, *trains]
        )
        first.append(own)
        final = n_ex - 1
        sums = [own] + [None] * final
        for t in range(1, n_ex):
            for c, (start, here) in enumerate(zip(starts, columns)):
                if (t, c) == (final, CHUNKS - 1):
                    pieces = [swap(hop(piece)) for piece in jnp.split(held[c], 2, axis=1)]
                    parts = sum(pieces, [])
                    operands = [*parts, scale, trains[c]]
                    continue
                held[c] = hop(held[c])
                parts = swap(held[c])
                operands = [*parts, scale, trains[c]]
                base = [] if sums[t] is None else [sums[t]]
                sums[t] = call(
                    functools.partial(part_kernel, start, unit, len(parts), len(base)),
                    queries, docs, here.stop - here.start, operands + base,
                )
                made.append(sums[t])
        total = call(
            functools.partial(last_kernel, n_grp, n_ex, n_feat, start, unit, len(parts)),
            n_ex * queries, docs, here.stop - here.start, [*operands, *sums],
            [pltpu.VMEM((n_ex * queries, docs), jnp.float32)],
        )
        return sum_over_feat(total).T

    return jax.shard_map(
        on_device,
        mesh=mesh,
        in_specs=(P(("grp", "ex"), "feat"), P("ex", "feat"), P("feat")),
        out_specs=P(("grp", "ex"), "feat"),
        check_vma=False,
    )
```

```python
import functools

import jax
import jax.numpy as jnp
from jax import lax
from jax.experimental import pallas as pl
from jax.experimental.pallas import tpu as pltpu
from jax.sharding import PartitionSpec as P

CONTRACT = (((1,), (1,)), ((), ()))
LANES = 128
CHUNKS = 4


def product(rows, scale, train, unit):
    width, total = train.shape[1], None
    for at in range(0, width, unit):
        here = slice(at, min(at + unit, width))
        precond = (rows(here).astype(jnp.float32) * scale(here)).astype(jnp.bfloat16)
        part = lax.dot_general(
            precond, train[:, here], CONTRACT, preferred_element_type=jnp.float32
        )
        total = part if total is None else total + part
    return total


def own_kernel(starts, unit, test, scale, *refs):
    trains, out = refs[:-1], refs[-1]
    total = None
    for start, train in zip(starts, trains):
        column = lambda here: slice(start + here.start, start + here.stop)
        rows, scales = (lambda here, a=a: a[:, column(here)] for a in (test, scale))
        part = product(rows, scales, train, unit)
        total = part if total is None else total + part
    out[...] = total


def arrived_rows(parts):
    return lambda here: jnp.concatenate([p[:, here] for p in parts], axis=0)


def part_kernel(start, unit, n_parts, has_base, *refs):
    parts, (scale, train) = refs[:n_parts], refs[n_parts : n_parts + 2]
    column = lambda here: scale[:, start + here.start : start + here.stop]
    total = product(arrived_rows(parts), column, train, unit)
    refs[-1][...] = total + refs[n_parts + 2][...] if has_base else total


def last_kernel(n_grp, n_ex, n_feat, start, unit, n_parts, *refs):
    parts, (scale, train) = refs[:n_parts], refs[n_parts : n_parts + 2]
    sums, (out, kept) = refs[n_parts + 2 : -2], refs[-2:]
    column = lambda here: scale[:, start + here.start : start + here.stop]
    size = parts[0].shape[1]
    blocks = n_parts // (train.shape[1] // size)

    def rows(here):
        piece, at = here.start // size, here.start % size
        block = parts[piece * blocks : (piece + 1) * blocks]
        return jnp.concatenate([p[:, at : at + here.stop - here.start] for p in block], axis=0)

    total = product(rows, column, train, min(unit, size)) + sums[-1][...]
    queries = total.shape[0]
    half = queries // n_grp
    for t, value in enumerate([s[...] for s in sums[:-1]] + [total]):
        kept[t * queries : (t + 1) * queries, :] = value
    ex, grp, feat = (lax.axis_index(a) for a in ("ex", "grp", "feat"))
    units = n_ex * n_grp
    each = units // n_feat
    for to in range(units):
        unit_of = (feat ^ (to // each)) * each + to % each
        t = lax.rem(ex + (n_ex - lax.div(unit_of, n_grp)), n_ex)
        h = lax.rem(unit_of, n_grp)
        place = jnp.where(t == 0, h, lax.rem(h + n_grp - grp, n_grp))
        at = pl.multiple_of(t * queries + place * half, half)
        out[to * half : (to + 1) * half, :] = kept[pl.ds(at, half), :]


def call(kernel, rows, docs, width, operands, scratch=()):
    return pl.pallas_call(
        kernel,
        out_shape=jax.ShapeDtypeStruct((rows, docs), jnp.float32),
        in_specs=[pl.BlockSpec(memory_space=pltpu.VMEM)] * len(operands),
        out_specs=pl.BlockSpec(memory_space=pltpu.VMEM),
        scratch_shapes=scratch,
        cost_estimate=pl.CostEstimate(
            flops=2 * rows * docs * width, bytes_accessed=2 * (rows + docs) * width, transcendentals=0
        ),
        compiler_params=pltpu.CompilerParams(vmem_limit_bytes=16 * 1024 * 1024),
    )(*operands)


def solution(mesh):
    n_grp, n_ex, n_feat = (mesh.shape[a] for a in ("grp", "ex", "feat"))
    assert n_grp <= 2

    def on_device(train, test, hess):
        docs, feats = train.shape
        queries = test.shape[0]
        half = queries // n_grp
        unit = 8 * LANES
        lanes = feats // LANES
        cuts = [c * lanes // CHUNKS * LANES for c in range(CHUNKS + 1)]
        starts, columns = cuts[:-1], [slice(*ends) for ends in zip(cuts[:-1], cuts[1:])]
        first_grp = lax.axis_index("grp") == 0
        ring = [(i, (i + 1) % n_ex) for i in range(n_ex)]
        hops, swaps, made, first = [], [], [], []

        def after(block, *waits):
            return lax.optimization_barrier((block, waits))[0] if waits else block

        def hop(block, *ahead):
            waits = hops[-2:-1] + swaps[-4:-3] + made[-4:-3] + (first if len(hops) == 3 else [])
            hops.append(lax.ppermute(after(block, *waits, *ahead), "ex", ring))
            return hops[-1]

        def swap(block):
            if n_grp == 1:
                return [block]
            waits = swaps[-2:-1]
            if len(swaps) > (n_ex - 2) * CHUNKS:
                waits = swaps[-3:-2] + made[-3:-2]
            swaps.append(lax.ppermute(after(block, *waits), "grp", [(0, 1), (1, 0)]))
            return [block, swaps[-1]]

        def sum_over_feat(sums):
            held = sums.reshape(n_feat, -1, docs)
            bit = 1
            while bit < n_feat:
                pairs = held.reshape((-1, 2) + held.shape[1:])
                partner = [(i, i ^ bit) for i in range(n_feat)]
                held = pairs[:, 0] + lax.ppermute(pairs[:, 1], "feat", partner)
                bit *= 2
            return held[0]

        def share(rows, columns):
            if n_grp == 1:
                return rows[:, columns]
            return jnp.where(first_grp, rows[:half, columns], rows[half:, columns])

        scale = (1.0 / (hess + jnp.float32(0.1))).reshape(1, feats)
        held = []
        for here in columns:
            held.append(share(after(test, *held[-1:]), here))
        trains = [train[:, here] for here in columns]
        own = call(
            functools.partial(own_kernel, starts, unit), queries, docs, feats, [test, scale, *trains]
        )
        first.append(own)
        final = n_ex - 1
        sums = [own] + [None] * final
        for t in range(1, n_ex):
            for c, (start, here) in enumerate(zip(starts, columns)):
                if (t, c) == (final, CHUNKS - 1):
                    near, far = jnp.split(held[c], 2, axis=1)
                    pieces = [swap(hop(near))]
                    pieces.append(swap(hop(far, hops[-1])))
                    parts = sum(pieces, [])
                    operands = [*parts, scale, trains[c]]
                    continue
                held[c] = hop(held[c])
                parts = swap(held[c])
                operands = [*parts, scale, trains[c]]
                base = [] if sums[t] is None else [sums[t]]
                sums[t] = call(
                    functools.partial(part_kernel, start, unit, len(parts), len(base)),
                    queries, docs, here.stop - here.start, operands + base,
                )
                made.append(sums[t])
        total = call(
            functools.partial(last_kernel, n_grp, n_ex, n_feat, start, unit, len(parts)),
            n_ex * queries, docs, here.stop - here.start, [*operands, *sums],
            [pltpu.VMEM((n_ex * queries, docs), jnp.float32)],
        )
        return sum_over_feat(total).T

    return jax.shard_map(
        on_device,
        mesh=mesh,
        in_specs=(P(("grp", "ex"), "feat"), P("ex", "feat"), P("feat")),
        out_specs=P(("grp", "ex"), "feat"),
        check_vma=False,
    )
```
